512 devices in a mesh: gz: 128 (over x, z, y_hi, core), tile: 4 (over y_lo).
Axes of the slice: x: 4, y: 8 (y_hi: 2, y_lo: 4; y = y_hi * 4 + y_lo), z: 8, core: 2. Of those that a mesh axis runs over, the one named last changes fastest.
Arguments:
- sections: bfloat16 [128, 32, 256, 256], P('gz', 'tile'), may hold values from -6 to 6
- offsets: int32 [2, 2, 128, 32], P(None, None, 'gz', 'tile'), may hold values from -3 to 3
- node_links: int32 [4, 128, 32], P(None, 'gz', 'tile'), may hold values from 0 to 31, as said below
Outputs:
- shifts_found: float32 [2, 2, 128, 32], P(None, None, 'gz', 'tile')
- positions: float32 [2, 128, 32], P(None, 'gz', 'tile')
The draws below stay inside these ranges and needn't reach their ends.
Inputs may be any that keep to these rules, and one draw needn't show every extreme that they name: `node_links`: each entry names a node of the same section at most one row and one column away from node i in the grid of 8 rows of 4 nodes (node number = row * 4 + column), never node i itself; entry 0 lies in the same row and entry 1 in the same column.
All inputs are finite; a program needn't handle non-finite values.
Results may differ from the reference program's by a relative error of at most 0.0013.
Values may be sent and summed in bfloat16 or wider, within the bound.
No kernel may reach another device: no remote copies, remote signals or barrier semaphores. Data moves between devices by JAX's collectives and lax.ppermute only.
A program may use at most 64 MiB of HBM per device.

```python
import math
import jax
import jax.numpy as jnp
from jax import lax

PATCH = 256
NODE_COLS = 4
STEPS = 2
GRID_ROWS = 8
NODES = 32
SECTIONS = 128


def draw_node_links(key, part):
    key = jax.random.fold_in(key, 11)
    node_ids = jnp.arange(NODES, dtype=jnp.int32)
    row_ids = node_ids // NODE_COLS
    col_ids = node_ids % NODE_COLS
    horizontal = jnp.where(col_ids > 0, node_ids - 1, node_ids + 1)
    vertical = jnp.where(row_ids < GRID_ROWS - 1, node_ids + NODE_COLS, node_ids - NODE_COLS)
    key_rows, key_cols = jax.random.split(key)
    row_step = jax.random.randint(key_rows, (2, SECTIONS, NODES), -1, 2)
    col_step = jax.random.randint(key_cols, (2, SECTIONS, NODES), -1, 2)
    col_step = jnp.where((row_step == 0) & (col_step == 0), jnp.where(col_ids > 0, -1, 1), col_step)
    row_new = row_ids + row_step
    row_new = jnp.where((row_new < 0) | (row_new >= GRID_ROWS), row_ids - row_step, row_new)
    col_new = col_ids + col_step
    col_new = jnp.where((col_new < 0) | (col_new >= NODE_COLS), col_ids - col_step, col_new)
    random_links = row_new * NODE_COLS + col_new
    fixed_links = jnp.broadcast_to(jnp.stack([horizontal, vertical])[:, None, :], (2, SECTIONS, NODES))
    return jnp.concatenate([fixed_links, random_links], axis=0).astype(jnp.int32)


def set_ends(entries, key, least, top_value):
    index_at = [jax.random.randint(jax.random.fold_in(key, axis), (), 0, length) for axis, length in enumerate(entries.shape)]
    widest = entries.shape.index(max(entries.shape))
    neighbour = index_at[:widest] + [(index_at[widest] + 1) % entries.shape[widest]] + index_at[widest + 1:]
    return entries.at[tuple(index_at)].set(least).at[tuple(neighbour)].set(top_value)


def shard_levels(own_key, shape, cuts, smallest, top_value):
    level = 1.0
    for dim, shards_of in cuts:
        steps = jax.random.uniform(jax.random.fold_in(jax.random.fold_in(own_key, 6), dim), (shards_of,), jnp.float32, smallest / len(cuts), top_value / len(cuts))
        level = level * jnp.repeat(jnp.exp(steps), shape[dim] // shards_of).reshape((-1,) + (1,) * (len(shape) - 1 - dim))
    return level


def centred(key, extent, spread, most, cuts=(), held_as=jnp.bfloat16):
    drawn = spread * jax.random.normal(key, extent, jnp.float32)
    if cuts:
        drawn = drawn * shard_levels(key, extent, cuts, -0.22, 0.18)
    return jnp.clip(drawn, -most, most).astype(held_as)


def setup_inputs(seed: int = 0) -> dict:
    splits = jax.random.split(jax.random.key(seed), 4)
    return {
        "sections": centred(splits[0], (SECTIONS, NODES, PATCH, PATCH), 1.0, 6.0, ((0, 128), (1, 4))),
        "offsets": set_ends(jax.random.randint(splits[1], (2, 2, SECTIONS, NODES), -3, 4), jax.random.fold_in(splits[1], 1), -3, 3).astype(jnp.int32),
        "node_links": draw_node_links(jax.random.fold_in(splits[3], 71), 0),
    }


def dft_tables(length):
    indices = jnp.arange(length, dtype=jnp.int32)
    phases = indices[:, None] * indices[None, :] % length
    angles = phases.astype(jnp.float32) * (2.0 * math.pi / length)
    return (jnp.cos(angles).astype(jnp.bfloat16), jnp.sin(angles).astype(jnp.bfloat16))

def spectrum_one(patch, right_table, left_table):
    length = patch.shape[0]
    half_product = jnp.dot(patch.astype(jnp.float32), right_table.astype(jnp.float32), preferred_element_type=jnp.float32).astype(jnp.bfloat16)
    full_product = jnp.dot(left_table.astype(jnp.float32), half_product.astype(jnp.float32), preferred_element_type=jnp.float32)
    real_part = full_product[:length, :length] - full_product[length:, length:]
    imag_part = -(full_product[:length, length:] + full_product[length:, :length])
    return jnp.concatenate([real_part, imag_part], axis=1).astype(jnp.bfloat16)

def refine(spec_a, spec_b, offset_y, offset_x):
    length = spec_a.shape[0]
    highest = lax.Precision.HIGHEST
    spec_first = spec_a.astype(jnp.float32)
    spec_other = spec_b.astype(jnp.float32)
    a_real, a_imag = (spec_first[:, :length], spec_first[:, length:])
    b_real, b_imag = (spec_other[:, :length], spec_other[:, length:])
    cross_real = a_real * b_real + a_imag * b_imag
    cross_imag = a_imag * b_real - a_real * b_imag
    magnitude = jnp.sqrt(cross_real * cross_real + cross_imag * cross_imag)
    denominator = magnitude + jnp.mean(magnitude) + 1e-06
    power = jnp.concatenate([cross_real / denominator, cross_imag / denominator], axis=1)
    step_offsets = jnp.arange(-1, 2, dtype=jnp.int32)
    indices = jnp.arange(length, dtype=jnp.int32)
    row_phases = (offset_y + step_offsets)[:, None] * indices[None, :] % length
    col_phases = (offset_x + step_offsets)[:, None] * indices[None, :] % length
    row_angles = row_phases.astype(jnp.float32) * (2.0 * math.pi / length)
    col_angles = col_phases.astype(jnp.float32) * (2.0 * math.pi / length)
    left_rows = jnp.concatenate([jnp.cos(row_angles), jnp.sin(row_angles)], axis=0)
    folded = jnp.dot(left_rows, power, precision=highest, preferred_element_type=jnp.float32)
    col_cos = jnp.cos(col_angles).T
    col_sin = jnp.sin(col_angles).T
    cos_real, sin_real = (folded[:3, :length], folded[3:, :length])
    cos_imag, sin_imag = (folded[:3, length:], folded[3:, length:])
    correlation = (jnp.dot(cos_real, col_cos, precision=highest, preferred_element_type=jnp.float32) - jnp.dot(sin_real, col_sin, precision=highest, preferred_element_type=jnp.float32) - jnp.dot(sin_imag, col_cos, precision=highest, preferred_element_type=jnp.float32) - jnp.dot(cos_imag, col_sin, precision=highest, preferred_element_type=jnp.float32)) / length
    weight = jnp.exp(3.0 * jnp.tanh(correlation))
    weight_sum = jnp.sum(weight)
    step_float = step_offsets.astype(jnp.float32)
    shift_y = offset_y.astype(jnp.float32) + jnp.sum(step_float[:, None] * weight) / weight_sum
    shift_x = offset_x.astype(jnp.float32) + jnp.sum(step_float[None, :] * weight) / weight_sum
    return jnp.stack([shift_y, shift_x])

def refine_both(spec_here, spec_next, spec_second, offset_pair):
    first_pair = refine(spec_here, spec_next, offset_pair[0, 0], offset_pair[0, 1])
    second_pair = refine(spec_here, spec_second, offset_pair[1, 0], offset_pair[1, 1])
    return jnp.stack([first_pair, second_pair])

def reference(sections, offsets, node_links):
    cos_table, sin_table = dft_tables(PATCH)
    right_table = jnp.concatenate([cos_table, sin_table], axis=1)
    left_table = jnp.concatenate([cos_table, sin_table], axis=0)

    def transform(patch):
        return spectrum_one(patch, right_table, left_table)

    def one_section(carried, inputs):
        spec_next, spec_second = carried
        patches, offset_rows = inputs
        spec_here = jax.vmap(transform)(patches)
        pair_shifts = jax.vmap(refine_both)(spec_here, spec_next, spec_second, jnp.moveaxis(offset_rows, 2, 0))
        return ((spec_here, spec_next), pair_shifts)
    zero_spectra = jnp.zeros((NODES, PATCH, 2 * PATCH), jnp.bfloat16)
    _, found_all = lax.scan(one_section, (zero_spectra, zero_spectra), (sections, jnp.moveaxis(offsets, 2, 0)), reverse=True)
    shifts_found = jnp.transpose(found_all, (2, 3, 0, 1))
    section_ids = jnp.arange(SECTIONS, dtype=jnp.int32)[:, None]
    has_next = (jnp.arange(SECTIONS) + 1 < SECTIONS).astype(jnp.float32)[None, :, None]
    zero_layer = jnp.zeros((2, 1, NODES), jnp.float32)
    positions = jnp.zeros((2, SECTIONS, NODES), jnp.float32)
    for relax_step in range(STEPS):
        neighbours = positions[:, section_ids, node_links[0]]
        for link_number in range(1, 4):
            neighbours = neighbours + positions[:, section_ids, node_links[link_number]]
        in_plane = 0.25 * (neighbours - 4.0 * positions)
        ahead_pos = jnp.concatenate([positions[:, 1:], zero_layer], axis=1)
        spring_pull = has_next * (ahead_pos - positions - shifts_found[0])
        behind_pull = jnp.concatenate([zero_layer, spring_pull[:, :-1]], axis=1)
        spring_force = in_plane + 0.5 * (spring_pull - behind_pull)
        positions = positions + 0.5 * spring_force
    return (shifts_found, positions)
```

```python
import functools
import math

import jax
import jax.numpy as jnp
import ml_dtypes
import numpy as np
from jax import lax
from jax.experimental import pallas as pl
from jax.experimental.pallas import tpu as pltpu
from jax.sharding import PartitionSpec as P

NODE_COLS = 4
STEPS = 2
SIDE = 256
HALF = SIDE // 2
ROWS = 144
REACH = 4
SPAN = 16
GROUP = 4
EXTRA = 16
BLOCK = GROUP * SIDE + EXTRA

SLOTS = ((0, 1, 4, 3, 2), (1, 0, 3, -1, None), (2, 3, 0, 4, None), (3, 2, -1, 0, 1))
STAGES = (
    ((), ((0, 1), (1, 3)), ((2, 3), (0, 2)), ()),
    (((3, 4),), ((-1, 0), (-1, 1)), ((3, 4), (2, 4)), ((-1, 0),)),
    (((1, 2), (2, 3), (0, 2), (2, 4)), (), (), ((0, 1), (1, 2), (-1, 1), (1, 3))),
)


def pair_places():
    places = {}
    for device in range(4):
        order = [pair for stage in STAGES for pair in stage[device]]
        for place, pair in enumerate(order):
            places[(device // 2, pair)] = (device, place)
    return places


def pair_table():
    table = np.zeros((3, 4, 17), np.int32)
    places = pair_places()
    for number, stage in enumerate(STAGES):
        for device in range(4):
            table[number, device, 0] = len(stage[device])
            for k, (a, b) in enumerate(stage[device]):
                slots = SLOTS[device]
                entry = (slots.index(a), slots.index(b), b - a - 1, places[(device // 2, (a, b))][1])
                table[number, device, 1 + 4 * k : 5 + 4 * k] = entry
    return table


def tables():
    index = np.arange(SIDE)

    def angle(phases):
        return (phases % SIDE).astype(np.float32) * np.float32(2.0 * math.pi / SIDE)

    phases = np.outer(index, index)
    cos_table = np.cos(angle(phases)).astype(ml_dtypes.bfloat16)
    sin_table = np.sin(angle(phases)).astype(ml_dtypes.bfloat16)
    right = np.concatenate([cos_table[: HALF + 1], sin_table[1:HALF]], axis=0)
    left = np.ascontiguousarray(right.T)
    row_freq = np.concatenate([np.arange(HALF + 1), -np.arange(1, HALF)])
    window = np.arange(-REACH, REACH + 1)
    fold_phase = 2.0 * math.pi * (np.outer(row_freq, window) % SIDE) / SIDE
    fold_cos, fold_sin = np.cos(fold_phase), np.sin(fold_phase)
    fold = np.zeros((GROUP, 2, SIDE, 2, 2, GROUP, SPAN), np.float32)
    for j in range(GROUP):
        for part, out, value in ((0, 0, fold_cos), (1, 0, -fold_sin), (0, 1, fold_sin), (1, 1, fold_cos)):
            high = value.astype(np.float32).astype(ml_dtypes.bfloat16).astype(np.float32)
            fold[j, part, :, out, 0, j, : window.size] = high
            fold[j, part, :, out, 1, j, : window.size] = value - high
    fold = fold.reshape(GROUP * 2 * SIDE, SIDE).astype(ml_dtypes.bfloat16)
    col_freq = np.arange(HALF + 1)
    twice = np.where((col_freq == 0) | (col_freq == HALF), 1.0, 2.0)[None, :] / SIDE
    col_phase = 2.0 * math.pi * (np.outer(window, col_freq) % SIDE) / SIDE
    close = np.zeros((2, SPAN, ROWS), np.float32)
    close[0, : window.size, : HALF + 1] = twice * np.cos(col_phase)
    close[1, : window.size, : HALF + 1] = twice * np.sin(col_phase)
    return right, left, fold, close.reshape(2 * SPAN, ROWS)


def transform(patch, right, left):
    half_product = lax.dot_general(
        right, patch, (((1,), (1,)), ((), ())), preferred_element_type=jnp.float32
    ).astype(jnp.bfloat16)
    full = jnp.dot(half_product, left, preferred_element_type=jnp.float32)
    lane = lax.broadcasted_iota(jnp.int32, (HALF, HALF), 1)
    row = lax.broadcasted_iota(jnp.int32, (HALF, HALF), 0)
    first_lane, first_row = lane == 0, row == 0
    cc, sc = full[:HALF, :HALF], full[:HALF, HALF:]
    last_c, last_s = full[HALF:, :HALF], full[HALF:, HALF:]
    cs, ss = jnp.where(first_row, 0.0, last_c), jnp.where(first_row, 0.0, last_s)

    def parts(cc, sc, cs, ss, edge):
        low_sc, low_ss = jnp.where(edge, 0.0, sc), jnp.where(edge, 0.0, ss)
        return jnp.concatenate(
            [
                cc - low_ss,
                jnp.where(edge, sc, cc + ss),
                -(cs + low_sc),
                jnp.where(edge, -ss, sc - cs),
            ],
            axis=1,
        ).astype(jnp.bfloat16)

    tail = ROWS - HALF
    keep = row[:tail] == 0
    end_c, end_s = jnp.where(keep, last_c[:tail], 0.0), jnp.where(keep, last_s[:tail], 0.0)
    none = jnp.zeros_like(end_c)
    return parts(cc, sc, cs, ss, first_lane), parts(end_c, end_s, none, none, first_lane[:tail])


def stage_kernel(number, new_count, old_count, *refs):
    table, right, left, fold, close, before = refs[:6]
    payloads = refs[6 : 6 + 2 * new_count]
    old_specs = refs[6 + 2 * new_count : 6 + 2 * new_count + old_count]
    old_offs = refs[6 + 2 * new_count + old_count : 6 + 2 * new_count + 2 * old_count]
    rest = refs[6 + 2 * new_count + 2 * old_count :]
    found, new_specs, new_offs = rest[0], rest[1 : 1 + new_count], rest[1 + new_count : 1 + 2 * new_count]
    specs, cross_r, cross_i, size, power, offs, old_sem, new_sem = rest[1 + 2 * new_count :]
    device = lax.rem(lax.axis_index("gz"), 4)
    chunk = 16

    old_copies = [
        pltpu.make_async_copy(old_specs[k], specs.at[pl.ds(GROUP * k, GROUP)], old_sem.at[k]) for k in range(old_count)
    ]
    for copy in old_copies:
        copy.start()
    for k in range(old_count):
        offs[k] = old_offs[k][...]
    right_table, left_table = right[...], left[...]
    for k in range(new_count):
        first, other = payloads[2 * k], payloads[2 * k + 1]
        slot = old_count + k
        both = first[GROUP * SIDE :, :] + other[GROUP * SIDE :, :]
        offs[slot] = both
        new_offs[k][...] = both

        @pl.loop(0, GROUP)
        def _(n, first=first, other=other, slot=slot):
            rows = pl.ds(pl.multiple_of(n * SIDE, SIDE), SIDE)
            main, end = transform(first[rows, :] + other[rows, :], right_table, left_table)
            specs[slot * GROUP + n, :HALF, :] = main
            specs[slot * GROUP + n, HALF:, :] = end

    new_copies = [
        pltpu.make_async_copy(specs.at[pl.ds(GROUP * (old_count + k), GROUP)], new_specs[k], new_sem.at[k])
        for k in range(new_count)
    ]
    for copy in old_copies:
        copy.wait()
    for copy in new_copies:
        copy.start()

    found[...] = before[...]
    lane = lax.broadcasted_iota(jnp.int32, (SPAN, 128), 1)
    step_u = (lax.rem(lane, SPAN) - REACH).astype(jnp.float32)
    step_v = (lax.broadcasted_iota(jnp.int32, (SPAN, 128), 0) - REACH).astype(jnp.float32)
    place_row = lax.broadcasted_iota(jnp.int32, (16, 128), 0)

    @pl.loop(0, table[number, device, 0])
    def _(k):
        base = 1 + 4 * k
        slot_a, slot_b = table[number, device, base], table[number, device, base + 1]
        partner, place = table[number, device, base + 2], table[number, device, base + 3]
        for j in range(GROUP):
            total = jnp.zeros((8, SIDE), jnp.float32)
            for start in range(0, ROWS, chunk):
                rows = slice(start, start + chunk)
                a = specs[slot_a * GROUP + j, rows, :].astype(jnp.float32)
                b = specs[slot_b * GROUP + j, rows, :].astype(jnp.float32)
                ar, ai, br, bi = a[:, :SIDE], a[:, SIDE:], b[:, :SIDE], b[:, SIDE:]
                real = ar * br + ai * bi
                imag = ai * br - ar * bi
                square = real * real + imag * imag
                magnitude = square * lax.rsqrt(jnp.maximum(square, 1e-30))
                cross_r[j, rows, :] = real
                cross_i[j, rows, :] = imag
                size[j, rows, :] = magnitude
                if start == 0:
                    edge = lax.broadcasted_iota(jnp.int32, (chunk, SIDE), 0) == 0
                    magnitude = jnp.where(edge, 0.5 * magnitude, magnitude)
                elif start == HALF:
                    magnitude = 0.5 * magnitude
                total = total + magnitude[:8] + magnitude[8:]
            mean = jnp.sum(total) * (2.0 / (SIDE * SIDE))
            floor = mean + 1e-6
            for start in range(0, ROWS, chunk):
                rows = slice(start, start + chunk)
                scale = pl.reciprocal(size[j, rows, :] + floor, approx=False)
                power[rows, 2 * SIDE * j : 2 * SIDE * j + SIDE] = (cross_r[j, rows, :] * scale).astype(jnp.bfloat16)
                power[rows, 2 * SIDE * j + SIDE : 2 * SIDE * (j + 1)] = (cross_i[j, rows, :] * scale).astype(jnp.bfloat16)
        folded = jnp.dot(power[...], fold[...], preferred_element_type=jnp.float32)
        closed = jnp.dot(
            close[...], folded, precision=lax.Precision.HIGHEST, preferred_element_type=jnp.float32
        )
        correlation = closed[:SPAN, :128] - closed[SPAN:, 128:]
        correlation = correlation + pltpu.roll(correlation, 64, axis=1)
        own = offs[slot_a].astype(jnp.float32)
        here = jnp.where(partner == 0, own[0:2, :128], own[2:4, :128])
        off_y, off_x = here[0:1], here[1:2]
        from_y, from_x = step_u - off_y, step_v - off_x
        inside = (jnp.abs(from_y) < 1.5) & (jnp.abs(from_x) < 1.5)
        weight = jnp.where(inside, jnp.exp(3.0 * jnp.tanh(correlation)), 0.0)
        sums = jnp.concatenate(
            [
                jnp.sum(weight, axis=0, keepdims=True),
                jnp.sum(weight * from_y, axis=0, keepdims=True),
                jnp.sum(weight * from_x, axis=0, keepdims=True),
                jnp.zeros((5, 128), jnp.float32),
            ],
            axis=0,
        )
        for shift in (8, 4, 2, 1):
            sums = sums + pltpu.roll(sums, 128 - shift, axis=1)
        shift_y = off_y + sums[1:2] / sums[0:1]
        shift_x = off_x + sums[2:3] / sums[0:1]
        found[...] = jnp.where(
            place_row == 2 * place, shift_y, jnp.where(place_row == 2 * place + 1, shift_x, found[...])
        )

    for copy in new_copies:
        copy.wait()


def run_stage(number, consts, before, payloads, old_specs, old_offs):
    new_count, old_count = len(payloads), len(old_specs)
    vmem, hbm = pl.BlockSpec(memory_space=pltpu.VMEM), pl.BlockSpec(memory_space=pl.ANY)
    slots = new_count + old_count
    spec_shape = jax.ShapeDtypeStruct((GROUP, ROWS, 2 * SIDE), jnp.bfloat16)
    off_shape = jax.ShapeDtypeStruct((EXTRA, SIDE), jnp.bfloat16)
    out = pl.pallas_call(
        functools.partial(stage_kernel, number, new_count, old_count),
        out_shape=(jax.ShapeDtypeStruct((16, 128), jnp.float32),)
        + (spec_shape,) * new_count
        + (off_shape,) * new_count,
        in_specs=[pl.BlockSpec(memory_space=pltpu.SMEM)]
        + [vmem] * (5 + 2 * new_count)
        + [hbm] * old_count
        + [vmem] * old_count,
        out_specs=(vmem,) + (hbm,) * new_count + (vmem,) * new_count,
        scratch_shapes=[
            pltpu.VMEM((slots * GROUP, ROWS, 2 * SIDE), jnp.bfloat16),
            pltpu.VMEM((GROUP, ROWS, SIDE), jnp.float32),
            pltpu.VMEM((GROUP, ROWS, SIDE), jnp.float32),
            pltpu.VMEM((GROUP, ROWS, SIDE), jnp.float32),
            pltpu.VMEM((ROWS, 2 * SIDE * GROUP), jnp.bfloat16),
            pltpu.VMEM((slots, EXTRA, SIDE), jnp.bfloat16),
            pltpu.SemaphoreType.DMA((max(old_count, 1),)),
            pltpu.SemaphoreType.DMA((max(new_count, 1),)),
        ],
        compiler_params=pltpu.CompilerParams(vmem_limit_bytes=40 * 1024 * 1024),
        name=f"stage{number}",
    )(*consts, before, *[p for pair in payloads for p in pair], *old_specs, *old_offs)
    return out[0], out[1 : 1 + new_count], out[1 + new_count :]


def shards(sections, offsets, node_links):
    patches = sections[0]
    sections_total, tiles = lax.axis_size("gz"), lax.axis_size("tile")
    position = lax.axis_index("gz")
    tile_index = lax.axis_index("tile")
    device = position % 4
    chip = device // 2

    def send(value, moves):
        pairs = [(i, i + moves[i % 4]) for i in range(sections_total) if i % 4 in moves]
        return lax.ppermute(value, "gz", [(i, j) for i, j in pairs if 0 <= j < sections_total])

    lanes = jnp.repeat(offsets[:, :, 0, :].reshape(4, 2, GROUP).astype(jnp.bfloat16), SPAN, axis=2)
    lanes = jnp.pad(jnp.moveaxis(lanes, 1, 0), ((0, 0), (0, EXTRA - 4), (0, SIDE - GROUP * SPAN)))
    flat = patches.reshape(2, GROUP * SIDE, SIDE)

    def block(row):
        return jnp.concatenate(
            [
                lax.dynamic_index_in_dim(flat, row, 0, keepdims=False),
                lax.dynamic_index_in_dim(lanes, row, 0, keepdims=False),
            ],
            axis=0,
        )

    away, own = block(1 - chip), block(chip)
    first = send(away, {0: 2, 3: -2})
    second = send(away, {2: -2, 1: 2})
    beside = send(own, {0: 1, 1: -1, 2: 1, 3: -1})
    border = send(own, {0: -4, 3: 4})
    border_late = send(first, {2: -4, 1: 4})
    first_on = send(first, {1: -1, 2: 1})

    right, left, fold, close = tables()
    consts = (jnp.asarray(pair_table()), *(jnp.asarray(t) for t in (right, left, fold, close)))
    nothing = jnp.zeros((16, 128), jnp.float32)
    zeros = jnp.zeros((BLOCK, SIDE), jnp.bfloat16)
    found, specs, offs = run_stage(
        0, consts, nothing, [(own, zeros), (beside, zeros), (first, border)], [], []
    )
    found, more_specs, more_offs = run_stage(1, consts, found, [(first_on, border_late)], specs, offs)
    found, _, _ = run_stage(2, consts, found, [(second, zeros)], specs + more_specs, offs + more_offs)

    quads = [list(range(4 * g, 4 * g + 4)) for g in range(sections_total // 4)]
    every = lax.all_gather(found, "gz", axis_index_groups=quads)
    values = every[:, :, : GROUP * SPAN : SPAN].reshape(4, 8, 2, GROUP)
    places = pair_places()

    def shift_of(pair):
        return jnp.concatenate([values[places[(row, pair)]] for row in range(2)], axis=1)

    next_all = jnp.stack([shift_of((s, s + 1)) for s in range(-1, 4)])
    second_all = jnp.stack([shift_of((s, s + 2)) for s in range(-1, 3)])
    halo_out = jnp.where(
        device == 0, jnp.stack([next_all[3], second_all[0]]), jnp.stack([next_all[1], second_all[0]])
    )
    halo = send(halo_out, {0: 4, 3: -4})
    found_behind = lax.dynamic_index_in_dim(next_all, device, 0, keepdims=False)
    found_next = lax.dynamic_index_in_dim(next_all, device + 1, 0, keepdims=False)
    found_behind2 = jnp.where(
        device == 0, halo[0], lax.dynamic_index_in_dim(next_all, jnp.maximum(device - 1, 0), 0, keepdims=False)
    )
    found_ahead = jnp.where(
        device == 3, halo[0], lax.dynamic_index_in_dim(next_all, jnp.minimum(device + 2, 4), 0, keepdims=False)
    )
    found_second = jnp.where(
        device == 3, halo[1], lax.dynamic_index_in_dim(second_all, jnp.minimum(device + 1, 3), 0, keepdims=False)
    )
    own_offsets = offsets[:, :, 0, :].astype(jnp.float32)
    found_second = jnp.where(position + 2 < sections_total, found_second, own_offsets[1])
    has_next = [
        ((position + d >= 0) & (position + d + 1 < sections_total)).astype(jnp.float32) for d in (-2, -1, 0, 1)
    ]
    pulls = [-h * f for h, f in zip(has_next, (found_behind2, found_behind, found_next, found_ahead))]
    behind_pos, positions, ahead_pos = (0.25 * (pulls[k + 1] - pulls[k]) for k in range(3))
    up = [(i, i + 1) for i in range(tiles - 1)]
    above = lax.ppermute(positions[:, GROUP:], "tile", up)
    below = lax.ppermute(positions[:, :GROUP], "tile", [(j, i) for i, j in up])
    widened = jnp.concatenate([above, positions, below], axis=1)
    count = positions.shape[1]
    links = node_links[:, 0, :] - (tile_index * count - NODE_COLS)
    extent = jnp.arange(count + 2 * NODE_COLS, dtype=jnp.int32)
    counts = jnp.sum((links[:, :, None] == extent[None, None, :]).astype(jnp.float32), axis=0)
    neighbours = jnp.sum(counts[None] * widened[:, None, :], axis=2)
    in_plane = 0.25 * (neighbours - 4.0 * positions)
    pull = has_next[2] * (ahead_pos - positions - found_next)
    pull_behind = has_next[1] * (positions - behind_pos - found_behind)
    positions = positions + 0.5 * (in_plane + 0.5 * (pull - pull_behind))
    shifts_found = jnp.stack([found_next, found_second])
    return (shifts_found[:, :, None, :], positions[:, None, :])


def solution(mesh):
    return jax.shard_map(
        shards,
        mesh=mesh,
        in_specs=(P("gz", "tile", None, None), P(None, None, "gz", "tile"), P(None, "gz", "tile")),
        out_specs=(P(None, None, "gz", "tile"), P(None, "gz", "tile")),
        check_vma=False,
    )
```

```python
import functools
import math

import jax
import jax.numpy as jnp
import ml_dtypes
import numpy as np
from jax import lax
from jax.experimental import pallas as pl
from jax.experimental.pallas import tpu as pltpu
from jax.sharding import PartitionSpec as P

NODE_COLS = 4
SIDE = 256
HALF = SIDE // 2
ROWS = 144
REACH = 4
SPAN = 16
GROUP = 4
NODES = 2
EXTRA = 16
BLOCK = NODES * SIDE + EXTRA
WINDOW = 6

STAGES = (
    ((), ()),
    (
        (((0, 1), (4, 5)), ((1, 2), (0, 2)), ((2, 4), (0, 1))),
        (((0, 1), (4, 5)), ((3, 4), (1, 3)), ((3, 5), (0, 1))),
    ),
    ((((2, 3), (3, 4)), ((1, 3), (3, 5))), (((2, 3), (1, 2)), ((0, 2), (2, 4)))),
)
GROUPS = 5
FOUND = 2 * GROUP * GROUPS


def pair_places(side):
    places, group = {}, 0
    for stage in STAGES:
        for pairs in stage[side]:
            for number, pair in enumerate(pairs):
                places.setdefault(pair, (group, number))
            group += 1
    return places


def stage_codes(number, side):
    codes = []
    for groups in zip(*STAGES[number]):
        both = [
            sum((a | b << 3 | (b - a - 1) << 6) << 8 * k for k, (a, b) in enumerate(pairs)) for pairs in groups
        ]
        codes.append(jnp.where(side == 0, jnp.int32(both[0]), jnp.int32(both[1])))
    return codes


def tables():
    index = np.arange(SIDE)

    def angle(phases):
        return (phases % SIDE).astype(np.float32) * np.float32(2.0 * math.pi / SIDE)

    phases = np.outer(index, index)
    cos_table = np.cos(angle(phases)).astype(ml_dtypes.bfloat16)
    sin_table = np.sin(angle(phases)).astype(ml_dtypes.bfloat16)
    right = np.concatenate([cos_table[: HALF + 1], sin_table[1:HALF]], axis=0)
    left = np.ascontiguousarray(right.T)
    row_freq = np.concatenate([np.arange(HALF + 1), -np.arange(1, HALF)])
    window = np.arange(-REACH, REACH + 1)
    fold_phase = 2.0 * math.pi * (np.outer(row_freq, window) % SIDE) / SIDE
    fold_cos, fold_sin = np.cos(fold_phase), np.sin(fold_phase)
    fold = np.zeros((GROUP, 2, SIDE, 2, 2, GROUP, SPAN), np.float32)
    for j in range(GROUP):
        for part, out, value in ((0, 0, fold_cos), (1, 0, -fold_sin), (0, 1, fold_sin), (1, 1, fold_cos)):
            high = value.astype(np.float32).astype(ml_dtypes.bfloat16).astype(np.float32)
            fold[j, part, :, out, 0, j, : window.size] = high
            fold[j, part, :, out, 1, j, : window.size] = value - high
    fold = fold.reshape(GROUP * 2 * SIDE, SIDE).astype(ml_dtypes.bfloat16)
    col_freq = np.arange(HALF + 1)
    twice = np.where((col_freq == 0) | (col_freq == HALF), 1.0, 2.0)[None, :] / SIDE
    col_phase = 2.0 * math.pi * (np.outer(window, col_freq) % SIDE) / SIDE
    close = np.zeros((2, SPAN, ROWS), np.float32)
    close[0, : window.size, : HALF + 1] = twice * np.cos(col_phase)
    close[1, : window.size, : HALF + 1] = twice * np.sin(col_phase)
    close = close.reshape(2 * SPAN, ROWS)
    high = close.astype(ml_dtypes.bfloat16)
    low = (close - high.astype(np.float32)).astype(ml_dtypes.bfloat16)
    lane, wide = np.arange(128)[:, None], np.arange(128 * GROUP)[None, :]
    spread = (lane // SPAN == wide // 128).astype(ml_dtypes.bfloat16)
    return right, left, fold, np.concatenate([high, low], axis=0), spread


def transform(patch, right, left):
    half_product = lax.dot_general(
        right, patch, (((1,), (1,)), ((), ())), preferred_element_type=jnp.float32
    ).astype(jnp.bfloat16)
    full = jnp.dot(half_product, left, preferred_element_type=jnp.float32)
    lane = lax.broadcasted_iota(jnp.int32, (HALF, HALF), 1)
    row = lax.broadcasted_iota(jnp.int32, (HALF, HALF), 0)
    first_lane, first_row = lane == 0, row == 0
    cc, sc = full[:HALF, :HALF], full[:HALF, HALF:]
    last_c, last_s = full[HALF:, :HALF], full[HALF:, HALF:]
    cs, ss = jnp.where(first_row, 0.0, last_c), jnp.where(first_row, 0.0, last_s)

    def parts(cc, sc, cs, ss, edge):
        low_sc, low_ss = jnp.where(edge, 0.0, sc), jnp.where(edge, 0.0, ss)
        return jnp.concatenate(
            [
                cc - low_ss,
                jnp.where(edge, sc, cc + ss),
                -(cs + low_sc),
                jnp.where(edge, -ss, sc - cs),
            ],
            axis=1,
        ).astype(jnp.bfloat16)

    def with_size(spectrum):
        real, imag = spectrum[:, :SIDE].astype(jnp.float32), spectrum[:, SIDE:].astype(jnp.float32)
        square = real * real + imag * imag
        return spectrum, square * lax.rsqrt(jnp.maximum(square, 1e-30))

    tail = ROWS - HALF
    keep = row[:tail] == 0
    end_c, end_s = jnp.where(keep, last_c[:tail], 0.0), jnp.where(keep, last_s[:tail], 0.0)
    none = jnp.zeros_like(end_c)
    main = with_size(parts(cc, sc, cs, ss, first_lane))
    return main, with_size(parts(end_c, end_s, none, none, first_lane[:tail]))


def stage_kernel(number, consts, blocks, state, scratch):
    right, left, fold, close, spread = consts
    specs, sizes, offs, found = state
    power, folded = scratch
    device = lax.rem(lax.axis_index("gz"), 4)
    row, side = device // 2, lax.rem(device, 2)
    codes = stage_codes(number, side)
    first_group = sum(len(stage[0]) for stage in STAGES[:number])
    near, far = 4 * row, 4 * (1 - row)
    places = ((near + side, 2 + side), (near + 1 - side, far + side, far + 1 - side), (3 - side,))[number]
    chunk = 16

    right_table, left_table = right[...], left[...]
    for block, place in zip(blocks, places):
        offs[place] = block[NODES * SIDE :, :]
        for n in range(NODES):
            patch = block[n * SIDE : (n + 1) * SIDE, :]
            main, end = transform(patch, right_table, left_table)
            specs[place * NODES + n, :HALF, :], sizes[place * NODES + n, :HALF, :] = main
            specs[place * NODES + n, HALF:, :], sizes[place * NODES + n, HALF:, :] = end

    for k, code in enumerate(codes):
        for j in range(GROUP):
            bits = jnp.right_shift(code, 8 * (j // NODES))
            a_at = (bits & 7) * NODES + j % NODES
            b_at = (jnp.right_shift(bits, 3) & 7) * NODES + j % NODES
            total = jnp.zeros((8, SIDE), jnp.float32)
            for start in range(0, ROWS, chunk):
                rows = slice(start, start + chunk)
                size = sizes[a_at, rows, :] * sizes[b_at, rows, :]
                if start == 0:
                    edge = lax.broadcasted_iota(jnp.int32, (chunk, SIDE), 0) == 0
                    size = jnp.where(edge, 0.5 * size, size)
                elif start == HALF:
                    size = 0.5 * size
                total = total + size[:8] + size[8:]
            floor = jnp.sum(total) * (2.0 / (SIDE * SIDE)) + 1e-6
            for start in range(0, ROWS, chunk):
                rows = slice(start, start + chunk)
                scale = pl.reciprocal(sizes[a_at, rows, :] * sizes[b_at, rows, :] + floor, approx=True)
                a = specs[a_at, rows, :].astype(jnp.float32)
                b = specs[b_at, rows, :].astype(jnp.float32)
                ar, ai, br, bi = a[:, :SIDE], a[:, SIDE:], b[:, :SIDE], b[:, SIDE:]
                br, bi = br * scale, bi * scale
                at = 2 * SIDE * j
                power[k, rows, at : at + SIDE] = (ar * br + ai * bi).astype(jnp.bfloat16)
                power[k, rows, at + SIDE : at + 2 * SIDE] = (ai * br - ar * bi).astype(jnp.bfloat16)
        folded[k] = jnp.dot(power[k], fold[...], preferred_element_type=jnp.float32)

    lane = lax.broadcasted_iota(jnp.int32, (SPAN, 128), 1)
    step_u = ((lane & (SPAN - 1)) - REACH).astype(jnp.float32)
    step_v = (lax.broadcasted_iota(jnp.int32, (SPAN, 128), 0) - REACH).astype(jnp.float32)
    for k, code in enumerate(codes):
        sums = folded[k]
        high = sums.astype(jnp.bfloat16)
        low = (sums - high.astype(jnp.float32)).astype(jnp.bfloat16)
        closed = jnp.dot(close[...], high, preferred_element_type=jnp.float32)
        rest = jnp.dot(close[: 2 * SPAN], low, preferred_element_type=jnp.float32)
        closed = closed[: 2 * SPAN] + closed[2 * SPAN :] + rest
        correlation = closed[:SPAN, :128] - closed[SPAN:, 128:]
        correlation = correlation + pltpu.roll(correlation, 64, axis=1)
        off_rows = []
        for pair in range(2):
            bits = jnp.right_shift(code, 8 * pair)
            own = offs[bits & 7].astype(jnp.float32)[:8, :128]
            own = jnp.where((jnp.right_shift(bits, 6) & 1) == 0, own[:4], own[4:])
            off_rows += [(own[n : n + 1], own[NODES + n : NODES + n + 1]) for n in range(NODES)]
        off_y, off_x = off_rows[3]
        for j in range(3):
            below = lane[:1] < SPAN * (j + 1)
            first = lane[:1] >= SPAN * j
            off_y = jnp.where(below & first, off_rows[j][0], off_y)
            off_x = jnp.where(below & first, off_rows[j][1], off_x)
        from_y, from_x = step_u - off_y, step_v - off_x
        inside = (jnp.abs(from_y) < 1.5) & (jnp.abs(from_x) < 1.5)
        weight = jnp.where(inside, jnp.exp(3.0 * jnp.tanh(correlation)), 0.0)
        sums = jnp.concatenate(
            [
                jnp.sum(weight, axis=0, keepdims=True),
                jnp.sum(weight * from_y, axis=0, keepdims=True),
                jnp.sum(weight * from_x, axis=0, keepdims=True),
                jnp.zeros((5, 128), jnp.float32),
            ],
            axis=0,
        )
        pieces = []
        for _ in range(3):
            pieces.append(sums.astype(jnp.bfloat16))
            sums = sums - pieces[-1].astype(jnp.float32)
        whole = jnp.dot(jnp.concatenate(pieces, axis=0), spread[...], preferred_element_type=jnp.float32)
        whole = whole[:8] + whole[8:16] + whole[16:]
        ratio_y, ratio_x = whole[1:2] / whole[0:1], whole[2:3] / whole[0:1]
        lines = []
        for j in range(GROUP):
            at = slice(128 * j, 128 * (j + 1))
            lines += [off_rows[j][0] + ratio_y[:, at], off_rows[j][1] + ratio_x[:, at]]
        found[8 * (first_group + k) : 8 * (first_group + k + 1), :] = jnp.concatenate(lines, axis=0)


def run_stage(number, consts, state, blocks):
    vmem, hbm = pl.BlockSpec(memory_space=pltpu.VMEM), pl.BlockSpec(memory_space=pltpu.HBM)
    shapes = (
        ((WINDOW * NODES, ROWS, 2 * SIDE), jnp.bfloat16),
        ((WINDOW * NODES, ROWS, SIDE), jnp.float32),
        ((WINDOW, EXTRA, SIDE), jnp.bfloat16),
        ((FOUND, 128), jnp.float32),
    )
    first = number == 0
    if first:
        consts = [pltpu.with_memory_space_constraint(c, pltpu.HBM) for c in consts]
        shapes += tuple((c.shape, c.dtype) for c in consts)
    count = len(consts)
    args = [*consts, *blocks, *state]
    fixed = count + len(blocks)

    def kernel(*refs):
        outs, scratch = refs[len(args) : len(args) + len(shapes)], refs[len(args) + len(shapes) :]
        tables_in, blocks_in = refs[:count], refs[count:fixed]
        if first:
            held, sems = outs[4:], scratch[-1]
            copies = [pltpu.make_async_copy(tables_in[k], held[k], sems.at[k]) for k in range(count)]
            for copy in copies:
                copy.start()
            for copy in copies:
                copy.wait()
            tables_in = held
        stage_kernel(number, tables_in, blocks_in, outs[:4], scratch[:2])

    groups = max(len(STAGES[number][0]), 1)
    out = pl.pallas_call(
        kernel,
        out_shape=tuple(pltpu.VMEM(shape, dtype) for shape, dtype in shapes),
        in_specs=[hbm if first else vmem] * count + [vmem] * (len(args) - count),
        out_specs=(vmem,) * len(shapes),
        input_output_aliases={fixed + k: k for k in range(len(state))},
        scratch_shapes=[
            pltpu.VMEM((groups, ROWS, 2 * SIDE * GROUP), jnp.bfloat16),
            pltpu.VMEM((groups, ROWS, SIDE), jnp.float32),
        ]
        + ([pltpu.SemaphoreType.DMA((count,))] if first else []),
        compiler_params=pltpu.CompilerParams(vmem_limit_bytes=24 * 1024 * 1024),
        cost_estimate=pl.CostEstimate(flops=1, bytes_accessed=1, transcendentals=0),
        name=f"stage{number}",
    )(*args)
    return tuple(out[:4]), tuple(out[4:])


def prepare_kernel(patches, offsets, *refs):
    blocks, sems = refs[:4], refs[4]
    device = lax.rem(lax.axis_index("gz"), 4)
    row, side = device // 2, lax.rem(device, 2)
    numbers = [2 * r + s for r in (row, 1 - row) for s in (side, 1 - side)]
    copies = []
    for k in (2, 3, 1, 0):
        copies.append(
            pltpu.make_async_copy(patches.at[numbers[k]], blocks[k].at[pl.ds(0, NODES * SIDE)], sems.at[k])
        )
        copies[-1].start()
    line = lax.broadcasted_iota(jnp.int32, (EXTRA, SIDE), 0)
    for block, number in zip(blocks, numbers):
        rows = jnp.zeros((EXTRA, SIDE), jnp.float32)
        for partner in range(2):
            for part in range(2):
                for n in range(NODES):
                    value = offsets[partner, part, NODES * number + n].astype(jnp.float32)
                    rows = jnp.where(line == 4 * partner + 2 * part + n, value, rows)
        block[NODES * SIDE :, :] = rows.astype(jnp.bfloat16)
    for copy in copies:
        copy.wait()


def prepare(patches, offsets):
    return pl.pallas_call(
        prepare_kernel,
        out_shape=tuple(pltpu.VMEM((BLOCK, SIDE), jnp.bfloat16) for _ in range(4)),
        in_specs=[pl.BlockSpec(memory_space=pltpu.HBM), pl.BlockSpec(memory_space=pltpu.SMEM)],
        out_specs=(pl.BlockSpec(memory_space=pltpu.VMEM),) * 4,
        scratch_shapes=[pltpu.SemaphoreType.DMA((4,))],
        cost_estimate=pl.CostEstimate(flops=1, bytes_accessed=1, transcendentals=0),
        name="prepare",
    )(
        pltpu.with_memory_space_constraint(patches.reshape(4, NODES * SIDE, SIDE), pltpu.HBM),
        offsets[:, :, 0, :],
    )


def finish_kernel(total, every, links, offsets, shifts, moved):
    position = lax.axis_index("gz")
    device = lax.rem(position, 4)
    lane = lax.broadcasted_iota(jnp.int32, (2, 128), 1)
    places = [pair_places(side) for side in range(2)]

    def put(held, start, row, section, partner, source):
        first = section + 2 * row
        for side in range(2):
            group, number = places[side][(first, first + partner)]
            for n in range(NODES):
                at = FOUND * source + 8 * group + 4 * number + 2 * n
                held = jnp.where(lane == start + 2 * side + n, every[2 * row + side, at : at + 2, :], held)
        return held

    def put_next(held, start, row, section, source):
        if row == 0 and section < 0:
            return put(held, start, 0, section + 4, 1, source + 2)
        if row == 1 and section > 2:
            return put(held, start, 1, section - 4, 1, source + 2)
        return put(held, start, row, section, 1, source)

    blank = jnp.zeros((2, 128), jnp.float32)
    next_all, second_all = [], []
    for section in range(-2, 5):
        held = put_next(blank, NODE_COLS, 0, section, 0)
        held = put_next(held, 2 * NODE_COLS, 1, section, 0)
        if -1 <= section < 4:
            held = put_next(held, 0, 1, section, 1)
            held = put_next(held, 3 * NODE_COLS, 0, section, 1)
        next_all.append(held)
    for section in range(4):
        held = put(blank, NODE_COLS, 0, section, 2, 0)
        if section < 2:
            held = put(held, 2 * NODE_COLS, 1, section, 2, 0)
        else:
            held = put(held, 2 * NODE_COLS, 1, section - 4, 2, 2)
        second_all.append(held)

    def pick(values):
        chosen = values[3]
        for r in range(3):
            chosen = jnp.where(device == r, values[r], chosen)
        return chosen

    behind2, behind, here, ahead = (pick(next_all[k : k + 4]) for k in range(4))
    found_next = jnp.where(position + 1 < total, here, offsets[0:2, :])
    found_second = jnp.where(position + 2 < total, pick(second_all), offsets[2:4, :])
    has_next = [
        jnp.where((position + d >= 0) & (position + d + 1 < total), 1.0, 0.0).astype(jnp.float32)
        for d in (-2, -1, 0, 1)
    ]
    pulls = [-h * f for h, f in zip(has_next, (behind2, behind, here, ahead))]
    behind_pos, positions, ahead_pos = (0.25 * (pulls[k + 1] - pulls[k]) for k in range(3))
    neighbours = blank
    for e in range(4 * NODE_COLS):
        count = jnp.sum(jnp.where(links[...] == e, 1.0, 0.0), axis=0, keepdims=True)
        neighbours = neighbours + count * positions[:, e : e + 1]
    in_plane = 0.25 * (neighbours - 4.0 * positions)
    pull = has_next[2] * (ahead_pos - positions - here)
    pull_behind = has_next[1] * (positions - behind_pos - behind)
    positions = positions + 0.5 * (in_plane + 0.5 * (pull - pull_behind))
    own = slice(NODE_COLS, 3 * NODE_COLS)
    for part in range(2):
        shifts[0, part] = found_next[part : part + 1, own]
        shifts[1, part] = found_second[part : part + 1, own]
        moved[part] = positions[part : part + 1, own]


def finish(every, links, offsets, total):
    vmem = pl.BlockSpec(memory_space=pltpu.VMEM)
    count = 2 * NODE_COLS
    return pl.pallas_call(
        functools.partial(finish_kernel, total),
        out_shape=(
            jax.ShapeDtypeStruct((2, 2, 1, count), jnp.float32),
            jax.ShapeDtypeStruct((2, 1, count), jnp.float32),
        ),
        in_specs=[vmem] * 3,
        out_specs=(vmem, vmem),
        cost_estimate=pl.CostEstimate(flops=1, bytes_accessed=1, transcendentals=0),
        name="finish",
    )(every, links, offsets)


def shards(sections, offsets, node_links):
    patches = sections[0]
    total, tiles = lax.axis_size("gz"), lax.axis_size("tile")
    tile_index = lax.axis_index("tile")

    def send(value, steps, tile_steps=(0, 0, 0, 0)):
        pairs = []
        for i in range(total):
            for t in range(tiles):
                j, to = i + steps[i % 4], t + tile_steps[i % 4]
                if 0 <= j < total and 0 <= to < tiles:
                    pairs.append((i * tiles + t, j * tiles + to))
        return lax.ppermute(value, ("gz", "tile"), pairs)

    kept, beside, across, slanted = prepare(patches, offsets)
    across_in = send(across, (2, 2, -2, -2))
    beside_in = send(beside, (1, -1, 1, -1))
    border_in = send(kept, (-4, -4, 4, 4))
    border_beside_in = send(beside, (-3, -5, 5, 3))
    slanted_in = send(slanted, (3, 1, -1, -3))
    state, consts = run_stage(0, [jnp.asarray(t) for t in tables()], (), [kept, across_in])
    state, _ = run_stage(1, consts, state, [beside_in, border_in, border_beside_in])
    state, _ = run_stage(2, consts, state, [slanted_in])
    found = state[3]

    from_tile = send(found, (0, 0, 0, 0), (-1, -1, 1, 1))
    both = jnp.concatenate([found, from_tile], axis=0)
    from_group = send(both, (4, 4, -4, -4))
    quads = [list(range(4 * g, 4 * g + 4)) for g in range(total // 4)]
    every = lax.all_gather(jnp.concatenate([both, from_group], axis=0), "gz", axis_index_groups=quads)
    count = 2 * NODE_COLS
    links = node_links[:, 0, :] - (tile_index * count - NODE_COLS)
    side_lanes = ((0, 0), (NODE_COLS, 128 - NODE_COLS - count))
    links = jnp.pad(links, side_lanes, constant_values=-1)
    own_offsets = jnp.pad(offsets.reshape(4, count).astype(jnp.float32), side_lanes)
    return finish(every, links, own_offsets, total)


def solution(mesh):
    return jax.shard_map(
        shards,
        mesh=mesh,
        in_specs=(P("gz", "tile", None, None), P(None, None, "gz", "tile"), P(None, "gz", "tile")),
        out_specs=(P(None, None, "gz", "tile"), P(None, "gz", "tile")),
        check_vma=False,
    )
```

```python
import functools
import math

import jax
import jax.numpy as jnp
import ml_dtypes
import numpy as np
from jax import lax
from jax.experimental import pallas as pl
from jax.experimental.pallas import tpu as pltpu
from jax.sharding import PartitionSpec as P

NODE_COLS = 4
SIDE = 256
HALF = SIDE // 2
ROWS = 144
REACH = 4
SPAN = 16
GROUP = 4
NODES = 2
EXTRA = 16
BLOCK = NODES * SIDE + EXTRA
BORDER = BLOCK + 16
LONG = BLOCK + 32
WINDOW = 6

STAGES = (
    ((), ()),
    (
        (((0, 1), (4, 5)), ((1, 2), (0, 2)), ((2, 4), (0, 1))),
        (((0, 1), (4, 5)), ((3, 4), (1, 3)), ((3, 5), (0, 1))),
    ),
    ((((2, 3), (3, 4)), ((1, 3), (3, 5))), (((2, 3), (1, 2)), ((0, 2), (2, 4)))),
)
GROUPS = 5
FOUND = 2 * GROUP


def pair_places(side):
    places, group = {}, 0
    for stage in STAGES:
        for pairs in stage[side]:
            for number, pair in enumerate(pairs):
                places.setdefault(pair, (group, number))
            group += 1
    return places


def stage_codes(number, side):
    codes = []
    for groups in zip(*STAGES[number]):
        both = [
            sum((a | b << 3 | (b - a - 1) << 6) << 8 * k for k, (a, b) in enumerate(pairs)) for pairs in groups
        ]
        codes.append(jnp.where(side == 0, jnp.int32(both[0]), jnp.int32(both[1])))
    return codes


def tables():
    index = np.arange(SIDE)

    def angle(phases):
        return (phases % SIDE).astype(np.float32) * np.float32(2.0 * math.pi / SIDE)

    phases = np.outer(index, index)
    cos_table = np.cos(angle(phases)).astype(ml_dtypes.bfloat16)
    sin_table = np.sin(angle(phases)).astype(ml_dtypes.bfloat16)
    right = np.concatenate([cos_table[: HALF + 1], sin_table[1:HALF]], axis=0)
    left = np.ascontiguousarray(right.T)
    row_freq = np.concatenate([np.arange(HALF + 1), -np.arange(1, HALF)])
    window = np.arange(-REACH, REACH + 1)
    fold_phase = 2.0 * math.pi * (np.outer(row_freq, window) % SIDE) / SIDE
    fold_cos, fold_sin = np.cos(fold_phase), np.sin(fold_phase)
    fold = np.zeros((GROUP, 2, SIDE, 2, 2, GROUP, SPAN), np.float32)
    for j in range(GROUP):
        for part, out, value in ((0, 0, fold_cos), (1, 0, -fold_sin), (0, 1, fold_sin), (1, 1, fold_cos)):
            high = value.astype(np.float32).astype(ml_dtypes.bfloat16).astype(np.float32)
            fold[j, part, :, out, 0, j, : window.size] = high
            fold[j, part, :, out, 1, j, : window.size] = value - high
    fold = fold.reshape(GROUP * 2 * SIDE, SIDE).astype(ml_dtypes.bfloat16)
    col_freq = np.arange(HALF + 1)
    twice = np.where((col_freq == 0) | (col_freq == HALF), 1.0, 2.0)[None, :] / SIDE
    col_phase = 2.0 * math.pi * (np.outer(window, col_freq) % SIDE) / SIDE
    close = np.zeros((2, SPAN, ROWS), np.float32)
    close[0, : window.size, : HALF + 1] = twice * np.cos(col_phase)
    close[1, : window.size, : HALF + 1] = twice * np.sin(col_phase)
    close = close.reshape(2 * SPAN, ROWS)
    high = close.astype(ml_dtypes.bfloat16)
    low = (close - high.astype(np.float32)).astype(ml_dtypes.bfloat16)
    lane, wide = np.arange(128)[:, None], np.arange(128 * GROUP)[None, :]
    spread = (lane // SPAN == wide // 128).astype(ml_dtypes.bfloat16)
    return right, left, fold, np.concatenate([high, low], axis=0), spread


def transform(patch, right, left):
    half_product = lax.dot_general(
        right, patch, (((1,), (1,)), ((), ())), preferred_element_type=jnp.float32
    ).astype(jnp.bfloat16)
    full = jnp.dot(half_product, left, preferred_element_type=jnp.float32)
    lane = lax.broadcasted_iota(jnp.int32, (HALF, HALF), 1)
    row = lax.broadcasted_iota(jnp.int32, (HALF, HALF), 0)
    first_lane, first_row = lane == 0, row == 0
    cc, sc = full[:HALF, :HALF], full[:HALF, HALF:]
    last_c, last_s = full[HALF:, :HALF], full[HALF:, HALF:]
    cs, ss = jnp.where(first_row, 0.0, last_c), jnp.where(first_row, 0.0, last_s)

    def parts(cc, sc, cs, ss, edge):
        low_sc, low_ss = jnp.where(edge, 0.0, sc), jnp.where(edge, 0.0, ss)
        return jnp.concatenate(
            [
                cc - low_ss,
                jnp.where(edge, sc, cc + ss),
                -(cs + low_sc),
                jnp.where(edge, -ss, sc - cs),
            ],
            axis=1,
        ).astype(jnp.bfloat16)

    def with_size(spectrum):
        real, imag = spectrum[:, :SIDE].astype(jnp.float32), spectrum[:, SIDE:].astype(jnp.float32)
        square = real * real + imag * imag
        return spectrum, square * lax.rsqrt(jnp.maximum(square, 1e-30))

    tail = ROWS - HALF
    keep = row[:tail] == 0
    end_c, end_s = jnp.where(keep, last_c[:tail], 0.0), jnp.where(keep, last_s[:tail], 0.0)
    none = jnp.zeros_like(end_c)
    main = with_size(parts(cc, sc, cs, ss, first_lane))
    return main, with_size(parts(end_c, end_s, none, none, first_lane[:tail]))


def stage_kernel(number, consts, blocks, state, scratch):
    right, left, fold, close, spread = consts
    specs, sizes, offs, found = state
    power, folded = scratch
    device = lax.axis_index("member")
    row, side = device // 2, lax.rem(device, 2)
    codes = stage_codes(number, side)
    first_group = sum(len(stage[0]) for stage in STAGES[:number])
    near, far = 4 * row, 4 * (1 - row)
    places = ((near + side, 2 + side), (near + 1 - side, far + side, far + 1 - side), (3 - side,))[number]
    chunk = 16

    if number == 0:
        found[...] = jnp.zeros_like(found)
    right_table, left_table = right[...], left[...]
    for block, place in zip(blocks, places):
        offs[place] = block[NODES * SIDE : BLOCK, :]
        for n in range(NODES):
            patch = block[n * SIDE : (n + 1) * SIDE, :]
            main, end = transform(patch, right_table, left_table)
            specs[place * NODES + n, :HALF, :], sizes[place * NODES + n, :HALF, :] = main
            specs[place * NODES + n, HALF:, :], sizes[place * NODES + n, HALF:, :] = end

    for k, code in enumerate(codes):
        for j in range(GROUP):
            bits = jnp.right_shift(code, 8 * (j // NODES))
            a_at = (bits & 7) * NODES + j % NODES
            b_at = (jnp.right_shift(bits, 3) & 7) * NODES + j % NODES
            total = jnp.zeros((8, SIDE), jnp.float32)
            for start in range(0, ROWS, chunk):
                rows = slice(start, start + chunk)
                size = sizes[a_at, rows, :] * sizes[b_at, rows, :]
                if start == 0:
                    edge = lax.broadcasted_iota(jnp.int32, (chunk, SIDE), 0) == 0
                    size = jnp.where(edge, 0.5 * size, size)
                elif start == HALF:
                    size = 0.5 * size
                total = total + size[:8] + size[8:]
            floor = jnp.sum(total) * (2.0 / (SIDE * SIDE)) + 1e-6
            for start in range(0, ROWS, chunk):
                rows = slice(start, start + chunk)
                scale = pl.reciprocal(sizes[a_at, rows, :] * sizes[b_at, rows, :] + floor, approx=True)
                a = specs[a_at, rows, :].astype(jnp.float32)
                b = specs[b_at, rows, :].astype(jnp.float32)
                ar, ai, br, bi = a[:, :SIDE], a[:, SIDE:], b[:, :SIDE], b[:, SIDE:]
                br, bi = br * scale, bi * scale
                at = 2 * SIDE * j
                power[k, rows, at : at + SIDE] = (ar * br + ai * bi).astype(jnp.bfloat16)
                power[k, rows, at + SIDE : at + 2 * SIDE] = (ai * br - ar * bi).astype(jnp.bfloat16)
        folded[k] = jnp.dot(power[k], fold[...], preferred_element_type=jnp.float32)

    lane = lax.broadcasted_iota(jnp.int32, (SPAN, 128), 1)
    step_u = ((lane & (SPAN - 1)) - REACH).astype(jnp.float32)
    step_v = (lax.broadcasted_iota(jnp.int32, (SPAN, 128), 0) - REACH).astype(jnp.float32)
    for k, code in enumerate(codes):
        sums = folded[k]
        high = sums.astype(jnp.bfloat16)
        low = (sums - high.astype(jnp.float32)).astype(jnp.bfloat16)
        closed = jnp.dot(close[...], high, preferred_element_type=jnp.float32)
        rest = jnp.dot(close[: 2 * SPAN], low, preferred_element_type=jnp.float32)
        closed = closed[: 2 * SPAN] + closed[2 * SPAN :] + rest
        correlation = closed[:SPAN, :128] - closed[SPAN:, 128:]
        correlation = correlation + pltpu.roll(correlation, 64, axis=1)
        off_rows = []
        for pair in range(2):
            bits = jnp.right_shift(code, 8 * pair)
            own = offs[bits & 7].astype(jnp.float32)[:8, :128]
            own = jnp.where((jnp.right_shift(bits, 6) & 1) == 0, own[:4], own[4:])
            off_rows += [(own[n : n + 1], own[NODES + n : NODES + n + 1]) for n in range(NODES)]
        off_y, off_x = off_rows[3]
        for j in range(3):
            below = lane[:1] < SPAN * (j + 1)
            first = lane[:1] >= SPAN * j
            off_y = jnp.where(below & first, off_rows[j][0], off_y)
            off_x = jnp.where(below & first, off_rows[j][1], off_x)
        from_y, from_x = step_u - off_y, step_v - off_x
        inside = (jnp.abs(from_y) < 1.5) & (jnp.abs(from_x) < 1.5)
        weight = jnp.where(inside, jnp.exp(3.0 * jnp.tanh(correlation)), 0.0)
        sums = jnp.concatenate(
            [
                jnp.sum(weight, axis=0, keepdims=True),
                jnp.sum(weight * from_y, axis=0, keepdims=True),
                jnp.sum(weight * from_x, axis=0, keepdims=True),
                jnp.zeros((5, 128), jnp.float32),
            ],
            axis=0,
        )
        pieces = []
        for _ in range(3):
            pieces.append(sums.astype(jnp.bfloat16))
            sums = sums - pieces[-1].astype(jnp.float32)
        whole = jnp.dot(jnp.concatenate(pieces, axis=0), spread[...], preferred_element_type=jnp.float32)
        whole = whole[:8] + whole[8:16] + whole[16:]
        ratio_y, ratio_x = whole[1:2] / whole[0:1], whole[2:3] / whole[0:1]
        lines = []
        for j in range(GROUP):
            at = slice(128 * j, 128 * (j + 1))
            lines += [off_rows[j][0] + ratio_y[:, at], off_rows[j][1] + ratio_x[:, at]]
        found[...] = jnp.where(lane[:FOUND] == first_group + k, jnp.concatenate(lines, axis=0), found[...])


def run_stage(number, consts, state, blocks):
    vmem, hbm = pl.BlockSpec(memory_space=pltpu.VMEM), pl.BlockSpec(memory_space=pltpu.HBM)
    shapes = (
        ((WINDOW * NODES, ROWS, 2 * SIDE), jnp.bfloat16),
        ((WINDOW * NODES, ROWS, SIDE), jnp.float32),
        ((WINDOW, EXTRA, SIDE), jnp.bfloat16),
        ((FOUND, 128), jnp.float32),
    )
    first = number == 0
    if first:
        consts = [pltpu.with_memory_space_constraint(c, pltpu.HBM) for c in consts]
        shapes += tuple((c.shape, c.dtype) for c in consts)
    count = len(consts)
    args = [*consts, *blocks, *state]
    fixed = count + len(blocks)

    def kernel(*refs):
        outs, scratch = refs[len(args) : len(args) + len(shapes)], refs[len(args) + len(shapes) :]
        tables_in, blocks_in = refs[:count], refs[count:fixed]
        if first:
            held, sems = outs[4:], scratch[-1]
            copies = [pltpu.make_async_copy(tables_in[k], held[k], sems.at[k]) for k in range(count)]
            for copy in copies:
                copy.start()
            for copy in copies[:2]:
                copy.wait()
            tables_in = held
        stage_kernel(number, tables_in, blocks_in, outs[:4], scratch[:2])
        if first:
            for copy in copies[2:]:
                copy.wait()

    groups = max(len(STAGES[number][0]), 1)
    out = pl.pallas_call(
        kernel,
        out_shape=tuple(pltpu.VMEM(shape, dtype) for shape, dtype in shapes),
        in_specs=[hbm if first else vmem] * count + [vmem] * (len(args) - count),
        out_specs=(vmem,) * len(shapes),
        input_output_aliases={fixed + k: k for k in range(len(state))},
        scratch_shapes=[
            pltpu.VMEM((groups, ROWS, 2 * SIDE * GROUP), jnp.bfloat16),
            pltpu.VMEM((groups, ROWS, SIDE), jnp.float32),
        ]
        + ([pltpu.SemaphoreType.DMA((count,))] if first else []),
        compiler_params=pltpu.CompilerParams(vmem_limit_bytes=24 * 1024 * 1024),
        cost_estimate=pl.CostEstimate(flops=1, bytes_accessed=1, transcendentals=0),
        name=f"stage{number}",
    )(*args)
    return tuple(out[:4]), tuple(out[4:])


def prepare_kernel(patches, offsets, *refs):
    blocks, sems = refs[:5], refs[5]
    device = lax.axis_index("member")
    row, side = device // 2, lax.rem(device, 2)
    numbers = [2 * r + s for r in (row, 1 - row) for s in (side, 1 - side)]
    numbers.append(numbers[1])
    copies = []
    for k in (2, 3, 0, 1, 4):
        copies.append(
            pltpu.make_async_copy(patches.at[numbers[k]], blocks[k].at[pl.ds(0, NODES * SIDE)], sems.at[k])
        )
        copies[-1].start()
    line = lax.broadcasted_iota(jnp.int32, (EXTRA, SIDE), 0)
    for block, number in zip(blocks, numbers):
        rows = jnp.zeros((EXTRA, SIDE), jnp.float32)
        for partner in range(2):
            for part in range(2):
                for n in range(NODES):
                    value = offsets[partner, part, 0, NODES * number + n].astype(jnp.float32)
                    rows = jnp.where(line == 4 * partner + 2 * part + n, value, rows)
        block[NODES * SIDE : BLOCK, :] = rows.astype(jnp.bfloat16)
    for block in blocks[:4]:
        block[BLOCK:, :] = jnp.zeros((block.shape[0] - BLOCK, SIDE), jnp.bfloat16)
    for copy in copies:
        copy.wait()


def prepare(patches, offsets):
    return pl.pallas_call(
        prepare_kernel,
        out_shape=tuple(pltpu.VMEM((rows, SIDE), jnp.bfloat16) for rows in (BORDER, BORDER, LONG, LONG, BLOCK)),
        in_specs=[pl.BlockSpec(memory_space=pltpu.HBM), pl.BlockSpec(memory_space=pltpu.SMEM)],
        out_specs=(pl.BlockSpec(memory_space=pltpu.VMEM),) * 5,
        scratch_shapes=[pltpu.SemaphoreType.DMA((5,))],
        cost_estimate=pl.CostEstimate(flops=1, bytes_accessed=1, transcendentals=0),
        name="prepare",
    )(
        pltpu.with_memory_space_constraint(patches.reshape(4, NODES * SIDE, SIDE), pltpu.HBM),
        offsets,
    )


def finish_kernel(total, every, node_links, node_offsets, shifts, moved, links, offsets):
    device, tile = lax.axis_index("member"), lax.axis_index("tile")
    position = 4 * lax.axis_index("group") + device
    lane = lax.broadcasted_iota(jnp.int32, (2, 128), 1)
    own = slice(NODE_COLS, 3 * NODE_COLS)
    tiles = lax.axis_size("tile")
    links[...] = jnp.full_like(links, -1)
    offsets[...] = jnp.zeros_like(offsets)
    for k in range(4):
        links[k : k + 1, own] = node_links[k] - (tile * 2 * NODE_COLS - NODE_COLS)
        offsets[k : k + 1, own] = node_offsets[k // 2, k % 2].astype(jnp.float32)
    places = [pair_places(side) for side in range(2)]
    spread = {}
    near_tiles = {0: tile, -1: jnp.maximum(tile - 1, 0), 1: jnp.minimum(tile + 1, tiles - 1)}

    def shifts_of(member, step, column):
        if (member, step, column) not in spread:
            values = every[member * tiles + near_tiles[step]][:, column : column + 1]
            spread[member, step, column] = jnp.broadcast_to(values, (FOUND, 128))
        return spread[member, step, column]

    def put(held, start, row, section, partner, step, source=0):
        first = section + 2 * row
        for side in range(2):
            group, number = places[side][(first, first + partner)]
            for n in range(NODES):
                at = 4 * number + 2 * n
                value = shifts_of(2 * row + side, step, GROUPS * source + group)[at : at + 2]
                held = jnp.where(lane == start + 2 * side + n, value, held)
        return held

    def put_next(held, start, row, section, step):
        if row == 0 and section < 0:
            return put(held, start, 0, section + 4, 1, step, 1)
        if row == 1 and section > 2:
            return put(held, start, 1, section - 4, 1, step, 1)
        return put(held, start, row, section, 1, step)

    blank = jnp.zeros((2, 128), jnp.float32)
    next_all, second_all = [], []
    for section in range(-2, 5):
        held = put_next(blank, NODE_COLS, 0, section, 0)
        held = put_next(held, 2 * NODE_COLS, 1, section, 0)
        if -1 <= section < 4:
            held = put_next(held, 0, 1, section, -1)
            held = put_next(held, 3 * NODE_COLS, 0, section, 1)
        next_all.append(held)
    for section in range(4):
        held = put(blank, NODE_COLS, 0, section, 2, 0)
        if section < 2:
            held = put(held, 2 * NODE_COLS, 1, section, 2, 0)
        else:
            held = put(held, 2 * NODE_COLS, 1, section - 4, 2, 0, 1)
        second_all.append(held)

    def pick(values):
        chosen = values[3]
        for r in range(3):
            chosen = jnp.where(device == r, values[r], chosen)
        return chosen

    behind2, behind, here, ahead = (pick(next_all[k : k + 4]) for k in range(4))
    found_next = jnp.where(position + 1 < total, here, offsets[0:2, :])
    found_second = jnp.where(position + 2 < total, pick(second_all), offsets[2:4, :])
    has_next = [
        jnp.where((position + d >= 0) & (position + d + 1 < total), 1.0, 0.0).astype(jnp.float32)
        for d in (-2, -1, 0, 1)
    ]
    pulls = [-h * f for h, f in zip(has_next, (behind2, behind, here, ahead))]
    behind_pos, positions, ahead_pos = (0.25 * (pulls[k + 1] - pulls[k]) for k in range(3))
    neighbours = blank
    for e in range(4 * NODE_COLS):
        count = jnp.sum(jnp.where(links[0:4, :] == e, 1.0, 0.0), axis=0, keepdims=True)
        neighbours = neighbours + count * positions[:, e : e + 1]
    in_plane = 0.25 * (neighbours - 4.0 * positions)
    pull = has_next[2] * (ahead_pos - positions - here)
    pull_behind = has_next[1] * (positions - behind_pos - behind)
    positions = positions + 0.5 * (in_plane + 0.5 * (pull - pull_behind))
    for part in range(2):
        shifts[0, part] = found_next[part : part + 1, own]
        shifts[1, part] = found_second[part : part + 1, own]
        moved[part] = positions[part : part + 1, own]


def finish(every, links, offsets, total):
    vmem = pl.BlockSpec(memory_space=pltpu.VMEM)
    count = 2 * NODE_COLS
    return pl.pallas_call(
        functools.partial(finish_kernel, total),
        out_shape=(
            jax.ShapeDtypeStruct((2, 2, 1, count), jnp.float32),
            jax.ShapeDtypeStruct((2, 1, count), jnp.float32),
        ),
        in_specs=[vmem] * 3,
        out_specs=(vmem, vmem),
        scratch_shapes=[pltpu.VMEM((8, 128), jnp.int32), pltpu.VMEM((8, 128), jnp.float32)],
        cost_estimate=pl.CostEstimate(flops=1, bytes_accessed=1, transcendentals=0),
        name="finish",
    )(every, links, offsets)


def shards(sections, offsets, node_links):
    patches = sections[0]
    groups, tiles = lax.axis_size("group"), lax.axis_size("tile")

    def send(value, steps):
        total = 4 * groups
        pairs = [(i, i + steps[i % 4]) for i in range(total) if 0 <= i + steps[i % 4] < total]
        return lax.ppermute(value, ("group", "member"), pairs)

    kept, beside, across, slanted, beside_core = prepare(patches, offsets)
    across_in = send(across, (2, 2, -2, -2))
    beside_in = send(beside_core, (1, -1, 1, -1))
    border_in = send(kept, (-4, -4, 4, 4))
    border_beside_in = send(beside, (-3, -5, 5, 3))
    slanted_in = send(slanted, (3, 1, -1, -3))
    state, consts = run_stage(0, [jnp.asarray(t) for t in tables()], (), [kept, across_in])
    state, _ = run_stage(1, consts, state, [beside_in, border_in, border_beside_in])
    state, _ = run_stage(2, consts, state, [slanted_in])
    found = state[3]

    rest = jnp.zeros((FOUND, 128 - 2 * GROUPS), jnp.float32)
    near = send(found, (4, 4, -4, -4))
    found = jnp.concatenate([found[:, :GROUPS], near[:, :GROUPS], rest], axis=1)
    every = lax.all_to_all(jnp.broadcast_to(found[None], (4 * tiles, FOUND, 128)), ("member", "tile"), 0, 0)
    return finish(every, node_links, offsets, 4 * groups)


def solution(mesh):
    sections, tiles = mesh.devices.shape
    mesh = jax.sharding.Mesh(mesh.devices.reshape(sections // 4, 4, tiles), ("group", "member", "tile"))
    gz = ("group", "member")
    return jax.shard_map(
        shards,
        mesh=mesh,
        in_specs=(P(gz, "tile", None, None), P(None, None, gz, "tile"), P(None, gz, "tile")),
        out_specs=(P(None, None, gz, "tile"), P(None, gz, "tile")),
        check_vma=False,
    )
```

```python
import functools
import math

import jax
import jax.numpy as jnp
import ml_dtypes
import numpy as np
from jax import lax
from jax.experimental import pallas as pl
from jax.experimental.pallas import tpu as pltpu
from jax.sharding import PartitionSpec as P

NODE_COLS = 4
SIDE = 256
HALF = SIDE // 2
ROWS = 144
REACH = 4
SPAN = 16
GROUP = 4
NODES = 2
EXTRA = 16
BLOCK = NODES * SIDE + EXTRA
LONG = BLOCK + 16
WINDOW = 6

STAGES = (
    ((), ()),
    ((((0, 2), (2, 4)),), (((1, 3), (3, 5)),)),
    ((((0, 1), (4, 5)), ((1, 2),)), (((0, 1), (4, 5)), ((3, 4),))),
    ((((2, 3), (3, 4)), ((1, 3), (3, 5))), (((2, 3), (1, 2)), ((0, 2), (2, 4)))),
)
GROUPS = 5
FOUND = GROUP * GROUPS


def pair_places(side):
    places, group = {}, 0
    for stage in STAGES:
        for pairs in stage[side]:
            for number, pair in enumerate(pairs):
                places.setdefault(pair, (group, number))
            group += 1
    return places


def stage_codes(number, side):
    codes = []
    for groups in zip(*STAGES[number]):
        both = [
            sum((a | b << 3 | (b - a - 1) << 6) << 8 * k for k, (a, b) in enumerate(pairs)) for pairs in groups
        ]
        codes.append(jnp.where(side == 0, jnp.int32(both[0]), jnp.int32(both[1])))
    return codes


def tables():
    index = np.arange(SIDE)

    def angle(phases):
        return (phases % SIDE).astype(np.float32) * np.float32(2.0 * math.pi / SIDE)

    phases = np.outer(index, index)
    cos_table = np.cos(angle(phases)).astype(ml_dtypes.bfloat16)
    sin_table = np.sin(angle(phases)).astype(ml_dtypes.bfloat16)
    right = np.concatenate([cos_table[: HALF + 1], sin_table[1:HALF]], axis=0)
    left = np.ascontiguousarray(right.T)
    row_freq = np.concatenate([np.arange(HALF + 1), -np.arange(1, HALF)])
    window = np.arange(-REACH, REACH + 1)
    fold_phase = 2.0 * math.pi * (np.outer(row_freq, window) % SIDE) / SIDE
    fold_cos, fold_sin = np.cos(fold_phase), np.sin(fold_phase)
    fold = np.zeros((GROUP, 2, SIDE, 2, 2, GROUP, SPAN), np.float32)
    for j in range(GROUP):
        for part, out, value in ((0, 0, fold_cos), (1, 0, -fold_sin), (0, 1, fold_sin), (1, 1, fold_cos)):
            high = value.astype(np.float32).astype(ml_dtypes.bfloat16).astype(np.float32)
            fold[j, part, :, out, 0, j, : window.size] = high
            fold[j, part, :, out, 1, j, : window.size] = value - high
    fold = fold.reshape(GROUP * 2 * SIDE, SIDE).astype(ml_dtypes.bfloat16)
    col_freq = np.arange(HALF + 1)
    twice = np.where((col_freq == 0) | (col_freq == HALF), 1.0, 2.0)[None, :] / SIDE
    col_phase = 2.0 * math.pi * (np.outer(window, col_freq) % SIDE) / SIDE
    close = np.zeros((2, SPAN, ROWS), np.float32)
    close[0, : window.size, : HALF + 1] = twice * np.cos(col_phase)
    close[1, : window.size, : HALF + 1] = twice * np.sin(col_phase)
    close = close.reshape(2 * SPAN, ROWS)
    high = close.astype(ml_dtypes.bfloat16)
    low = (close - high.astype(np.float32)).astype(ml_dtypes.bfloat16)
    lane, wide = np.arange(128)[:, None], np.arange(128 * GROUP)[None, :]
    spread = (lane // SPAN == wide // 128).astype(ml_dtypes.bfloat16)
    return right, left, fold, np.concatenate([high, low], axis=0), spread


def transform(patch, right, left):
    half_product = lax.dot_general(
        right, patch, (((1,), (1,)), ((), ())), preferred_element_type=jnp.float32
    ).astype(jnp.bfloat16)
    full = jnp.dot(half_product, left, preferred_element_type=jnp.float32)
    lane = lax.broadcasted_iota(jnp.int32, (HALF, HALF), 1)
    row = lax.broadcasted_iota(jnp.int32, (HALF, HALF), 0)
    first_lane, first_row = lane == 0, row == 0
    cc, sc = full[:HALF, :HALF], full[:HALF, HALF:]
    last_c, last_s = full[HALF:, :HALF], full[HALF:, HALF:]
    cs, ss = jnp.where(first_row, 0.0, last_c), jnp.where(first_row, 0.0, last_s)

    def parts(cc, sc, cs, ss, edge):
        low_sc, low_ss = jnp.where(edge, 0.0, sc), jnp.where(edge, 0.0, ss)
        return jnp.concatenate(
            [
                cc - low_ss,
                jnp.where(edge, sc, cc + ss),
                -(cs + low_sc),
                jnp.where(edge, -ss, sc - cs),
            ],
            axis=1,
        ).astype(jnp.bfloat16)

    def with_size(spectrum):
        real, imag = spectrum[:, :SIDE].astype(jnp.float32), spectrum[:, SIDE:].astype(jnp.float32)
        square = real * real + imag * imag
        return spectrum, square * lax.rsqrt(jnp.maximum(square, 1e-30))

    tail = ROWS - HALF
    keep = row[:tail] == 0
    end_c, end_s = jnp.where(keep, last_c[:tail], 0.0), jnp.where(keep, last_s[:tail], 0.0)
    none = jnp.zeros_like(end_c)
    main = with_size(parts(cc, sc, cs, ss, first_lane))
    return main, with_size(parts(end_c, end_s, none, none, first_lane[:tail]))


def stage_kernel(number, consts, blocks, state, scratch):
    right, left, fold, close, spread = consts
    specs, sizes, offs, found = state
    power, folded = scratch
    device = lax.axis_index("member")
    row, side = device // 2, lax.rem(device, 2)
    codes = stage_codes(number, side)
    first_group = sum(len(stage[0]) for stage in STAGES[:number])
    near, far = 4 * row, 4 * (1 - row)
    places = ((near + side, far + side), (2 + side,), (far + 1 - side, near + 1 - side), (3 - side,))[number]
    chunk = 16

    if number == 0:
        found[...] = jnp.zeros_like(found)
    right_table, left_table = right[...], left[...]
    for block, place in zip(blocks, places):
        offs[place] = block[NODES * SIDE : BLOCK, :]
        for n in range(NODES):
            patch = block[n * SIDE : (n + 1) * SIDE, :]
            main, end = transform(patch, right_table, left_table)
            specs[place * NODES + n, :HALF, :], sizes[place * NODES + n, :HALF, :] = main
            specs[place * NODES + n, HALF:, :], sizes[place * NODES + n, HALF:, :] = end

    for k, code in enumerate(codes):
        held = NODES * len(STAGES[number][0][k])
        if held < GROUP:
            power[k, :, 2 * SIDE * held :] = jnp.zeros((ROWS, 2 * SIDE * (GROUP - held)), jnp.bfloat16)
        for j in range(held):
            bits = jnp.right_shift(code, 8 * (j // NODES))
            a_at = (bits & 7) * NODES + j % NODES
            b_at = (jnp.right_shift(bits, 3) & 7) * NODES + j % NODES
            total = jnp.zeros((8, SIDE), jnp.float32)
            for start in range(0, ROWS, chunk):
                rows = slice(start, start + chunk)
                size = sizes[a_at, rows, :] * sizes[b_at, rows, :]
                if start == 0:
                    edge = lax.broadcasted_iota(jnp.int32, (chunk, SIDE), 0) == 0
                    size = jnp.where(edge, 0.5 * size, size)
                elif start == HALF:
                    size = 0.5 * size
                total = total + size[:8] + size[8:]
            floor = jnp.sum(total) * (2.0 / (SIDE * SIDE)) + 1e-6
            for start in range(0, ROWS, chunk):
                rows = slice(start, start + chunk)
                scale = pl.reciprocal(sizes[a_at, rows, :] * sizes[b_at, rows, :] + floor, approx=True)
                a = specs[a_at, rows, :].astype(jnp.float32)
                b = specs[b_at, rows, :].astype(jnp.float32)
                ar, ai, br, bi = a[:, :SIDE], a[:, SIDE:], b[:, :SIDE], b[:, SIDE:]
                br, bi = br * scale, bi * scale
                at = 2 * SIDE * j
                power[k, rows, at : at + SIDE] = (ar * br + ai * bi).astype(jnp.bfloat16)
                power[k, rows, at + SIDE : at + 2 * SIDE] = (ai * br - ar * bi).astype(jnp.bfloat16)
        folded[k] = jnp.dot(power[k], fold[...], preferred_element_type=jnp.float32)

    lane = lax.broadcasted_iota(jnp.int32, (SPAN, 128), 1)
    step_u = ((lane & (SPAN - 1)) - REACH).astype(jnp.float32)
    step_v = (lax.broadcasted_iota(jnp.int32, (SPAN, 128), 0) - REACH).astype(jnp.float32)
    for k, code in enumerate(codes):
        sums = folded[k]
        high = sums.astype(jnp.bfloat16)
        low = (sums - high.astype(jnp.float32)).astype(jnp.bfloat16)
        closed = jnp.dot(close[...], high, preferred_element_type=jnp.float32)
        rest = jnp.dot(close[: 2 * SPAN], low, preferred_element_type=jnp.float32)
        closed = closed[: 2 * SPAN] + closed[2 * SPAN :] + rest
        correlation = closed[:SPAN, :128] - closed[SPAN:, 128:]
        correlation = correlation + pltpu.roll(correlation, 64, axis=1)
        off_rows = []
        for pair in range(2):
            bits = jnp.right_shift(code, 8 * pair)
            own = offs[bits & 7].astype(jnp.float32)[:8, :128]
            own = jnp.where((jnp.right_shift(bits, 6) & 1) == 0, own[:4], own[4:])
            off_rows += [(own[n : n + 1], own[NODES + n : NODES + n + 1]) for n in range(NODES)]
        off_y, off_x = off_rows[3]
        for j in range(3):
            below = lane[:1] < SPAN * (j + 1)
            first = lane[:1] >= SPAN * j
            off_y = jnp.where(below & first, off_rows[j][0], off_y)
            off_x = jnp.where(below & first, off_rows[j][1], off_x)
        from_y, from_x = step_u - off_y, step_v - off_x
        inside = (jnp.abs(from_y) < 1.5) & (jnp.abs(from_x) < 1.5)
        weight = jnp.where(inside, jnp.exp(3.0 * jnp.tanh(correlation)), 0.0)
        sums = jnp.concatenate(
            [
                jnp.sum(weight, axis=0, keepdims=True),
                jnp.sum(weight * from_y, axis=0, keepdims=True),
                jnp.sum(weight * from_x, axis=0, keepdims=True),
                jnp.zeros((5, 128), jnp.float32),
            ],
            axis=0,
        )
        pieces = []
        for _ in range(3):
            pieces.append(sums.astype(jnp.bfloat16))
            sums = sums - pieces[-1].astype(jnp.float32)
        whole = jnp.dot(jnp.concatenate(pieces, axis=0), spread[...], preferred_element_type=jnp.float32)
        whole = whole[:8] + whole[8:16] + whole[16:]
        ratio_y, ratio_x = whole[1:2] / whole[0:1], whole[2:3] / whole[0:1]
        for j in range(GROUP):
            at = slice(128 * j, 128 * (j + 1))
            both = jnp.concatenate([off_rows[j][0] + ratio_y[:, at], off_rows[j][1] + ratio_x[:, at]], axis=0)
            found[...] = jnp.where(lane[:2] == GROUP * (first_group + k) + j, both, found[...])


def run_stage(number, consts, state, blocks, mesh_inputs=()):
    vmem, hbm = pl.BlockSpec(memory_space=pltpu.VMEM), pl.BlockSpec(memory_space=pltpu.HBM)
    shapes = (
        ((WINDOW * NODES, ROWS, 2 * SIDE), jnp.bfloat16),
        ((WINDOW * NODES, ROWS, SIDE), jnp.float32),
        ((WINDOW, EXTRA, SIDE), jnp.bfloat16),
        ((2, 128), jnp.float32),
    )
    first = number == 0
    if first:
        consts = [pltpu.with_memory_space_constraint(c, pltpu.HBM) for c in consts]
        shapes += tuple((c.shape, c.dtype) for c in consts)
        shapes += (((4 * NODE_COLS, 128), jnp.float32), ((8, 128), jnp.float32))
        mesh_inputs = [pltpu.with_memory_space_constraint(x, pltpu.HBM) for x in mesh_inputs]
    count = len(consts)
    args = [*consts, *blocks, *state, *mesh_inputs]
    fixed = count + len(blocks)

    def kernel(*refs):
        outs, scratch = refs[len(args) : len(args) + len(shapes)], refs[len(args) + len(shapes) :]
        tables_in, blocks_in = refs[:count], refs[count:fixed]
        if first:
            held, sems = outs[4 : 4 + count], scratch[-1]
            sources = [*tables_in, *refs[fixed : len(args)]]
            targets = [*held, *scratch[2:4]]
            copies = [pltpu.make_async_copy(a, b, sems.at[k]) for k, (a, b) in enumerate(zip(sources, targets))]
            for copy in copies:
                copy.start()
            for copy in copies[:2]:
                copy.wait()
            tables_in = held
        stage_kernel(number, tables_in, blocks_in, outs[:4], scratch[:2])
        if first:
            for copy in copies[2:]:
                copy.wait()
            mesh_rows(*scratch[2:4], *outs[4 + count :], scratch[4])

    groups = max(len(STAGES[number][0]), 1)
    out = pl.pallas_call(
        kernel,
        out_shape=tuple(pltpu.VMEM(shape, dtype) for shape, dtype in shapes),
        in_specs=[hbm if first else vmem] * count
        + [vmem] * (len(args) - count - len(mesh_inputs))
        + [hbm] * len(mesh_inputs),
        out_specs=(vmem,) * len(shapes),
        input_output_aliases={fixed + k: k for k in range(len(state))},
        scratch_shapes=[
            pltpu.VMEM((groups, ROWS, 2 * SIDE * GROUP), jnp.bfloat16),
            pltpu.VMEM((groups, ROWS, SIDE), jnp.float32),
        ]
        + [pltpu.VMEM(x.shape, x.dtype) for x in mesh_inputs]
        + ([pltpu.VMEM((8, 128), jnp.int32), pltpu.SemaphoreType.DMA((count + 2,))] if first else []),
        compiler_params=pltpu.CompilerParams(vmem_limit_bytes=24 * 1024 * 1024),
        cost_estimate=pl.CostEstimate(flops=1, bytes_accessed=1, transcendentals=0),
        name=f"stage{number}",
    )(*args)
    return tuple(out[:4]), tuple(out[4:])


def mesh_rows(node_links, node_offsets, counts, offsets, links):
    own = slice(NODE_COLS, 3 * NODE_COLS)
    links[...] = jnp.full_like(links, -1)
    offsets[...] = jnp.zeros_like(offsets)
    first = (lax.axis_index("tile") * 2 - 1) * NODE_COLS
    for k in range(4):
        links[k : k + 1, own] = node_links[k] - first
        offsets[k : k + 1, own] = node_offsets[k // 2, k % 2].astype(jnp.float32)
    for e in range(4 * NODE_COLS):
        counts[e : e + 1, :] = jnp.sum(jnp.where(links[0:4, :] == e, 1.0, 0.0), axis=0, keepdims=True)


def prepare_kernel(patches, all_offsets, *refs):
    blocks, offsets, sems = refs[:4], refs[4], refs[5]
    device = lax.axis_index("member")
    row, side = device // 2, lax.rem(device, 2)
    numbers = [2 * r + s for r in (row, 1 - row) for s in (side, 1 - side)]
    copies = []
    for k in (2, 3, 0, 1):
        copies.append(
            pltpu.make_async_copy(patches.at[numbers[k]], blocks[k].at[pl.ds(0, NODES * SIDE)], sems.at[k])
        )
        copies[-1].start()
    offsets_copy = pltpu.make_async_copy(all_offsets, offsets, sems.at[4])
    offsets_copy.start()
    offsets_copy.wait()
    line = lax.broadcasted_iota(jnp.int32, (EXTRA, SIDE), 0)
    for block, number in zip(blocks, numbers):
        rows = jnp.zeros((EXTRA, SIDE), jnp.float32)
        for partner in range(2):
            for part in range(2):
                for n in range(NODES):
                    value = offsets[partner, part, 0, NODES * number + n].astype(jnp.float32)
                    rows = jnp.where(line == 4 * partner + 2 * part + n, value, rows)
        block[NODES * SIDE : BLOCK, :] = rows.astype(jnp.bfloat16)
    for block in blocks[2:]:
        block[BLOCK:, :] = jnp.zeros((block.shape[0] - BLOCK, SIDE), jnp.bfloat16)
    for copy in copies:
        copy.wait()


def prepare(patches, offsets):
    return pl.pallas_call(
        prepare_kernel,
        out_shape=tuple(pltpu.VMEM((rows, SIDE), jnp.bfloat16) for rows in (BLOCK, BLOCK, LONG, LONG)),
        in_specs=[pl.BlockSpec(memory_space=pltpu.HBM)] * 2,
        out_specs=(pl.BlockSpec(memory_space=pltpu.VMEM),) * 4,
        scratch_shapes=[pltpu.SMEM((2, 2, 1, 2 * GROUP), jnp.int32), pltpu.SemaphoreType.DMA((5,))],
        cost_estimate=pl.CostEstimate(flops=1, bytes_accessed=1, transcendentals=0),
        name="prepare",
    )(
        pltpu.with_memory_space_constraint(patches.reshape(4, NODES * SIDE, SIDE), pltpu.HBM),
        pltpu.with_memory_space_constraint(offsets, pltpu.HBM),
    )


def finish_kernel(total, every, counts, offsets, shifts, moved):
    device, tile = lax.axis_index("member"), lax.axis_index("tile")
    position = 4 * lax.axis_index("group") + device
    lane = lax.broadcasted_iota(jnp.int32, (2, 128), 1)
    own = slice(NODE_COLS, 3 * NODE_COLS)
    tiles = lax.axis_size("tile")
    places = [pair_places(side) for side in range(2)]
    spread = {}
    near_tiles = {0: tile, -1: jnp.maximum(tile - 1, 0), 1: jnp.minimum(tile + 1, tiles - 1)}

    def shifts_of(member, step, column):
        if (member, step, column) not in spread:
            values = every[member * tiles + near_tiles[step]][:, column : column + 1]
            spread[member, step, column] = jnp.broadcast_to(values, (2, 128))
        return spread[member, step, column]

    def put(held, start, row, section, partner, step, source=0):
        first = section + 2 * row
        for side in range(2):
            group, number = places[side][(first, first + partner)]
            for n in range(NODES):
                value = shifts_of(2 * row + side, step, FOUND * source + GROUP * group + NODES * number + n)
                held = jnp.where(lane == start + 2 * side + n, value, held)
        return held

    def put_next(held, start, row, section, step):
        if row == 0 and section < 0:
            return put(held, start, 0, section + 4, 1, step, 1)
        if row == 1 and section > 2:
            return put(held, start, 1, section - 4, 1, step, 1)
        return put(held, start, row, section, 1, step)

    blank = jnp.zeros((2, 128), jnp.float32)
    next_all, second_all = [], []
    for section in range(-2, 5):
        held = put_next(blank, NODE_COLS, 0, section, 0)
        held = put_next(held, 2 * NODE_COLS, 1, section, 0)
        if -1 <= section < 4:
            held = put_next(held, 0, 1, section, -1)
            held = put_next(held, 3 * NODE_COLS, 0, section, 1)
        next_all.append(held)
    for section in range(4):
        held = put(blank, NODE_COLS, 0, section, 2, 0)
        if section < 2:
            held = put(held, 2 * NODE_COLS, 1, section, 2, 0)
        else:
            held = put(held, 2 * NODE_COLS, 1, section - 4, 2, 0, 1)
        second_all.append(held)

    def pick(values):
        chosen = values[3]
        for r in range(3):
            chosen = jnp.where(device == r, values[r], chosen)
        return chosen

    behind2, behind, here, ahead = (pick(next_all[k : k + 4]) for k in range(4))
    found_next = jnp.where(position + 1 < total, here, offsets[0:2, :])
    found_second = jnp.where(position + 2 < total, pick(second_all), offsets[2:4, :])
    has_next = [
        jnp.where((position + d >= 0) & (position + d + 1 < total), 1.0, 0.0).astype(jnp.float32)
        for d in (-2, -1, 0, 1)
    ]
    pulls = [-h * f for h, f in zip(has_next, (behind2, behind, here, ahead))]
    behind_pos, positions, ahead_pos = (0.25 * (pulls[k + 1] - pulls[k]) for k in range(3))
    neighbours = blank
    for e in range(4 * NODE_COLS):
        neighbours = neighbours + counts[e : e + 1, :] * positions[:, e : e + 1]
    in_plane = 0.25 * (neighbours - 4.0 * positions)
    pull = has_next[2] * (ahead_pos - positions - here)
    pull_behind = has_next[1] * (positions - behind_pos - behind)
    positions = positions + 0.5 * (in_plane + 0.5 * (pull - pull_behind))
    for part in range(2):
        shifts[0, part] = found_next[part : part + 1, own]
        shifts[1, part] = found_second[part : part + 1, own]
        moved[part] = positions[part : part + 1, own]


def finish(every, counts, offsets, total):
    vmem = pl.BlockSpec(memory_space=pltpu.VMEM)
    nodes = 2 * NODE_COLS
    return pl.pallas_call(
        functools.partial(finish_kernel, total),
        out_shape=(
            jax.ShapeDtypeStruct((2, 2, 1, nodes), jnp.float32),
            jax.ShapeDtypeStruct((2, 1, nodes), jnp.float32),
        ),
        in_specs=[vmem] * 3,
        out_specs=(vmem, vmem),
        cost_estimate=pl.CostEstimate(flops=1, bytes_accessed=1, transcendentals=0),
        name="finish",
    )(every, counts, offsets)


def shards(sections, offsets, node_links):
    patches = sections[0]
    groups, tiles = lax.axis_size("group"), lax.axis_size("tile")

    def send(value, steps):
        total = 4 * groups
        pairs = [(i, i + steps[i % 4]) for i in range(total) if 0 <= i + steps[i % 4] < total]
        return lax.ppermute(value, ("group", "member"), pairs)

    kept, beside, across, slanted = prepare(patches, offsets)
    across_in = send(across, (2, 2, -2, -2))
    border_in = send(kept, (-4, -4, 4, 4))
    border_beside_in = send(beside, (-3, -5, 5, 3))
    beside_in = send(beside, (1, -1, 1, -1))
    slanted_in = send(slanted, (3, 1, -1, -3))
    state, held = run_stage(0, [jnp.asarray(t) for t in tables()], (), [kept, border_in], (node_links, offsets))
    *consts, counts, own_offsets = held
    state, _ = run_stage(1, consts, state, [across_in])
    state, _ = run_stage(2, consts, state, [border_beside_in, beside_in])
    state, _ = run_stage(3, consts, state, [slanted_in])
    found = state[3]

    near = send(found, (4, 4, -4, -4))
    rest = jnp.zeros((2, 128 - 2 * FOUND), jnp.float32)
    found = jnp.concatenate([found[:, :FOUND], near[:, :FOUND], rest], axis=1)
    every = lax.all_to_all(jnp.broadcast_to(found[None], (4 * tiles, 2, 128)), ("member", "tile"), 0, 0)
    return finish(every, counts, own_offsets, 4 * groups)


def solution(mesh):
    sections, tiles = mesh.devices.shape
    mesh = jax.sharding.Mesh(mesh.devices.reshape(sections // 4, 4, tiles), ("group", "member", "tile"))
    gz = ("group", "member")
    return jax.shard_map(
        shards,
        mesh=mesh,
        in_specs=(P(gz, "tile", None, None), P(None, None, gz, "tile"), P(None, gz, "tile")),
        out_specs=(P(None, None, gz, "tile"), P(None, gz, "tile")),
        check_vma=False,
    )
```

```python
import functools
import math

import jax
import jax.numpy as jnp
import ml_dtypes
import numpy as np
from jax import lax
from jax.experimental import pallas as pl
from jax.experimental.pallas import tpu as pltpu
from jax.sharding import PartitionSpec as P

NODE_COLS = 4
SIDE = 256
HALF = SIDE // 2
ROWS = 144
REACH = 4
SPAN = 16
GROUP = 4
NODES = 2
EXTRA = 16
BLOCK = NODES * SIDE + EXTRA
HALVES = 2 * NODES * SIDE + EXTRA
WINDOW = 6

STAGES = (
    ((), ()),
    ((((0, 2), (2, 4)),), (((1, 3), (3, 5)),)),
    ((((0, 1), (4, 5)), ((1, 2),)), (((0, 1), (4, 5)), ((3, 4),))),
    ((((2, 3), (3, 4)), ((1, 3), (3, 5))), (((2, 3), (1, 2)), ((0, 2), (2, 4)))),
)
GROUPS = 5
FOUND = GROUP * GROUPS


def pair_places(side):
    places, group = {}, 0
    for stage in STAGES:
        for pairs in stage[side]:
            for number, pair in enumerate(pairs):
                places.setdefault(pair, (group, number))
            group += 1
    return places


def stage_codes(number, side):
    codes = []
    for groups in zip(*STAGES[number]):
        both = [
            sum((a | b << 3 | (b - a - 1) << 6) << 8 * k for k, (a, b) in enumerate(pairs)) for pairs in groups
        ]
        codes.append(jnp.where(side == 0, jnp.int32(both[0]), jnp.int32(both[1])))
    return codes


def tables():
    index = np.arange(SIDE)

    def angle(phases):
        return (phases % SIDE).astype(np.float32) * np.float32(2.0 * math.pi / SIDE)

    phases = np.outer(index, index)
    cos_table = np.cos(angle(phases)).astype(ml_dtypes.bfloat16)
    sin_table = np.sin(angle(phases)).astype(ml_dtypes.bfloat16)
    right = np.concatenate([cos_table[: HALF + 1], sin_table[1:HALF]], axis=0)
    left = np.ascontiguousarray(right.T)
    row_freq = np.concatenate([np.arange(HALF + 1), -np.arange(1, HALF)])
    window = np.arange(-REACH, REACH + 1)
    fold_phase = 2.0 * math.pi * (np.outer(row_freq, window) % SIDE) / SIDE
    fold_cos, fold_sin = np.cos(fold_phase), np.sin(fold_phase)
    fold = np.zeros((2, 2, SIDE, 2, 2, 2, SPAN), np.float32)
    for odd in range(2):
        for part, out, value in ((0, 0, fold_cos), (1, 0, -fold_sin), (0, 1, fold_sin), (1, 1, fold_cos)):
            high = value.astype(np.float32).astype(ml_dtypes.bfloat16).astype(np.float32)
            fold[odd, part, :, odd, out, 0, : window.size] = high
            fold[odd, part, :, odd, out, 1, : window.size] = value - high
    fold = fold.reshape(2, 2 * SIDE, 128).astype(ml_dtypes.bfloat16)
    col_freq = np.arange(HALF + 1)
    twice = np.where((col_freq == 0) | (col_freq == HALF), 1.0, 2.0)[None, :] / SIDE
    col_phase = 2.0 * math.pi * (np.outer(window, col_freq) % SIDE) / SIDE
    close = np.zeros((2, SPAN, ROWS), np.float32)
    close[0, : window.size, : HALF + 1] = twice * np.cos(col_phase)
    close[1, : window.size, : HALF + 1] = twice * np.sin(col_phase)
    close = close.reshape(2 * SPAN, ROWS)
    high = close.astype(ml_dtypes.bfloat16)
    low = (close - high.astype(np.float32)).astype(ml_dtypes.bfloat16)
    lane, wide = np.arange(128)[:, None], np.arange(256)[None, :]
    spread = ((lane // 64 == wide // 128) & (lane % 64 < SPAN)).astype(ml_dtypes.bfloat16)
    return right, left, fold, np.concatenate([high, low], axis=0), spread


def transform(patch, right, left):
    half_product = lax.dot_general(
        right, patch, (((1,), (1,)), ((), ())), preferred_element_type=jnp.float32
    ).astype(jnp.bfloat16)
    full = jnp.dot(half_product, left, preferred_element_type=jnp.float32)
    lane = lax.broadcasted_iota(jnp.int32, (HALF, HALF), 1)
    row = lax.broadcasted_iota(jnp.int32, (HALF, HALF), 0)
    first_lane, first_row = lane == 0, row == 0
    cc, sc = full[:HALF, :HALF], full[:HALF, HALF:]
    last_c, last_s = full[HALF:, :HALF], full[HALF:, HALF:]
    cs, ss = jnp.where(first_row, 0.0, last_c), jnp.where(first_row, 0.0, last_s)

    def parts(cc, sc, cs, ss, edge):
        low_sc, low_ss = jnp.where(edge, 0.0, sc), jnp.where(edge, 0.0, ss)
        return jnp.concatenate(
            [
                cc - low_ss,
                jnp.where(edge, sc, cc + ss),
                -(cs + low_sc),
                jnp.where(edge, -ss, sc - cs),
            ],
            axis=1,
        ).astype(jnp.bfloat16)

    def with_size(spectrum):
        real, imag = spectrum[:, :SIDE].astype(jnp.float32), spectrum[:, SIDE:].astype(jnp.float32)
        square = real * real + imag * imag
        return spectrum, square * lax.rsqrt(jnp.maximum(square, 1e-30))

    tail = ROWS - HALF
    keep = row[:tail] == 0
    end_c, end_s = jnp.where(keep, last_c[:tail], 0.0), jnp.where(keep, last_s[:tail], 0.0)
    none = jnp.zeros_like(end_c)
    main = with_size(parts(cc, sc, cs, ss, first_lane))
    return main, with_size(parts(end_c, end_s, none, none, first_lane[:tail]))


def stage_kernel(number, consts, blocks, state, scratch):
    right, left, fold, close, spread = consts
    specs, sizes, offs, found = state
    power, folded = scratch
    device = lax.axis_index("member")
    row, side = device // 2, lax.rem(device, 2)
    codes = stage_codes(number, side)
    first_group = sum(len(stage[0]) for stage in STAGES[:number])
    near, far = 4 * row, 4 * (1 - row)
    places = ((near + side, far + side), (2 + side,), (far + 1 - side, near + 1 - side), (3 - side,))[number]
    chunk = 16

    if number == 0:
        found[...] = jnp.zeros_like(found)
    right_table, left_table = right[...], left[...]
    for block, place in zip(blocks, places):
        offs[place] = block[block.shape[0] - EXTRA :, :128]
        for n in range(NODES):
            patch = block[n * SIDE : (n + 1) * SIDE, :]
            if block.shape[1] < SIDE:
                patch = jnp.concatenate([patch, block[(NODES + n) * SIDE : (NODES + n + 1) * SIDE, :]], axis=1)
            main, end = transform(patch, right_table, left_table)
            specs[place * NODES + n, :HALF, :], sizes[place * NODES + n, :HALF, :] = main
            specs[place * NODES + n, HALF:, :], sizes[place * NODES + n, HALF:, :] = end

    for k, code in enumerate(codes):
        held = NODES * len(STAGES[number][0][k])
        for j in range(held):
            bits = jnp.right_shift(code, 8 * (j // NODES))
            a_at = (bits & 7) * NODES + j % NODES
            b_at = (jnp.right_shift(bits, 3) & 7) * NODES + j % NODES
            total = jnp.zeros((8, SIDE), jnp.float32)
            for start in range(0, ROWS, chunk):
                rows = slice(start, start + chunk)
                size = sizes[a_at, rows, :] * sizes[b_at, rows, :]
                if start == 0:
                    edge = lax.broadcasted_iota(jnp.int32, (chunk, SIDE), 0) == 0
                    size = jnp.where(edge, 0.5 * size, size)
                elif start == HALF:
                    size = 0.5 * size
                total = total + size[:8] + size[8:]
            floor = jnp.sum(total) * (2.0 / (SIDE * SIDE)) + 1e-6
            for start in range(0, ROWS, chunk):
                rows = slice(start, start + chunk)
                scale = pl.reciprocal(sizes[a_at, rows, :] * sizes[b_at, rows, :] + floor, approx=True)
                a = specs[a_at, rows, :].astype(jnp.float32)
                b = specs[b_at, rows, :].astype(jnp.float32)
                ar, ai, br, bi = a[:, :SIDE], a[:, SIDE:], b[:, :SIDE], b[:, SIDE:]
                br, bi = br * scale, bi * scale
                to = slice(ROWS * (j // 2) + start, ROWS * (j // 2) + start + chunk)
                power[k, j % 2, to, :SIDE] = (ar * br + ai * bi).astype(jnp.bfloat16)
                power[k, j % 2, to, SIDE:] = (ai * br - ar * bi).astype(jnp.bfloat16)
        used = ROWS * held // 2
        both = sum(
            jnp.dot(power[k, odd, :used, :], fold[odd], preferred_element_type=jnp.float32) for odd in range(2)
        )
        folded[:, 256 * k : 256 * k + 128] = both[:ROWS]
        folded[:, 256 * k + 128 : 256 * (k + 1)] = both[ROWS:] if held > 2 else jnp.zeros_like(both)
    if not codes:
        return

    sums = folded[...]
    high = sums.astype(jnp.bfloat16)
    low = (sums - high.astype(jnp.float32)).astype(jnp.bfloat16)
    closed = jnp.dot(close[...], high, preferred_element_type=jnp.float32)
    rest = jnp.dot(close[: 2 * SPAN], low, preferred_element_type=jnp.float32)
    closed = closed[: 2 * SPAN] + closed[2 * SPAN :] + rest
    lane = lax.broadcasted_iota(jnp.int32, (SPAN, 128), 1)
    step_u = ((lane & (SPAN - 1)) - REACH).astype(jnp.float32)
    step_v = (lax.broadcasted_iota(jnp.int32, (SPAN, 128), 0) - REACH).astype(jnp.float32)
    all_offs, pieces = [], []
    for k, code in enumerate(codes):
        for pair in range(2):
            bits = jnp.right_shift(code, 8 * pair)
            own = offs[bits & 7].astype(jnp.float32)[:8]
            own = jnp.where((jnp.right_shift(bits, 6) & 1) == 0, own[:4], own[4:])
            off_y = jnp.where(lane[:1] < 64, own[0:1], own[1:2])
            off_x = jnp.where(lane[:1] < 64, own[2:3], own[3:4])
            all_offs.append(own)
            at = slice(256 * k + 128 * pair, 256 * k + 128 * (pair + 1))
            by_cos, by_sin = closed[:SPAN, at], closed[SPAN:, at]
            by_cos = by_cos + pltpu.roll(by_cos, 128 - SPAN, axis=1)
            by_sin = pltpu.roll(by_sin, 128 - 2 * SPAN, axis=1) + pltpu.roll(by_sin, 128 - 3 * SPAN, axis=1)
            correlation = by_cos - by_sin
            from_y, from_x = step_u - off_y, step_v - off_x
            inside = (jnp.abs(from_y) < 1.5) & (jnp.abs(from_x) < 1.5)
            weight = jnp.where(inside, jnp.exp(3.0 * jnp.tanh(correlation)), 0.0)
            sums = jnp.concatenate(
                [
                    jnp.sum(weight, axis=0, keepdims=True),
                    jnp.sum(weight * from_y, axis=0, keepdims=True),
                    jnp.sum(weight * from_x, axis=0, keepdims=True),
                    jnp.zeros((5, 128), jnp.float32),
                ],
                axis=0,
            )
            for _ in range(3):
                pieces.append(sums.astype(jnp.bfloat16))
                sums = sums - pieces[-1].astype(jnp.float32)
    whole = jnp.dot(jnp.concatenate(pieces, axis=0), spread[...], preferred_element_type=jnp.float32)
    result = found[...]
    for pair, own in enumerate(all_offs):
        parts = [whole[24 * pair + 8 * piece : 24 * pair + 8 * (piece + 1)] for piece in range(3)]
        total = parts[0] + parts[1] + parts[2]
        ratio_y, ratio_x = total[1:2] / total[0:1], total[2:3] / total[0:1]
        for n in range(NODES):
            at = slice(128 * n, 128 * (n + 1))
            both = jnp.concatenate(
                [own[n : n + 1] + ratio_y[:, at], own[NODES + n : NODES + n + 1] + ratio_x[:, at]], axis=0
            )
            result = jnp.where(lane[:2] == GROUP * first_group + NODES * pair + n, both, result)
    found[...] = result


def run_stage(number, consts, state, blocks, mesh_inputs=()):
    vmem, hbm = pl.BlockSpec(memory_space=pltpu.VMEM), pl.BlockSpec(memory_space=pltpu.HBM)
    shapes = (
        ((WINDOW * NODES, ROWS, 2 * SIDE), jnp.bfloat16),
        ((WINDOW * NODES, ROWS, SIDE), jnp.float32),
        ((WINDOW, EXTRA, 128), jnp.bfloat16),
        ((2, 128), jnp.float32),
    )
    first = number == 0
    if first:
        consts = [pltpu.with_memory_space_constraint(c, pltpu.HBM) for c in consts]
        shapes += tuple((c.shape, c.dtype) for c in consts)
        shapes += (((4 * NODE_COLS, 128), jnp.float32), ((8, 128), jnp.float32))
        mesh_inputs = [pltpu.with_memory_space_constraint(x, pltpu.HBM) for x in mesh_inputs]
    count = len(consts)
    args = [*consts, *blocks, *state, *mesh_inputs]
    fixed = count + len(blocks)

    def kernel(*refs):
        outs, scratch = refs[len(args) : len(args) + len(shapes)], refs[len(args) + len(shapes) :]
        tables_in, blocks_in = refs[:count], refs[count:fixed]
        if first:
            held, sems = outs[4 : 4 + count], scratch[-1]
            sources = [*tables_in, *refs[fixed : len(args)]]
            targets = [*held, *scratch[2:4]]
            copies = [pltpu.make_async_copy(a, b, sems.at[k]) for k, (a, b) in enumerate(zip(sources, targets))]
            for copy in copies:
                copy.start()
            for copy in copies[:2]:
                copy.wait()
            tables_in = held
        stage_kernel(number, tables_in, blocks_in, outs[:4], scratch[:2])
        if first:
            for copy in copies[2:]:
                copy.wait()
            mesh_rows(*scratch[2:4], *outs[4 + count :], scratch[4])

    groups = max(len(STAGES[number][0]), 1)
    out = pl.pallas_call(
        kernel,
        out_shape=tuple(pltpu.VMEM(shape, dtype) for shape, dtype in shapes),
        in_specs=[hbm if first else vmem] * count
        + [vmem] * (len(args) - count - len(mesh_inputs))
        + [hbm] * len(mesh_inputs),
        out_specs=(vmem,) * len(shapes),
        input_output_aliases={fixed + k: k for k in range(len(state))},
        scratch_shapes=[
            pltpu.VMEM((groups, 2, 2 * ROWS, 2 * SIDE), jnp.bfloat16),
            pltpu.VMEM((ROWS, 256 * groups), jnp.float32),
        ]
        + [pltpu.VMEM(x.shape, x.dtype) for x in mesh_inputs]
        + ([pltpu.VMEM((8, 128), jnp.int32), pltpu.SemaphoreType.DMA((count + 2,))] if first else []),
        compiler_params=pltpu.CompilerParams(vmem_limit_bytes=24 * 1024 * 1024),
        cost_estimate=pl.CostEstimate(flops=1, bytes_accessed=1, transcendentals=0),
        name=f"stage{number}",
    )(*args)
    return tuple(out[:4]), tuple(out[4:])


def mesh_rows(node_links, node_offsets, counts, offsets, links):
    own = slice(NODE_COLS, 3 * NODE_COLS)
    links[...] = jnp.full_like(links, -1)
    offsets[...] = jnp.zeros_like(offsets)
    first = (lax.axis_index("tile") * 2 - 1) * NODE_COLS
    for k in range(4):
        links[k : k + 1, own] = node_links[k] - first
        offsets[k : k + 1, own] = node_offsets[k // 2, k % 2].astype(jnp.float32)
    for e in range(4 * NODE_COLS):
        counts[e : e + 1, :] = jnp.sum(jnp.where(links[0:4, :] == e, 1.0, 0.0), axis=0, keepdims=True)


def prepare_kernel(patches, all_offsets, *refs):
    blocks, offsets, sems = refs[:4], refs[4], refs[5]
    device = lax.axis_index("member")
    row, side = device // 2, lax.rem(device, 2)
    numbers = [2 * r + s for r in (row, 1 - row) for s in (side, 1 - side)]
    copies = []
    for k in (2, 3, 0, 1):
        block, width = blocks[k], blocks[k].shape[1]
        for half in range(SIDE // width):
            source = patches.at[numbers[k], :, pl.ds(half * width, width)]
            target = block.at[pl.ds(half * NODES * SIDE, NODES * SIDE)]
            copies.append(pltpu.make_async_copy(source, target, sems.at[len(copies)]))
            copies[-1].start()
    offsets_copy = pltpu.make_async_copy(all_offsets, offsets, sems.at[6])
    offsets_copy.start()
    offsets_copy.wait()
    line = lax.broadcasted_iota(jnp.int32, (EXTRA, 128), 0)
    for block, number in zip(blocks, numbers):
        rows = jnp.zeros((EXTRA, 128), jnp.float32)
        for partner in range(2):
            for part in range(2):
                for n in range(NODES):
                    value = offsets[partner, part, 0, NODES * number + n].astype(jnp.float32)
                    rows = jnp.where(line == 4 * partner + 2 * part + n, value, rows)
        for start in range(0, block.shape[1], 128):
            block[block.shape[0] - EXTRA :, start : start + 128] = rows.astype(jnp.bfloat16)
    for copy in copies:
        copy.wait()


def prepare(patches, offsets):
    return pl.pallas_call(
        prepare_kernel,
        out_shape=tuple(pltpu.VMEM(shape, jnp.bfloat16) for shape in ((HALVES, 128),) * 2 + ((BLOCK, SIDE),) * 2),
        in_specs=[pl.BlockSpec(memory_space=pltpu.HBM)] * 2,
        out_specs=(pl.BlockSpec(memory_space=pltpu.VMEM),) * 4,
        scratch_shapes=[pltpu.SMEM((2, 2, 1, 2 * GROUP), jnp.int32), pltpu.SemaphoreType.DMA((7,))],
        cost_estimate=pl.CostEstimate(flops=1, bytes_accessed=1, transcendentals=0),
        name="prepare",
    )(
        pltpu.with_memory_space_constraint(patches.reshape(4, NODES * SIDE, SIDE), pltpu.HBM),
        pltpu.with_memory_space_constraint(offsets, pltpu.HBM),
    )


def finish_kernel(total, every, counts, offsets, shifts_out, moved_out, shifts, moved, sems):
    device, tile = lax.axis_index("member"), lax.axis_index("tile")
    position = 4 * lax.axis_index("group") + device
    lane = lax.broadcasted_iota(jnp.int32, (2, 128), 1)
    own = slice(NODE_COLS, 3 * NODE_COLS)
    tiles = lax.axis_size("tile")
    places = [pair_places(side) for side in range(2)]
    spread = {}
    near_tiles = {0: tile, -1: jnp.maximum(tile - 1, 0), 1: jnp.minimum(tile + 1, tiles - 1)}

    def shifts_of(member, step, column):
        if (member, step, column) not in spread:
            values = every[member * tiles + near_tiles[step]][:, column : column + 1]
            spread[member, step, column] = jnp.broadcast_to(values, (2, 128))
        return spread[member, step, column]

    def put(held, start, row, section, partner, step, source=0):
        first = section + 2 * row
        for side in range(2):
            group, number = places[side][(first, first + partner)]
            for n in range(NODES):
                value = shifts_of(2 * row + side, step, FOUND * source + GROUP * group + NODES * number + n)
                held = jnp.where(lane == start + 2 * side + n, value, held)
        return held

    def put_next(held, start, row, section, step):
        if row == 0 and section < 0:
            return put(held, start, 0, section + 4, 1, step, 1)
        if row == 1 and section > 2:
            return put(held, start, 1, section - 4, 1, step, 1)
        return put(held, start, row, section, 1, step)

    blank = jnp.zeros((2, 128), jnp.float32)
    next_all, second_all = [], []
    for section in range(-2, 5):
        held = put_next(blank, NODE_COLS, 0, section, 0)
        held = put_next(held, 2 * NODE_COLS, 1, section, 0)
        if -1 <= section < 4:
            held = put_next(held, 0, 1, section, -1)
            held = put_next(held, 3 * NODE_COLS, 0, section, 1)
        next_all.append(held)
    for section in range(4):
        held = put(blank, NODE_COLS, 0, section, 2, 0)
        if section < 2:
            held = put(held, 2 * NODE_COLS, 1, section, 2, 0)
        else:
            held = put(held, 2 * NODE_COLS, 1, section - 4, 2, 0, 1)
        second_all.append(held)

    def pick(values):
        chosen = values[3]
        for r in range(3):
            chosen = jnp.where(device == r, values[r], chosen)
        return chosen

    behind2, behind, here, ahead = (pick(next_all[k : k + 4]) for k in range(4))
    found_next = jnp.where(position + 1 < total, here, offsets[0:2, :])
    found_second = jnp.where(position + 2 < total, pick(second_all), offsets[2:4, :])
    has_next = [
        jnp.where((position + d >= 0) & (position + d + 1 < total), 1.0, 0.0).astype(jnp.float32)
        for d in (-2, -1, 0, 1)
    ]
    pulls = [-h * f for h, f in zip(has_next, (behind2, behind, here, ahead))]
    behind_pos, positions, ahead_pos = (0.25 * (pulls[k + 1] - pulls[k]) for k in range(3))
    neighbours = blank
    for e in range(4 * NODE_COLS):
        neighbours = neighbours + counts[e : e + 1, :] * positions[:, e : e + 1]
    in_plane = 0.25 * (neighbours - 4.0 * positions)
    pull = has_next[2] * (ahead_pos - positions - here)
    pull_behind = has_next[1] * (positions - behind_pos - behind)
    positions = positions + 0.5 * (in_plane + 0.5 * (pull - pull_behind))
    for part in range(2):
        shifts[0, part] = found_next[part : part + 1, own]
        shifts[1, part] = found_second[part : part + 1, own]
        moved[part] = positions[part : part + 1, own]
    copies = [
        pltpu.make_async_copy(shifts, shifts_out, sems.at[0]),
        pltpu.make_async_copy(moved, moved_out, sems.at[1]),
    ]
    for copy in copies:
        copy.start()
    for copy in copies:
        copy.wait()


def finish(every, counts, offsets, total):
    vmem, hbm = pl.BlockSpec(memory_space=pltpu.VMEM), pl.BlockSpec(memory_space=pltpu.HBM)
    nodes = 2 * NODE_COLS
    shapes = ((2, 2, 1, nodes), (2, 1, nodes))
    return pl.pallas_call(
        functools.partial(finish_kernel, total),
        out_shape=tuple(jax.ShapeDtypeStruct(shape, jnp.float32) for shape in shapes),
        in_specs=[vmem] * 3,
        out_specs=(hbm, hbm),
        scratch_shapes=[pltpu.VMEM(shape, jnp.float32) for shape in shapes] + [pltpu.SemaphoreType.DMA((2,))],
        cost_estimate=pl.CostEstimate(flops=1, bytes_accessed=1, transcendentals=0),
        name="finish",
    )(every, counts, offsets)


def shards(sections, offsets, node_links):
    patches = sections[0]
    groups, tiles = lax.axis_size("group"), lax.axis_size("tile")

    def send(value, steps):
        total = 4 * groups
        pairs = [(i, i + steps[i % 4]) for i in range(total) if 0 <= i + steps[i % 4] < total]
        return lax.ppermute(value, ("group", "member"), pairs)

    kept, beside, across, slanted = prepare(patches, offsets)
    across_in = send(across, (2, 2, -2, -2))
    border_in = send(kept, (-4, -4, 4, 4))
    border_beside_in = send(beside, (-3, -5, 5, 3))
    beside_in = send(beside, (1, -1, 1, -1))
    slanted_in = send(slanted, (3, 1, -1, -3))
    state, held = run_stage(0, [jnp.asarray(t) for t in tables()], (), [kept, border_in], (node_links, offsets))
    *consts, counts, own_offsets = held
    state, _ = run_stage(1, consts, state, [across_in])
    state, _ = run_stage(2, consts, state, [border_beside_in, beside_in])
    state, _ = run_stage(3, consts, state, [slanted_in])
    found = state[3]

    near = send(found, (4, 4, -4, -4))
    rest = jnp.zeros((2, 128 - 2 * FOUND), jnp.float32)
    found = jnp.concatenate([found[:, :FOUND], near[:, :FOUND], rest], axis=1)
    every = lax.all_to_all(jnp.broadcast_to(found[None], (4 * tiles, 2, 128)), ("member", "tile"), 0, 0)
    return finish(every, counts, own_offsets, 4 * groups)


def solution(mesh):
    sections, tiles = mesh.devices.shape
    mesh = jax.sharding.Mesh(mesh.devices.reshape(sections // 4, 4, tiles), ("group", "member", "tile"))
    gz = ("group", "member")
    return jax.shard_map(
        shards,
        mesh=mesh,
        in_specs=(P(gz, "tile", None, None), P(None, None, gz, "tile"), P(None, gz, "tile")),
        out_specs=(P(None, None, gz, "tile"), P(None, gz, "tile")),
        check_vma=False,
    )
```

```python
import functools
import math

import jax
import jax.numpy as jnp
import ml_dtypes
import numpy as np
from jax import lax
from jax.experimental import pallas as pl
from jax.experimental.pallas import tpu as pltpu
from jax.sharding import PartitionSpec as P

NODE_COLS = 4
SIDE = 256
HALF = SIDE // 2
ROWS = 144
REACH = 4
SPAN = 16
GROUP = 4
NODES = 2
EXTRA = 16
BLOCK = NODES * SIDE + EXTRA
HALVES = 2 * NODES * SIDE + EXTRA
WINDOW = 6

STAGES = (
    ((), ()),
    ((((0, 2), (2, 4)),), (((1, 3), (3, 5)),)),
    ((((0, 1), (4, 5)), ((1, 2),)), (((0, 1), (4, 5)), ((3, 4),))),
    ((((2, 3), (3, 4)), ((1, 3), (3, 5))), (((2, 3), (1, 2)), ((0, 2), (2, 4)))),
)
GROUPS = 5
FOUND = GROUP * GROUPS


def pair_places(side):
    places, group = {}, 0
    for stage in STAGES:
        for pairs in stage[side]:
            for number, pair in enumerate(pairs):
                places.setdefault(pair, (group, number))
            group += 1
    return places


def stage_codes(number, side):
    codes = []
    for groups in zip(*STAGES[number]):
        both = [
            sum((a | b << 3 | (b - a - 1) << 6) << 8 * k for k, (a, b) in enumerate(pairs)) for pairs in groups
        ]
        codes.append(jnp.where(side == 0, jnp.int32(both[0]), jnp.int32(both[1])))
    return codes


def tables():
    index = np.arange(SIDE)

    def angle(phases):
        return (phases % SIDE).astype(np.float32) * np.float32(2.0 * math.pi / SIDE)

    phases = np.outer(index, index)
    cos_table = np.cos(angle(phases)).astype(ml_dtypes.bfloat16)
    sin_table = np.sin(angle(phases)).astype(ml_dtypes.bfloat16)
    right = np.concatenate([cos_table[: HALF + 1], sin_table[1:HALF]], axis=0)
    left = np.ascontiguousarray(right.T)
    row_freq = np.concatenate([np.arange(HALF + 1), -np.arange(1, HALF)])
    window = np.arange(-REACH, REACH + 1)
    fold_phase = 2.0 * math.pi * (np.outer(row_freq, window) % SIDE) / SIDE
    fold_cos, fold_sin = np.cos(fold_phase), np.sin(fold_phase)
    fold = np.zeros((2, 2, SIDE, 2, 2, 2, SPAN), np.float32)
    for odd in range(2):
        for part, out, value in ((0, 0, fold_cos), (1, 0, -fold_sin), (0, 1, fold_sin), (1, 1, fold_cos)):
            high = value.astype(np.float32).astype(ml_dtypes.bfloat16).astype(np.float32)
            fold[odd, part, :, odd, out, 0, : window.size] = high
            fold[odd, part, :, odd, out, 1, : window.size] = value - high
    fold = fold.reshape(2, 2 * SIDE, 128).astype(ml_dtypes.bfloat16)
    col_freq = np.arange(HALF + 1)
    twice = np.where((col_freq == 0) | (col_freq == HALF), 1.0, 2.0)[None, :] / SIDE
    col_phase = 2.0 * math.pi * (np.outer(window, col_freq) % SIDE) / SIDE
    close = np.zeros((2, SPAN, ROWS), np.float32)
    close[0, : window.size, : HALF + 1] = twice * np.cos(col_phase)
    close[1, : window.size, : HALF + 1] = twice * np.sin(col_phase)
    close = close.reshape(2 * SPAN, ROWS)
    high = close.astype(ml_dtypes.bfloat16)
    low = (close - high.astype(np.float32)).astype(ml_dtypes.bfloat16)
    lane, wide = np.arange(128)[:, None], np.arange(256)[None, :]
    spread = ((lane // 64 == wide // 128) & (lane % 64 < SPAN)).astype(ml_dtypes.bfloat16)
    return right, left, fold, np.concatenate([high, low], axis=0), spread


def transform(patch, right, left):
    half_product = lax.dot_general(
        right, patch, (((1,), (1,)), ((), ())), preferred_element_type=jnp.float32
    ).astype(jnp.bfloat16)
    full = jnp.dot(half_product, left, preferred_element_type=jnp.float32)
    lane = lax.broadcasted_iota(jnp.int32, (HALF, HALF), 1)
    row = lax.broadcasted_iota(jnp.int32, (HALF, HALF), 0)
    first_lane, first_row = lane == 0, row == 0
    cc, sc = full[:HALF, :HALF], full[:HALF, HALF:]
    last_c, last_s = full[HALF:, :HALF], full[HALF:, HALF:]
    cs, ss = jnp.where(first_row, 0.0, last_c), jnp.where(first_row, 0.0, last_s)

    def parts(cc, sc, cs, ss, edge):
        low_sc, low_ss = jnp.where(edge, 0.0, sc), jnp.where(edge, 0.0, ss)
        return jnp.concatenate(
            [
                cc - low_ss,
                jnp.where(edge, sc, cc + ss),
                -(cs + low_sc),
                jnp.where(edge, -ss, sc - cs),
            ],
            axis=1,
        ).astype(jnp.bfloat16)

    def with_size(spectrum):
        real, imag = spectrum[:, :SIDE].astype(jnp.float32), spectrum[:, SIDE:].astype(jnp.float32)
        square = real * real + imag * imag
        return spectrum, square * lax.rsqrt(jnp.maximum(square, 1e-30))

    tail = ROWS - HALF
    keep = row[:tail] == 0
    end_c, end_s = jnp.where(keep, last_c[:tail], 0.0), jnp.where(keep, last_s[:tail], 0.0)
    none = jnp.zeros_like(end_c)
    main = with_size(parts(cc, sc, cs, ss, first_lane))
    return main, with_size(parts(end_c, end_s, none, none, first_lane[:tail]))


def stage_kernel(number, consts, blocks, state, scratch):
    right, left, fold, close, spread = consts
    specs, sizes, offs, found = state
    power, folded = scratch
    device = lax.axis_index("member")
    row, side = device // 2, lax.rem(device, 2)
    codes = stage_codes(number, side)
    first_group = sum(len(stage[0]) for stage in STAGES[:number])
    near, far = 4 * row, 4 * (1 - row)
    places = ((near + side, far + side), (2 + side,), (far + 1 - side, near + 1 - side), (3 - side,))[number]
    chunk = 16

    if number == 0:
        found[...] = jnp.zeros_like(found)
    right_table, left_table = right[...], left[...]
    for block, place in zip(blocks, places):
        offs[place] = block[block.shape[0] - EXTRA :, :128]
        for n in range(NODES):
            patch = block[n * SIDE : (n + 1) * SIDE, :]
            if block.shape[1] < SIDE:
                patch = jnp.concatenate([patch, block[(NODES + n) * SIDE : (NODES + n + 1) * SIDE, :]], axis=1)
            main, end = transform(patch, right_table, left_table)
            specs[place * NODES + n, :HALF, :], sizes[place * NODES + n, :HALF, :] = main
            specs[place * NODES + n, HALF:, :], sizes[place * NODES + n, HALF:, :] = end

    for k, code in enumerate(codes):
        held = NODES * len(STAGES[number][0][k])
        for j in range(held):
            bits = jnp.right_shift(code, 8 * (j // NODES))
            a_at = (bits & 7) * NODES + j % NODES
            b_at = (jnp.right_shift(bits, 3) & 7) * NODES + j % NODES
            total = jnp.zeros((8, SIDE), jnp.float32)
            for start in range(0, ROWS, chunk):
                rows = slice(start, start + chunk)
                size = sizes[a_at, rows, :] * sizes[b_at, rows, :]
                if start == 0:
                    edge = lax.broadcasted_iota(jnp.int32, (chunk, SIDE), 0) == 0
                    size = jnp.where(edge, 0.5 * size, size)
                elif start == HALF:
                    size = 0.5 * size
                total = total + size[:8] + size[8:]
            floor = jnp.sum(total) * (2.0 / (SIDE * SIDE)) + 1e-6
            for start in range(0, ROWS, chunk):
                rows = slice(start, start + chunk)
                scale = pl.reciprocal(sizes[a_at, rows, :] * sizes[b_at, rows, :] + floor, approx=True)
                a = specs[a_at, rows, :].astype(jnp.float32)
                b = specs[b_at, rows, :].astype(jnp.float32)
                ar, ai, br, bi = a[:, :SIDE], a[:, SIDE:], b[:, :SIDE], b[:, SIDE:]
                br, bi = br * scale, bi * scale
                to = slice(ROWS * (j // 2) + start, ROWS * (j // 2) + start + chunk)
                power[k, j % 2, to, :SIDE] = (ar * br + ai * bi).astype(jnp.bfloat16)
                power[k, j % 2, to, SIDE:] = (ai * br - ar * bi).astype(jnp.bfloat16)
        used = ROWS * held // 2
        both = sum(
            jnp.dot(power[k, odd, :used, :], fold[odd], preferred_element_type=jnp.float32) for odd in range(2)
        )
        folded[:, 256 * k : 256 * k + 128] = both[:ROWS]
        folded[:, 256 * k + 128 : 256 * (k + 1)] = both[ROWS:] if held > 2 else jnp.zeros_like(both)
    if not codes:
        return

    sums = folded[...]
    high = sums.astype(jnp.bfloat16)
    low = (sums - high.astype(jnp.float32)).astype(jnp.bfloat16)
    closed = jnp.dot(close[...], high, preferred_element_type=jnp.float32)
    rest = jnp.dot(close[: 2 * SPAN], low, preferred_element_type=jnp.float32)
    closed = closed[: 2 * SPAN] + closed[2 * SPAN :] + rest
    lane = lax.broadcasted_iota(jnp.int32, (SPAN, 128), 1)
    step_u = ((lane & (SPAN - 1)) - REACH).astype(jnp.float32)
    step_v = (lax.broadcasted_iota(jnp.int32, (SPAN, 128), 0) - REACH).astype(jnp.float32)
    all_offs, pieces = [], []
    for k, code in enumerate(codes):
        for pair in range(2):
            bits = jnp.right_shift(code, 8 * pair)
            own = offs[bits & 7].astype(jnp.float32)[:8]
            own = jnp.where((jnp.right_shift(bits, 6) & 1) == 0, own[:4], own[4:])
            off_y = jnp.where(lane[:1] < 64, own[0:1], own[1:2])
            off_x = jnp.where(lane[:1] < 64, own[2:3], own[3:4])
            all_offs.append(own)
            at = slice(256 * k + 128 * pair, 256 * k + 128 * (pair + 1))
            by_cos, by_sin = closed[:SPAN, at], closed[SPAN:, at]
            by_cos = by_cos + pltpu.roll(by_cos, 128 - SPAN, axis=1)
            by_sin = pltpu.roll(by_sin, 128 - 2 * SPAN, axis=1) + pltpu.roll(by_sin, 128 - 3 * SPAN, axis=1)
            correlation = by_cos - by_sin
            from_y, from_x = step_u - off_y, step_v - off_x
            inside = (jnp.abs(from_y) < 1.5) & (jnp.abs(from_x) < 1.5)
            weight = jnp.where(inside, jnp.exp(3.0 * jnp.tanh(correlation)), 0.0)
            sums = jnp.concatenate(
                [
                    jnp.sum(weight, axis=0, keepdims=True),
                    jnp.sum(weight * from_y, axis=0, keepdims=True),
                    jnp.sum(weight * from_x, axis=0, keepdims=True),
                    jnp.zeros((5, 128), jnp.float32),
                ],
                axis=0,
            )
            for _ in range(3):
                pieces.append(sums.astype(jnp.bfloat16))
                sums = sums - pieces[-1].astype(jnp.float32)
    whole = jnp.dot(jnp.concatenate(pieces, axis=0), spread[...], preferred_element_type=jnp.float32)
    result = found[...]
    for pair, own in enumerate(all_offs):
        parts = [whole[24 * pair + 8 * piece : 24 * pair + 8 * (piece + 1)] for piece in range(3)]
        total = parts[0] + parts[1] + parts[2]
        ratio_y, ratio_x = total[1:2] / total[0:1], total[2:3] / total[0:1]
        for n in range(NODES):
            at = slice(128 * n, 128 * (n + 1))
            both = jnp.concatenate(
                [own[n : n + 1] + ratio_y[:, at], own[NODES + n : NODES + n + 1] + ratio_x[:, at]], axis=0
            )
            result = jnp.where(lane[:2] == GROUP * first_group + NODES * pair + n, both, result)
    found[...] = result


def run_stage(number, consts, state, blocks, mesh_inputs=()):
    vmem, hbm = pl.BlockSpec(memory_space=pltpu.VMEM), pl.BlockSpec(memory_space=pltpu.HBM)
    shapes = (
        ((WINDOW * NODES, ROWS, 2 * SIDE), jnp.bfloat16),
        ((WINDOW * NODES, ROWS, SIDE), jnp.float32),
        ((WINDOW, EXTRA, 128), jnp.bfloat16),
        ((2, 128), jnp.float32),
    )
    first = number == 0
    if first:
        consts = [pltpu.with_memory_space_constraint(c, pltpu.HBM) for c in consts]
        shapes += tuple((c.shape, c.dtype) for c in consts)
        shapes += (((4 * NODE_COLS, 128), jnp.float32), ((8, 128), jnp.float32))
        mesh_inputs = [pltpu.with_memory_space_constraint(x, pltpu.HBM) for x in mesh_inputs]
    count = len(consts)
    args = [*consts, *blocks, *state, *mesh_inputs]
    fixed = count + len(blocks)

    def kernel(*refs):
        outs, scratch = refs[len(args) : len(args) + len(shapes)], refs[len(args) + len(shapes) :]
        tables_in, blocks_in = refs[:count], refs[count:fixed]
        if first:
            held, sems = outs[4 : 4 + count], scratch[-1]
            sources = [*tables_in, *refs[fixed : len(args)]]
            targets = [*held, *scratch[2:4]]
            copies = [pltpu.make_async_copy(a, b, sems.at[k]) for k, (a, b) in enumerate(zip(sources, targets))]
            for copy in copies:
                copy.start()
            for copy in copies[:2]:
                copy.wait()
            tables_in = held
        stage_kernel(number, tables_in, blocks_in, outs[:4], scratch[:2])
        if first:
            for copy in copies[2:]:
                copy.wait()
            mesh_rows(*scratch[2:4], *outs[4 + count :], scratch[4])

    groups = max(len(STAGES[number][0]), 1)
    out = pl.pallas_call(
        kernel,
        out_shape=tuple(pltpu.VMEM(shape, dtype) for shape, dtype in shapes),
        in_specs=[hbm if first else vmem] * count
        + [vmem] * (len(args) - count - len(mesh_inputs))
        + [hbm] * len(mesh_inputs),
        out_specs=(vmem,) * len(shapes),
        input_output_aliases={fixed + k: k for k in range(len(state))},
        scratch_shapes=[
            pltpu.VMEM((groups, 2, 2 * ROWS, 2 * SIDE), jnp.bfloat16),
            pltpu.VMEM((ROWS, 256 * groups), jnp.float32),
        ]
        + [pltpu.VMEM(x.shape, x.dtype) for x in mesh_inputs]
        + ([pltpu.VMEM((8, 128), jnp.int32), pltpu.SemaphoreType.DMA((count + 2,))] if first else []),
        compiler_params=pltpu.CompilerParams(vmem_limit_bytes=24 * 1024 * 1024),
        cost_estimate=pl.CostEstimate(flops=1, bytes_accessed=1, transcendentals=0),
        name=f"stage{number}",
    )(*args)
    return tuple(out[:4]), tuple(out[4:])


def mesh_rows(node_links, node_offsets, counts, offsets, links):
    own = slice(NODE_COLS, 3 * NODE_COLS)
    links[...] = jnp.full_like(links, -1)
    offsets[...] = jnp.zeros_like(offsets)
    first = (lax.axis_index("tile") * 2 - 1) * NODE_COLS
    for k in range(4):
        links[k : k + 1, own] = node_links[k] - first
        offsets[k : k + 1, own] = node_offsets[k // 2, k % 2].astype(jnp.float32)
    for e in range(4 * NODE_COLS):
        counts[e : e + 1, :] = jnp.sum(jnp.where(links[0:4, :] == e, 1.0, 0.0), axis=0, keepdims=True)


def prepare_kernel(patches, all_offsets, *refs):
    blocks, offsets, sems = refs[:4], refs[4], refs[5]
    device = lax.axis_index("member")
    row, side = device // 2, lax.rem(device, 2)
    numbers = [2 * r + s for r in (row, 1 - row) for s in (side, 1 - side)]
    copies = []
    for k in (2, 3, 0, 1):
        block, width = blocks[k], blocks[k].shape[1]
        for half in range(SIDE // width):
            source = patches.at[numbers[k], :, pl.ds(half * width, width)]
            target = block.at[pl.ds(half * NODES * SIDE, NODES * SIDE)]
            copies.append(pltpu.make_async_copy(source, target, sems.at[len(copies)]))
            copies[-1].start()
    offsets_copy = pltpu.make_async_copy(all_offsets, offsets, sems.at[6])
    offsets_copy.start()
    offsets_copy.wait()
    line = lax.broadcasted_iota(jnp.int32, (EXTRA, 128), 0)
    for block, number in zip(blocks, numbers):
        rows = jnp.zeros((EXTRA, 128), jnp.float32)
        for partner in range(2):
            for part in range(2):
                for n in range(NODES):
                    value = offsets[partner, part, 0, NODES * number + n].astype(jnp.float32)
                    rows = jnp.where(line == 4 * partner + 2 * part + n, value, rows)
        for start in range(0, block.shape[1], 128):
            block[block.shape[0] - EXTRA :, start : start + 128] = rows.astype(jnp.bfloat16)
    for copy in copies:
        copy.wait()


def prepare(patches, offsets):
    return pl.pallas_call(
        prepare_kernel,
        out_shape=tuple(pltpu.VMEM(shape, jnp.bfloat16) for shape in ((HALVES, 128),) * 2 + ((BLOCK, SIDE),) * 2),
        in_specs=[pl.BlockSpec(memory_space=pltpu.HBM)] * 2,
        out_specs=(pl.BlockSpec(memory_space=pltpu.VMEM),) * 4,
        scratch_shapes=[pltpu.SMEM((2, 2, 1, 2 * GROUP), jnp.int32), pltpu.SemaphoreType.DMA((7,))],
        cost_estimate=pl.CostEstimate(flops=1, bytes_accessed=1, transcendentals=0),
        name="prepare",
    )(
        pltpu.with_memory_space_constraint(patches.reshape(4, NODES * SIDE, SIDE), pltpu.HBM),
        pltpu.with_memory_space_constraint(offsets, pltpu.HBM),
    )


def finish_kernel(total, every, counts, offsets, shifts_out, moved_out, shifts, moved, sems):
    device, tile = lax.axis_index("member"), lax.axis_index("tile")
    position = 4 * lax.axis_index("group") + device
    lane = lax.broadcasted_iota(jnp.int32, (2, 128), 1)
    own = slice(NODE_COLS, 3 * NODE_COLS)
    tiles = lax.axis_size("tile")
    places = [pair_places(side) for side in range(2)]
    spread = {}
    near_tiles = {0: tile, -1: jnp.maximum(tile - 1, 0), 1: jnp.minimum(tile + 1, tiles - 1)}

    def shifts_of(member, step, column):
        if (member, step, column) not in spread:
            values = every[member * tiles + near_tiles[step]][:, column : column + 1]
            spread[member, step, column] = jnp.broadcast_to(values, (2, 128))
        return spread[member, step, column]

    def put(held, start, row, section, partner, step, source=0):
        first = section + 2 * row
        for side in range(2):
            group, number = places[side][(first, first + partner)]
            for n in range(NODES):
                value = shifts_of(2 * row + side, step, FOUND * source + GROUP * group + NODES * number + n)
                held = jnp.where(lane == start + 2 * side + n, value, held)
        return held

    def put_next(held, start, row, section, step):
        if row == 0 and section < 0:
            return put(held, start, 0, section + 4, 1, step, 1)
        if row == 1 and section > 2:
            return put(held, start, 1, section - 4, 1, step, 1)
        return put(held, start, row, section, 1, step)

    blank = jnp.zeros((2, 128), jnp.float32)
    next_all, second_all = [], []
    for section in range(-2, 5):
        held = put_next(blank, NODE_COLS, 0, section, 0)
        held = put_next(held, 2 * NODE_COLS, 1, section, 0)
        if -1 <= section < 4:
            held = put_next(held, 0, 1, section, -1)
            held = put_next(held, 3 * NODE_COLS, 0, section, 1)
        next_all.append(held)
    for section in range(4):
        held = put(blank, NODE_COLS, 0, section, 2, 0)
        if section < 2:
            held = put(held, 2 * NODE_COLS, 1, section, 2, 0)
        else:
            held = put(held, 2 * NODE_COLS, 1, section - 4, 2, 0, 1)
        second_all.append(held)

    def pick(values):
        chosen = values[3]
        for r in range(3):
            chosen = jnp.where(device == r, values[r], chosen)
        return chosen

    behind2, behind, here, ahead = (pick(next_all[k : k + 4]) for k in range(4))
    found_next = jnp.where(position + 1 < total, here, offsets[0:2, :])
    found_second = jnp.where(position + 2 < total, pick(second_all), offsets[2:4, :])
    has_next = [
        jnp.where((position + d >= 0) & (position + d + 1 < total), 1.0, 0.0).astype(jnp.float32)
        for d in (-2, -1, 0, 1)
    ]
    pulls = [-h * f for h, f in zip(has_next, (behind2, behind, here, ahead))]
    behind_pos, positions, ahead_pos = (0.25 * (pulls[k + 1] - pulls[k]) for k in range(3))
    neighbours = blank
    for e in range(4 * NODE_COLS):
        neighbours = neighbours + counts[e : e + 1, :] * positions[:, e : e + 1]
    in_plane = 0.25 * (neighbours - 4.0 * positions)
    pull = has_next[2] * (ahead_pos - positions - here)
    pull_behind = has_next[1] * (positions - behind_pos - behind)
    positions = positions + 0.5 * (in_plane + 0.5 * (pull - pull_behind))
    for part in range(2):
        shifts[0, part] = found_next[part : part + 1, own]
        shifts[1, part] = found_second[part : part + 1, own]
        moved[part] = positions[part : part + 1, own]
    copies = [
        pltpu.make_async_copy(shifts, shifts_out, sems.at[0]),
        pltpu.make_async_copy(moved, moved_out, sems.at[1]),
    ]
    for copy in copies:
        copy.start()
    for copy in copies:
        copy.wait()


def finish(every, counts, offsets, total):
    vmem, hbm = pl.BlockSpec(memory_space=pltpu.VMEM), pl.BlockSpec(memory_space=pltpu.HBM)
    nodes = 2 * NODE_COLS
    shapes = ((2, 2, 1, nodes), (2, 1, nodes))
    return pl.pallas_call(
        functools.partial(finish_kernel, total),
        out_shape=tuple(jax.ShapeDtypeStruct(shape, jnp.float32) for shape in shapes),
        in_specs=[vmem] * 3,
        out_specs=(hbm, hbm),
        scratch_shapes=[pltpu.VMEM(shape, jnp.float32) for shape in shapes] + [pltpu.SemaphoreType.DMA((2,))],
        cost_estimate=pl.CostEstimate(flops=1, bytes_accessed=1, transcendentals=0),
        name="finish",
    )(every, counts, offsets)


def shards(sections, offsets, node_links):
    patches = sections[0]
    groups, tiles = lax.axis_size("group"), lax.axis_size("tile")

    def send(value, steps):
        total = 4 * groups
        pairs = [(i, i + steps[i % 4]) for i in range(total) if 0 <= i + steps[i % 4] < total]
        return lax.ppermute(value, ("group", "member"), pairs)

    kept, beside, across, slanted = prepare(patches, offsets)
    across_in = send(across, (2, 2, -2, -2))
    border_in = send(kept, (-4, -4, 4, 4))
    border_beside_in = send(beside, (-3, -5, 5, 3))
    beside_in = send(beside, (1, -1, 1, -1))
    slanted_in = send(slanted, (3, 1, -1, -3))
    state, held = run_stage(0, [jnp.asarray(t) for t in tables()], (), [kept, border_in], (node_links, offsets))
    *consts, counts, own_offsets = held
    state, _ = run_stage(1, consts, state, [across_in])
    state, _ = run_stage(2, consts, state, [border_beside_in, beside_in])
    state, _ = run_stage(3, consts, state, [slanted_in])
    found = state[3]

    near = send(found, (4, 4, -4, -4))
    rest = jnp.zeros((2, 128 - 2 * FOUND), jnp.float32)
    found = jnp.concatenate([found[:, :FOUND], near[:, :FOUND], rest], axis=1)
    every = lax.all_to_all(jnp.broadcast_to(found[None], (4 * tiles, 2, 128)), ("member", "tile"), 0, 0)
    near_by = [pltpu.with_memory_space_constraint(x, pltpu.VMEM) for x in (every, counts, own_offsets)]
    return finish(*near_by, 4 * groups)


def solution(mesh):
    sections, tiles = mesh.devices.shape
    mesh = jax.sharding.Mesh(mesh.devices.reshape(sections // 4, 4, tiles), ("group", "member", "tile"))
    gz = ("group", "member")
    return jax.shard_map(
        shards,
        mesh=mesh,
        in_specs=(P(gz, "tile", None, None), P(None, None, gz, "tile"), P(None, gz, "tile")),
        out_specs=(P(None, None, gz, "tile"), P(None, gz, "tile")),
        check_vma=False,
    )
```

```python
import functools
import math

import jax
import jax.numpy as jnp
import ml_dtypes
import numpy as np
from jax import lax
from jax.experimental import pallas as pl
from jax.experimental.pallas import tpu as pltpu
from jax.sharding import PartitionSpec as P

NODE_COLS = 4
SIDE = 256
HALF = SIDE // 2
ROWS = 144
REACH = 4
SPAN = 16
GROUP = 4
NODES = 2
EXTRA = 16
BLOCK = NODES * SIDE + EXTRA
HALVES = 2 * NODES * SIDE + EXTRA
WINDOW = 6

STAGES = (
    ((), ()),
    ((((0, 2), (2, 4)),), (((1, 3), (3, 5)),)),
    ((((0, 1), (4, 5)), ((1, 2),)), (((0, 1), (4, 5)), ((3, 4),))),
    ((((2, 3), (3, 4)), ((1, 3), (3, 5))), (((2, 3), (1, 2)), ((0, 2), (2, 4)))),
)
GROUPS = 5
FOUND = 2 * GROUP * GROUPS


def pair_places(side):
    places, group = {}, 0
    for stage in STAGES:
        for pairs in stage[side]:
            for number, pair in enumerate(pairs):
                places.setdefault(pair, (group, number))
            group += 1
    return places


def stage_codes(number, side):
    codes = []
    for groups in zip(*STAGES[number]):
        both = [
            sum((a | b << 3 | (b - a - 1) << 6) << 8 * k for k, (a, b) in enumerate(pairs)) for pairs in groups
        ]
        codes.append(jnp.where(side == 0, jnp.int32(both[0]), jnp.int32(both[1])))
    return codes


def tables():
    index = np.arange(SIDE)

    def angle(phases):
        return (phases % SIDE).astype(np.float32) * np.float32(2.0 * math.pi / SIDE)

    phases = np.outer(index, index)
    cos_table = np.cos(angle(phases)).astype(ml_dtypes.bfloat16)
    sin_table = np.sin(angle(phases)).astype(ml_dtypes.bfloat16)
    right = np.concatenate([cos_table[: HALF + 1], sin_table[1:HALF]], axis=0)
    left = np.ascontiguousarray(right.T)
    row_freq = np.concatenate([np.arange(HALF + 1), -np.arange(1, HALF)])
    window = np.arange(-REACH, REACH + 1)
    fold_phase = 2.0 * math.pi * (np.outer(row_freq, window) % SIDE) / SIDE
    fold_cos, fold_sin = np.cos(fold_phase), np.sin(fold_phase)
    fold = np.zeros((2, 2, SIDE, 2, 2, 2, SPAN), np.float32)
    for odd in range(2):
        for part, out, value in ((0, 0, fold_cos), (1, 0, -fold_sin), (0, 1, fold_sin), (1, 1, fold_cos)):
            high = value.astype(np.float32).astype(ml_dtypes.bfloat16).astype(np.float32)
            fold[odd, part, :, odd, out, 0, : window.size] = high
            fold[odd, part, :, odd, out, 1, : window.size] = value - high
    fold = fold.reshape(2, 2 * SIDE, 128).astype(ml_dtypes.bfloat16)
    col_freq = np.arange(HALF + 1)
    twice = np.where((col_freq == 0) | (col_freq == HALF), 1.0, 2.0)[None, :] / SIDE
    col_phase = 2.0 * math.pi * (np.outer(window, col_freq) % SIDE) / SIDE
    close = np.zeros((2, SPAN, ROWS), np.float32)
    close[0, : window.size, : HALF + 1] = twice * np.cos(col_phase)
    close[1, : window.size, : HALF + 1] = twice * np.sin(col_phase)
    close = close.reshape(2 * SPAN, ROWS)
    high = close.astype(ml_dtypes.bfloat16)
    low = (close - high.astype(np.float32)).astype(ml_dtypes.bfloat16)
    lane, wide = np.arange(128)[:, None], np.arange(256)[None, :]
    spread = ((lane // 64 == wide // 128) & (lane % 64 < SPAN)).astype(ml_dtypes.bfloat16)
    return right, left, fold, np.concatenate([high, low], axis=0), spread


def transform(patch, right, left):
    half_product = lax.dot_general(
        right, patch, (((1,), (1,)), ((), ())), preferred_element_type=jnp.float32
    ).astype(jnp.bfloat16)
    full = jnp.dot(half_product, left, preferred_element_type=jnp.float32)
    lane = lax.broadcasted_iota(jnp.int32, (HALF, HALF), 1)
    row = lax.broadcasted_iota(jnp.int32, (HALF, HALF), 0)
    first_lane, first_row = lane == 0, row == 0
    cc, sc = full[:HALF, :HALF], full[:HALF, HALF:]
    last_c, last_s = full[HALF:, :HALF], full[HALF:, HALF:]
    cs, ss = jnp.where(first_row, 0.0, last_c), jnp.where(first_row, 0.0, last_s)

    def parts(cc, sc, cs, ss, edge):
        low_sc, low_ss = jnp.where(edge, 0.0, sc), jnp.where(edge, 0.0, ss)
        return jnp.concatenate(
            [
                cc - low_ss,
                jnp.where(edge, sc, cc + ss),
                -(cs + low_sc),
                jnp.where(edge, -ss, sc - cs),
            ],
            axis=1,
        ).astype(jnp.bfloat16)

    def with_size(spectrum):
        real, imag = spectrum[:, :SIDE].astype(jnp.float32), spectrum[:, SIDE:].astype(jnp.float32)
        square = real * real + imag * imag
        return spectrum, square * lax.rsqrt(jnp.maximum(square, 1e-30))

    tail = ROWS - HALF
    keep = row[:tail] == 0
    end_c, end_s = jnp.where(keep, last_c[:tail], 0.0), jnp.where(keep, last_s[:tail], 0.0)
    none = jnp.zeros_like(end_c)
    main = with_size(parts(cc, sc, cs, ss, first_lane))
    return main, with_size(parts(end_c, end_s, none, none, first_lane[:tail]))


def stage_kernel(number, consts, blocks, state, scratch):
    right, left, fold, close, spread = consts
    specs, sizes, offs, found = state
    power, folded, new_specs, new_sizes = scratch
    device = lax.axis_index("member")
    row, side = device // 2, lax.rem(device, 2)
    codes = stage_codes(number, side)
    first_group = sum(len(stage[0]) for stage in STAGES[:number])
    near, far = 4 * row, 4 * (1 - row)
    places = ((near + side, far + side), (2 + side,), (far + 1 - side, near + 1 - side), (3 - side,))[number]
    chunk = 16

    if number == 0:
        found[...] = jnp.zeros_like(found)
    right_table, left_table = right[...], left[...]

    def take(block, n, specs, sizes, at):
        patch = block[n * SIDE : (n + 1) * SIDE, :]
        if block.shape[1] < SIDE:
            patch = jnp.concatenate([patch, block[(NODES + n) * SIDE : (NODES + n + 1) * SIDE, :]], axis=1)
        main, end = transform(patch, right_table, left_table)
        specs[at, :HALF, :], sizes[at, :HALF, :] = main
        specs[at, HALF:, :], sizes[at, HALF:, :] = end

    for block, place in zip(blocks, places):
        offs[place] = block[block.shape[0] - EXTRA :, :128]
        for n in range(NODES if number < 3 else 0):
            take(block, n, specs, sizes, place * NODES + n)

    for n in range(NODES):
        if number == 3:
            take(blocks[0], n, new_specs, new_sizes, n)
        for k, j in [(k, j) for k, pairs in enumerate(STAGES[number][0]) for j in range(n, NODES * len(pairs), NODES)]:
            code = codes[k]
            bits = jnp.right_shift(code, 8 * (j // NODES))
            a_place, b_place = bits & 7, jnp.right_shift(bits, 3) & 7
            if number < 3:
                a_from, b_from = (specs, sizes, a_place * NODES + j % NODES), (specs, sizes, b_place * NODES + j % NODES)
            else:
                taken = a_place == places[0]
                a_from = (new_specs, new_sizes, j % NODES)
                b_from = (specs, sizes, jnp.where(taken, b_place, a_place) * NODES + j % NODES)
                sign = jnp.where(taken, 1.0, -1.0).astype(jnp.float32)

            def size_of(rows, a_from=a_from, b_from=b_from):
                return a_from[1][a_from[2], rows, :] * b_from[1][b_from[2], rows, :]

            total = jnp.zeros((8, SIDE), jnp.float32)
            for start in range(0, ROWS, chunk):
                rows = slice(start, start + chunk)
                size = size_of(rows)
                if start == 0:
                    edge = lax.broadcasted_iota(jnp.int32, (chunk, SIDE), 0) == 0
                    size = jnp.where(edge, 0.5 * size, size)
                elif start == HALF:
                    size = 0.5 * size
                total = total + size[:8] + size[8:]
            floor = jnp.sum(total) * (2.0 / (SIDE * SIDE)) + 1e-6
            for start in range(0, ROWS, chunk):
                rows = slice(start, start + chunk)
                scale = pl.reciprocal(size_of(rows) + floor, approx=True)
                a = a_from[0][a_from[2], rows, :].astype(jnp.float32)
                b = b_from[0][b_from[2], rows, :].astype(jnp.float32)
                ar, ai, br, bi = a[:, :SIDE], a[:, SIDE:], b[:, :SIDE], b[:, SIDE:]
                real = (ar * br + ai * bi) * scale
                imag = (ai * br - ar * bi) * (scale if number < 3 else scale * sign)
                to = slice(ROWS * (j // 2) + start, ROWS * (j // 2) + start + chunk)
                power[k, j % 2, to, :SIDE] = real.astype(jnp.bfloat16)
                power[k, j % 2, to, SIDE:] = imag.astype(jnp.bfloat16)
    for k, pairs in enumerate(STAGES[number][0]):
        held = NODES * len(pairs)
        used = ROWS * held // 2
        both = sum(
            jnp.dot(power[k, odd, :used, :], fold[odd], preferred_element_type=jnp.float32) for odd in range(2)
        )
        folded[:, 256 * k : 256 * k + 128] = both[:ROWS]
        folded[:, 256 * k + 128 : 256 * (k + 1)] = both[ROWS:] if held > 2 else jnp.zeros_like(both)
    if not codes:
        return

    sums = folded[...]
    high = sums.astype(jnp.bfloat16)
    low = (sums - high.astype(jnp.float32)).astype(jnp.bfloat16)
    closed = jnp.dot(close[...], high, preferred_element_type=jnp.float32)
    rest = jnp.dot(close[: 2 * SPAN], low, preferred_element_type=jnp.float32)
    closed = closed[: 2 * SPAN] + closed[2 * SPAN :] + rest
    lane = lax.broadcasted_iota(jnp.int32, (SPAN, 128), 1)
    step_u = ((lane & (SPAN - 1)) - REACH).astype(jnp.float32)
    step_v = (lax.broadcasted_iota(jnp.int32, (SPAN, 128), 0) - REACH).astype(jnp.float32)
    all_offs, pieces = [], []
    for k, code in enumerate(codes):
        for pair in range(2):
            bits = jnp.right_shift(code, 8 * pair)
            own = offs[bits & 7].astype(jnp.float32)[:8]
            own = jnp.where((jnp.right_shift(bits, 6) & 1) == 0, own[:4], own[4:])
            off_y = jnp.where(lane[:1] < 64, own[0:1], own[1:2])
            off_x = jnp.where(lane[:1] < 64, own[2:3], own[3:4])
            all_offs.append(own)
            at = slice(256 * k + 128 * pair, 256 * k + 128 * (pair + 1))
            by_cos, by_sin = closed[:SPAN, at], closed[SPAN:, at]
            by_cos = by_cos + pltpu.roll(by_cos, 128 - SPAN, axis=1)
            by_sin = pltpu.roll(by_sin, 128 - 2 * SPAN, axis=1) + pltpu.roll(by_sin, 128 - 3 * SPAN, axis=1)
            correlation = by_cos - by_sin
            from_y, from_x = step_u - off_y, step_v - off_x
            inside = (jnp.abs(from_y) < 1.5) & (jnp.abs(from_x) < 1.5)
            weight = jnp.where(inside, jnp.exp(3.0 * jnp.tanh(correlation)), 0.0)
            sums = jnp.concatenate(
                [
                    jnp.sum(weight, axis=0, keepdims=True),
                    jnp.sum(weight * from_y, axis=0, keepdims=True),
                    jnp.sum(weight * from_x, axis=0, keepdims=True),
                    jnp.zeros((5, 128), jnp.float32),
                ],
                axis=0,
            )
            for _ in range(3):
                pieces.append(sums.astype(jnp.bfloat16))
                sums = sums - pieces[-1].astype(jnp.float32)
    whole = jnp.dot(jnp.concatenate(pieces, axis=0), spread[...], preferred_element_type=jnp.float32)
    result = found[...]
    for pair, own in enumerate(all_offs):
        parts = [whole[24 * pair + 8 * piece : 24 * pair + 8 * (piece + 1)] for piece in range(3)]
        total = parts[0] + parts[1] + parts[2]
        ratio_y, ratio_x = total[1:2] / total[0:1], total[2:3] / total[0:1]
        for n in range(NODES):
            at = slice(128 * n, 128 * (n + 1))
            column = 2 * (GROUP * first_group + NODES * pair + n)
            result = jnp.where(lane[:1] == column, own[n : n + 1] + ratio_y[:, at], result)
            result = jnp.where(lane[:1] == column + 1, own[NODES + n : NODES + n + 1] + ratio_x[:, at], result)
    found[...] = result


def run_stage(number, consts, state, blocks, mesh_inputs=()):
    vmem, hbm = pl.BlockSpec(memory_space=pltpu.VMEM), pl.BlockSpec(memory_space=pltpu.HBM)
    shapes = (
        ((WINDOW * NODES, ROWS, 2 * SIDE), jnp.bfloat16),
        ((WINDOW * NODES, ROWS, SIDE), jnp.float32),
        ((WINDOW, EXTRA, 128), jnp.bfloat16),
        ((1, 128), jnp.float32),
    )
    first = number == 0
    if first:
        consts = [pltpu.with_memory_space_constraint(c, pltpu.HBM) for c in consts]
        shapes += tuple((c.shape, c.dtype) for c in consts)
        shapes += (((4 * NODE_COLS, 128), jnp.float32), ((8, 128), jnp.float32))
        mesh_inputs = [pltpu.with_memory_space_constraint(x, pltpu.HBM) for x in mesh_inputs]
    count = len(consts)
    args = [*consts, *blocks, *state, *mesh_inputs]
    fixed = count + len(blocks)

    def kernel(*refs):
        outs, scratch = refs[len(args) : len(args) + len(shapes)], refs[len(args) + len(shapes) :]
        tables_in, blocks_in = refs[:count], refs[count:fixed]
        if first:
            held, sems = outs[4 : 4 + count], scratch[-1]
            sources = [*tables_in, *refs[fixed : len(args)]]
            targets = [*held, *scratch[4:6]]
            copies = [pltpu.make_async_copy(a, b, sems.at[k]) for k, (a, b) in enumerate(zip(sources, targets))]
            for copy in copies:
                copy.start()
            for copy in copies[:2]:
                copy.wait()
            tables_in = held
        stage_kernel(number, tables_in, blocks_in, outs[:4], scratch[:4])
        if first:
            for copy in copies[2:]:
                copy.wait()
            mesh_rows(*scratch[4:6], *outs[4 + count :], scratch[6])

    groups = max(len(STAGES[number][0]), 1)
    out = pl.pallas_call(
        kernel,
        out_shape=tuple(pltpu.VMEM(shape, dtype) for shape, dtype in shapes),
        in_specs=[hbm if first else vmem] * count
        + [vmem] * (len(args) - count - len(mesh_inputs))
        + [hbm] * len(mesh_inputs),
        out_specs=(vmem,) * len(shapes),
        input_output_aliases={fixed + k: k for k in range(len(state))},
        scratch_shapes=[
            pltpu.VMEM((groups, 2, 2 * ROWS, 2 * SIDE), jnp.bfloat16),
            pltpu.VMEM((ROWS, 256 * groups), jnp.float32),
            pltpu.VMEM((NODES, ROWS, 2 * SIDE), jnp.bfloat16),
            pltpu.VMEM((NODES, ROWS, SIDE), jnp.float32),
        ]
        + [pltpu.VMEM(x.shape, x.dtype) for x in mesh_inputs]
        + ([pltpu.VMEM((8, 128), jnp.int32), pltpu.SemaphoreType.DMA((count + 2,))] if first else []),
        compiler_params=pltpu.CompilerParams(vmem_limit_bytes=24 * 1024 * 1024),
        cost_estimate=pl.CostEstimate(flops=1, bytes_accessed=1, transcendentals=0),
        name=f"stage{number}",
    )(*args)
    return tuple(out[:4]), tuple(out[4:])


def mesh_rows(node_links, node_offsets, counts, offsets, links):
    own = slice(NODE_COLS, 3 * NODE_COLS)
    links[...] = jnp.full_like(links, -1)
    offsets[...] = jnp.zeros_like(offsets)
    first = (lax.axis_index("tile") * 2 - 1) * NODE_COLS
    for k in range(4):
        links[k : k + 1, own] = node_links[k] - first
        offsets[k : k + 1, own] = node_offsets[k // 2, k % 2].astype(jnp.float32)
    for e in range(4 * NODE_COLS):
        counts[e : e + 1, :] = jnp.sum(jnp.where(links[0:4, :] == e, 1.0, 0.0), axis=0, keepdims=True)


def prepare_kernel(patches, all_offsets, *refs):
    blocks, offsets, sems = refs[:4], refs[4], refs[5]
    device = lax.axis_index("member")
    row, side = device // 2, lax.rem(device, 2)
    numbers = [2 * r + s for r in (row, 1 - row) for s in (side, 1 - side)]
    copies = []
    for k in (2, 3, 0, 1):
        block, width = blocks[k], blocks[k].shape[1]
        for half in range(SIDE // width):
            source = patches.at[numbers[k], :, pl.ds(half * width, width)]
            target = block.at[pl.ds(half * NODES * SIDE, NODES * SIDE)]
            copies.append(pltpu.make_async_copy(source, target, sems.at[len(copies)]))
            copies[-1].start()
    offsets_copy = pltpu.make_async_copy(all_offsets, offsets, sems.at[6])
    offsets_copy.start()
    offsets_copy.wait()
    line = lax.broadcasted_iota(jnp.int32, (EXTRA, 128), 0)
    for block, number in zip(blocks, numbers):
        rows = jnp.zeros((EXTRA, 128), jnp.float32)
        for partner in range(2):
            for part in range(2):
                for n in range(NODES):
                    value = offsets[partner, part, 0, NODES * number + n].astype(jnp.float32)
                    rows = jnp.where(line == 4 * partner + 2 * part + n, value, rows)
        for start in range(0, block.shape[1], 128):
            block[block.shape[0] - EXTRA :, start : start + 128] = rows.astype(jnp.bfloat16)
    for copy in copies:
        copy.wait()


def prepare(patches, offsets):
    return pl.pallas_call(
        prepare_kernel,
        out_shape=tuple(pltpu.VMEM(shape, jnp.bfloat16) for shape in ((HALVES, 128),) * 2 + ((BLOCK, SIDE),) * 2),
        in_specs=[pl.BlockSpec(memory_space=pltpu.HBM)] * 2,
        out_specs=(pl.BlockSpec(memory_space=pltpu.VMEM),) * 4,
        scratch_shapes=[pltpu.SMEM((2, 2, 1, 2 * GROUP), jnp.int32), pltpu.SemaphoreType.DMA((7,))],
        cost_estimate=pl.CostEstimate(flops=1, bytes_accessed=1, transcendentals=0),
        name="prepare",
    )(
        pltpu.with_memory_space_constraint(patches.reshape(4, NODES * SIDE, SIDE), pltpu.HBM),
        pltpu.with_memory_space_constraint(offsets, pltpu.HBM),
    )


def finish_kernel(total, every, counts, offsets, shifts_out, moved_out, shifts, moved, sems):
    device, tile = lax.axis_index("member"), lax.axis_index("tile")
    position = 4 * lax.axis_index("group") + device
    lane = lax.broadcasted_iota(jnp.int32, (2, 128), 1)
    own = slice(NODE_COLS, 3 * NODE_COLS)
    tiles = lax.axis_size("tile")
    places = [pair_places(side) for side in range(2)]
    spread = {}
    near_tiles = {0: tile, -1: jnp.maximum(tile - 1, 0), 1: jnp.minimum(tile + 1, tiles - 1)}

    def shifts_of(member, step, column):
        if (member, step, column) not in spread:
            values = every[member * tiles + near_tiles[step]]
            parts = [jnp.broadcast_to(values[:, column + part : column + part + 1], (1, 128)) for part in range(2)]
            spread[member, step, column] = jnp.concatenate(parts, axis=0)
        return spread[member, step, column]

    def put(held, start, row, section, partner, step, source=0):
        first = section + 2 * row
        for side in range(2):
            group, number = places[side][(first, first + partner)]
            for n in range(NODES):
                value = shifts_of(2 * row + side, step, FOUND * source + 2 * (GROUP * group + NODES * number + n))
                held = jnp.where(lane == start + 2 * side + n, value, held)
        return held

    def put_next(held, start, row, section, step):
        if row == 0 and section < 0:
            return put(held, start, 0, section + 4, 1, step, 1)
        if row == 1 and section > 2:
            return put(held, start, 1, section - 4, 1, step, 1)
        return put(held, start, row, section, 1, step)

    blank = jnp.zeros((2, 128), jnp.float32)
    next_all, second_all = [], []
    for section in range(-2, 5):
        held = put_next(blank, NODE_COLS, 0, section, 0)
        held = put_next(held, 2 * NODE_COLS, 1, section, 0)
        if -1 <= section < 4:
            held = put_next(held, 0, 1, section, -1)
            held = put_next(held, 3 * NODE_COLS, 0, section, 1)
        next_all.append(held)
    for section in range(4):
        held = put(blank, NODE_COLS, 0, section, 2, 0)
        if section < 2:
            held = put(held, 2 * NODE_COLS, 1, section, 2, 0)
        else:
            held = put(held, 2 * NODE_COLS, 1, section - 4, 2, 0, 1)
        second_all.append(held)

    def pick(values):
        chosen = values[3]
        for r in range(3):
            chosen = jnp.where(device == r, values[r], chosen)
        return chosen

    behind2, behind, here, ahead = (pick(next_all[k : k + 4]) for k in range(4))
    found_next = jnp.where(position + 1 < total, here, offsets[0:2, :])
    found_second = jnp.where(position + 2 < total, pick(second_all), offsets[2:4, :])
    has_next = [
        jnp.where((position + d >= 0) & (position + d + 1 < total), 1.0, 0.0).astype(jnp.float32)
        for d in (-2, -1, 0, 1)
    ]
    pulls = [-h * f for h, f in zip(has_next, (behind2, behind, here, ahead))]
    behind_pos, positions, ahead_pos = (0.25 * (pulls[k + 1] - pulls[k]) for k in range(3))
    neighbours = blank
    for e in range(4 * NODE_COLS):
        neighbours = neighbours + counts[e : e + 1, :] * positions[:, e : e + 1]
    in_plane = 0.25 * (neighbours - 4.0 * positions)
    pull = has_next[2] * (ahead_pos - positions - here)
    pull_behind = has_next[1] * (positions - behind_pos - behind)
    positions = positions + 0.5 * (in_plane + 0.5 * (pull - pull_behind))
    for part in range(2):
        shifts[0, part] = found_next[part : part + 1, own]
        shifts[1, part] = found_second[part : part + 1, own]
        moved[part] = positions[part : part + 1, own]
    copies = [
        pltpu.make_async_copy(shifts, shifts_out, sems.at[0]),
        pltpu.make_async_copy(moved, moved_out, sems.at[1]),
    ]
    for copy in copies:
        copy.start()
    for copy in copies:
        copy.wait()


def finish(every, counts, offsets, total):
    vmem, hbm = pl.BlockSpec(memory_space=pltpu.VMEM), pl.BlockSpec(memory_space=pltpu.HBM)
    nodes = 2 * NODE_COLS
    shapes = ((2, 2, 1, nodes), (2, 1, nodes))
    return pl.pallas_call(
        functools.partial(finish_kernel, total),
        out_shape=tuple(jax.ShapeDtypeStruct(shape, jnp.float32) for shape in shapes),
        in_specs=[vmem] * 3,
        out_specs=(hbm, hbm),
        scratch_shapes=[pltpu.VMEM(shape, jnp.float32) for shape in shapes] + [pltpu.SemaphoreType.DMA((2,))],
        cost_estimate=pl.CostEstimate(flops=1, bytes_accessed=1, transcendentals=0),
        name="finish",
    )(every, counts, offsets)


def shards(sections, offsets, node_links):
    patches = sections[0]
    groups, tiles = lax.axis_size("group"), lax.axis_size("tile")

    def send(value, steps):
        total = 4 * groups
        pairs = [(i, i + steps[i % 4]) for i in range(total) if 0 <= i + steps[i % 4] < total]
        return lax.ppermute(value, ("group", "member"), pairs)

    kept, beside, across, slanted = prepare(patches, offsets)
    across_in = send(across, (2, 2, -2, -2))
    border_in = send(kept, (-4, -4, 4, 4))
    border_beside_in = send(beside, (-3, -5, 5, 3))
    beside_in = send(beside, (1, -1, 1, -1))
    slanted_in = send(slanted, (3, 1, -1, -3))
    state, held = run_stage(0, [jnp.asarray(t) for t in tables()], (), [kept, border_in], (node_links, offsets))
    *consts, counts, own_offsets = held
    state, _ = run_stage(1, consts, state, [across_in])
    state, _ = run_stage(2, consts, state, [border_beside_in, beside_in])
    state, _ = run_stage(3, consts, state, [slanted_in])
    found = state[3]

    near = send(found, (4, 4, -4, -4))
    rest = jnp.zeros((1, 128 - 2 * FOUND), jnp.float32)
    found = jnp.concatenate([found[:, :FOUND], near[:, :FOUND], rest], axis=1)
    every = lax.all_to_all(jnp.broadcast_to(found[None], (4 * tiles, 1, 128)), ("member", "tile"), 0, 0)
    near_by = [pltpu.with_memory_space_constraint(x, pltpu.VMEM) for x in (every, counts, own_offsets)]
    return finish(*near_by, 4 * groups)


def solution(mesh):
    sections, tiles = mesh.devices.shape
    mesh = jax.sharding.Mesh(mesh.devices.reshape(sections // 4, 4, tiles), ("group", "member", "tile"))
    gz = ("group", "member")
    return jax.shard_map(
        shards,
        mesh=mesh,
        in_specs=(P(gz, "tile", None, None), P(None, None, gz, "tile"), P(None, gz, "tile")),
        out_specs=(P(None, None, gz, "tile"), P(None, gz, "tile")),
        check_vma=False,
    )
```

```python
import functools
import math

import jax
import jax.numpy as jnp
import ml_dtypes
import numpy as np
from jax import lax
from jax.experimental import pallas as pl
from jax.experimental.pallas import tpu as pltpu
from jax.sharding import PartitionSpec as P

NODE_COLS = 4
SIDE = 256
HALF = SIDE // 2
ROWS = 144
REACH = 4
SPAN = 16
GROUP = 4
NODES = 2
EXTRA = 16
BLOCK = NODES * SIDE + EXTRA
HALVES = 2 * NODES * SIDE + EXTRA
WINDOW = 6

STAGES = (
    ((), ()),
    ((((0, 2), (2, 4)),), (((1, 3), (3, 5)),)),
    ((((0, 1), (4, 5)), ((1, 2),)), (((0, 1), (4, 5)), ((3, 4),))),
    ((((2, 3), (3, 4)), ((1, 3), (3, 5))), (((2, 3), (1, 2)), ((0, 2), (2, 4)))),
)
GROUPS = 5
FOUND = 2 * GROUP * GROUPS


def pair_places(side):
    places, group = {}, 0
    for stage in STAGES:
        for pairs in stage[side]:
            for number, pair in enumerate(pairs):
                places.setdefault(pair, (group, number))
            group += 1
    return places


def stage_codes(number, side):
    codes = []
    for groups in zip(*STAGES[number]):
        both = [
            sum((a | b << 3 | (b - a - 1) << 6) << 8 * k for k, (a, b) in enumerate(pairs)) for pairs in groups
        ]
        codes.append(jnp.where(side == 0, jnp.int32(both[0]), jnp.int32(both[1])))
    return codes


def tables():
    index = np.arange(SIDE)

    def angle(phases):
        return (phases % SIDE).astype(np.float32) * np.float32(2.0 * math.pi / SIDE)

    phases = np.outer(index, index)
    cos_table = np.cos(angle(phases)).astype(ml_dtypes.bfloat16)
    sin_table = np.sin(angle(phases)).astype(ml_dtypes.bfloat16)
    right = np.concatenate([cos_table[: HALF + 1], sin_table[1:HALF]], axis=0)
    left = np.ascontiguousarray(right.T)
    row_freq = np.concatenate([np.arange(HALF + 1), -np.arange(1, HALF)])
    window = np.arange(-REACH, REACH + 1)
    fold_phase = 2.0 * math.pi * (np.outer(row_freq, window) % SIDE) / SIDE
    fold_cos, fold_sin = np.cos(fold_phase), np.sin(fold_phase)
    fold = np.zeros((2, 2, SIDE, 2, 2, 2, SPAN), np.float32)
    for odd in range(2):
        for part, out, value in ((0, 0, fold_cos), (1, 0, -fold_sin), (0, 1, fold_sin), (1, 1, fold_cos)):
            high = value.astype(np.float32).astype(ml_dtypes.bfloat16).astype(np.float32)
            fold[odd, part, :, odd, out, 0, : window.size] = high
            fold[odd, part, :, odd, out, 1, : window.size] = value - high
    fold = fold.reshape(2, 2 * SIDE, 128).astype(ml_dtypes.bfloat16)
    col_freq = np.arange(HALF + 1)
    twice = np.where((col_freq == 0) | (col_freq == HALF), 1.0, 2.0)[None, :] / SIDE
    col_phase = 2.0 * math.pi * (np.outer(window, col_freq) % SIDE) / SIDE
    close = np.zeros((2, SPAN, ROWS), np.float32)
    close[0, : window.size, : HALF + 1] = twice * np.cos(col_phase)
    close[1, : window.size, : HALF + 1] = twice * np.sin(col_phase)
    close = close.reshape(2 * SPAN, ROWS)
    high = close.astype(ml_dtypes.bfloat16)
    low = (close - high.astype(np.float32)).astype(ml_dtypes.bfloat16)
    lane, wide = np.arange(128)[:, None], np.arange(256)[None, :]
    spread = ((lane // 64 == wide // 128) & (lane % 64 < SPAN)).astype(ml_dtypes.bfloat16)
    return right, left, fold, np.concatenate([high, low], axis=0), spread


def transform(patch, right, left):
    half_product = lax.dot_general(
        right, patch, (((1,), (1,)), ((), ())), preferred_element_type=jnp.float32
    ).astype(jnp.bfloat16)
    full = jnp.dot(half_product, left, preferred_element_type=jnp.float32)
    lane = lax.broadcasted_iota(jnp.int32, (HALF, HALF), 1)
    row = lax.broadcasted_iota(jnp.int32, (HALF, HALF), 0)
    first_lane, first_row = lane == 0, row == 0
    cc, sc = full[:HALF, :HALF], full[:HALF, HALF:]
    last_c, last_s = full[HALF:, :HALF], full[HALF:, HALF:]
    cs, ss = jnp.where(first_row, 0.0, last_c), jnp.where(first_row, 0.0, last_s)

    def parts(cc, sc, cs, ss, edge):
        low_sc, low_ss = jnp.where(edge, 0.0, sc), jnp.where(edge, 0.0, ss)
        return jnp.concatenate(
            [
                cc - low_ss,
                jnp.where(edge, sc, cc + ss),
                -(cs + low_sc),
                jnp.where(edge, -ss, sc - cs),
            ],
            axis=1,
        ).astype(jnp.bfloat16)

    def with_size(spectrum):
        real, imag = spectrum[:, :SIDE].astype(jnp.float32), spectrum[:, SIDE:].astype(jnp.float32)
        square = real * real + imag * imag
        return spectrum, square * lax.rsqrt(jnp.maximum(square, 1e-30))

    tail = ROWS - HALF
    keep = row[:tail] == 0
    end_c, end_s = jnp.where(keep, last_c[:tail], 0.0), jnp.where(keep, last_s[:tail], 0.0)
    none = jnp.zeros_like(end_c)
    main = with_size(parts(cc, sc, cs, ss, first_lane))
    return main, with_size(parts(end_c, end_s, none, none, first_lane[:tail]))


def stage_kernel(number, consts, blocks, state, scratch):
    right, left, fold, close, spread = consts
    specs, sizes, offs, found = state
    power, folded, new_specs, new_sizes = scratch
    device = lax.axis_index("member")
    row, side = device // 2, lax.rem(device, 2)
    codes = stage_codes(number, side)
    first_group = sum(len(stage[0]) for stage in STAGES[:number])
    near, far = 4 * row, 4 * (1 - row)
    places = ((near + side, far + side), (2 + side,), (far + 1 - side, near + 1 - side), (3 - side,))[number]
    chunk = 16

    if number == 0:
        found[...] = jnp.zeros_like(found)
    right_table, left_table = right[...], left[...]

    def take(block, n, specs, sizes, at):
        patch = block[n * SIDE : (n + 1) * SIDE, :]
        if block.shape[1] < SIDE:
            patch = jnp.concatenate([patch, block[(NODES + n) * SIDE : (NODES + n + 1) * SIDE, :]], axis=1)
        main, end = transform(patch, right_table, left_table)
        specs[at, :HALF, :], sizes[at, :HALF, :] = main
        specs[at, HALF:, :], sizes[at, HALF:, :] = end

    for block, place in zip(blocks, places):
        offs[place] = block[block.shape[0] - EXTRA :, :128]
        for n in range(NODES if number < 3 else 0):
            take(block, n, specs, sizes, place * NODES + n)

    for n in range(NODES):
        if number == 3:
            take(blocks[0], n, new_specs, new_sizes, n)
        for k, j in [(k, j) for k, pairs in enumerate(STAGES[number][0]) for j in range(n, NODES * len(pairs), NODES)]:
            code = codes[k]
            bits = jnp.right_shift(code, 8 * (j // NODES))
            a_place, b_place = bits & 7, jnp.right_shift(bits, 3) & 7
            if number < 3:
                a_from, b_from = (specs, sizes, a_place * NODES + j % NODES), (specs, sizes, b_place * NODES + j % NODES)
            else:
                taken = a_place == places[0]
                a_from = (new_specs, new_sizes, j % NODES)
                b_from = (specs, sizes, jnp.where(taken, b_place, a_place) * NODES + j % NODES)
                sign = jnp.where(taken, 1.0, -1.0).astype(jnp.float32)

            def size_of(rows, a_from=a_from, b_from=b_from):
                return a_from[1][a_from[2], rows, :] * b_from[1][b_from[2], rows, :]

            total = jnp.zeros((8, SIDE), jnp.float32)
            for start in range(0, ROWS, chunk):
                rows = slice(start, start + chunk)
                size = size_of(rows)
                if start == 0:
                    edge = lax.broadcasted_iota(jnp.int32, (chunk, SIDE), 0) == 0
                    size = jnp.where(edge, 0.5 * size, size)
                elif start == HALF:
                    size = 0.5 * size
                total = total + size[:8] + size[8:]
            floor = jnp.sum(total) * (2.0 / (SIDE * SIDE)) + 1e-6
            for start in range(0, ROWS, chunk):
                rows = slice(start, start + chunk)
                scale = pl.reciprocal(size_of(rows) + floor, approx=True)
                a = a_from[0][a_from[2], rows, :].astype(jnp.float32)
                b = b_from[0][b_from[2], rows, :].astype(jnp.float32)
                ar, ai, br, bi = a[:, :SIDE], a[:, SIDE:], b[:, :SIDE], b[:, SIDE:]
                real = (ar * br + ai * bi) * scale
                imag = (ai * br - ar * bi) * (scale if number < 3 else scale * sign)
                to = slice(ROWS * (j // 2) + start, ROWS * (j // 2) + start + chunk)
                power[k, j % 2, to, :SIDE] = real.astype(jnp.bfloat16)
                power[k, j % 2, to, SIDE:] = imag.astype(jnp.bfloat16)
    for k, pairs in enumerate(STAGES[number][0]):
        held = NODES * len(pairs)
        used = ROWS * held // 2
        both = sum(
            jnp.dot(power[k, odd, :used, :], fold[odd], preferred_element_type=jnp.float32) for odd in range(2)
        )
        folded[:, 256 * k : 256 * k + 128] = both[:ROWS]
        folded[:, 256 * k + 128 : 256 * (k + 1)] = both[ROWS:] if held > 2 else jnp.zeros_like(both)
    if not codes:
        return

    sums = folded[...]
    high = sums.astype(jnp.bfloat16)
    low = (sums - high.astype(jnp.float32)).astype(jnp.bfloat16)
    closed = jnp.dot(close[...], high, preferred_element_type=jnp.float32)
    rest = jnp.dot(close[: 2 * SPAN], low, preferred_element_type=jnp.float32)
    closed = closed[: 2 * SPAN] + closed[2 * SPAN :] + rest
    lane = lax.broadcasted_iota(jnp.int32, (SPAN, 128), 1)
    step_u = ((lane & (SPAN - 1)) - REACH).astype(jnp.float32)
    step_v = (lax.broadcasted_iota(jnp.int32, (SPAN, 128), 0) - REACH).astype(jnp.float32)
    all_offs, pieces = [], []
    for k, code in enumerate(codes):
        for pair in range(2):
            bits = jnp.right_shift(code, 8 * pair)
            own = offs[bits & 7].astype(jnp.float32)[:8]
            own = jnp.where((jnp.right_shift(bits, 6) & 1) == 0, own[:4], own[4:])
            off_y = jnp.where(lane[:1] < 64, own[0:1], own[1:2])
            off_x = jnp.where(lane[:1] < 64, own[2:3], own[3:4])
            all_offs.append(own)
            at = slice(256 * k + 128 * pair, 256 * k + 128 * (pair + 1))
            by_cos, by_sin = closed[:SPAN, at], closed[SPAN:, at]
            by_cos = by_cos + pltpu.roll(by_cos, 128 - SPAN, axis=1)
            by_sin = pltpu.roll(by_sin, 128 - 2 * SPAN, axis=1) + pltpu.roll(by_sin, 128 - 3 * SPAN, axis=1)
            correlation = by_cos - by_sin
            from_y, from_x = step_u - off_y, step_v - off_x
            inside = (jnp.abs(from_y) < 1.5) & (jnp.abs(from_x) < 1.5)
            weight = jnp.where(inside, jnp.exp(3.0 * jnp.tanh(correlation)), 0.0)
            sums = jnp.concatenate(
                [
                    jnp.sum(weight, axis=0, keepdims=True),
                    jnp.sum(weight * from_y, axis=0, keepdims=True),
                    jnp.sum(weight * from_x, axis=0, keepdims=True),
                    jnp.zeros((5, 128), jnp.float32),
                ],
                axis=0,
            )
            for _ in range(3):
                pieces.append(sums.astype(jnp.bfloat16))
                sums = sums - pieces[-1].astype(jnp.float32)
    whole = jnp.dot(jnp.concatenate(pieces, axis=0), spread[...], preferred_element_type=jnp.float32)
    result = found[...]
    for pair, own in enumerate(all_offs):
        parts = [whole[24 * pair + 8 * piece : 24 * pair + 8 * (piece + 1)] for piece in range(3)]
        total = parts[0] + parts[1] + parts[2]
        ratio_y, ratio_x = total[1:2] / total[0:1], total[2:3] / total[0:1]
        for n in range(NODES):
            at = slice(128 * n, 128 * (n + 1))
            column = 2 * (GROUP * first_group + NODES * pair + n)
            result = jnp.where(lane[:1] == column, own[n : n + 1] + ratio_y[:, at], result)
            result = jnp.where(lane[:1] == column + 1, own[NODES + n : NODES + n + 1] + ratio_x[:, at], result)
    found[...] = result


def run_stage(number, consts, state, blocks, mesh_inputs=()):
    vmem, hbm = pl.BlockSpec(memory_space=pltpu.VMEM), pl.BlockSpec(memory_space=pltpu.HBM)
    shapes = (
        ((WINDOW * NODES, ROWS, 2 * SIDE), jnp.bfloat16),
        ((WINDOW * NODES, ROWS, SIDE), jnp.float32),
        ((WINDOW, EXTRA, 128), jnp.bfloat16),
        ((1, 128), jnp.float32),
    )
    first = number == 0
    if first:
        consts = [pltpu.with_memory_space_constraint(c, pltpu.HBM) for c in consts]
        shapes += tuple((c.shape, c.dtype) for c in consts)
        shapes += (((4 * NODE_COLS, 128), jnp.float32), ((8, 128), jnp.float32))
        mesh_inputs = [pltpu.with_memory_space_constraint(x, pltpu.HBM) for x in mesh_inputs]
    count = len(consts)
    args = [*consts, *blocks, *state, *mesh_inputs]
    fixed = count + len(blocks)

    def kernel(*refs):
        outs, scratch = refs[len(args) : len(args) + len(shapes)], refs[len(args) + len(shapes) :]
        tables_in, blocks_in = refs[:count], refs[count:fixed]
        if first:
            held, sems = outs[4 : 4 + count], scratch[-1]
            sources = [*tables_in, *refs[fixed : len(args)]]
            targets = [*held, *scratch[4:6]]
            copies = [pltpu.make_async_copy(a, b, sems.at[k]) for k, (a, b) in enumerate(zip(sources, targets))]
            for copy in copies:
                copy.start()
            for copy in copies[:2]:
                copy.wait()
            tables_in = held
        stage_kernel(number, tables_in, blocks_in, outs[:4], scratch[:4])
        if first:
            for copy in copies[2:]:
                copy.wait()
            mesh_rows(*scratch[4:6], *outs[4 + count :], scratch[6])

    groups = max(len(STAGES[number][0]), 1)
    out = pl.pallas_call(
        kernel,
        out_shape=tuple(pltpu.VMEM(shape, dtype) for shape, dtype in shapes),
        in_specs=[hbm if first else vmem] * count
        + [vmem] * (len(args) - count - len(mesh_inputs))
        + [hbm] * len(mesh_inputs),
        out_specs=(vmem,) * len(shapes),
        input_output_aliases={fixed + k: k for k in range(len(state))},
        scratch_shapes=[
            pltpu.VMEM((groups, 2, 2 * ROWS, 2 * SIDE), jnp.bfloat16),
            pltpu.VMEM((ROWS, 256 * groups), jnp.float32),
            pltpu.VMEM((NODES, ROWS, 2 * SIDE), jnp.bfloat16),
            pltpu.VMEM((NODES, ROWS, SIDE), jnp.float32),
        ]
        + [pltpu.VMEM(x.shape, x.dtype) for x in mesh_inputs]
        + ([pltpu.VMEM((8, 128), jnp.int32), pltpu.SemaphoreType.DMA((count + 2,))] if first else []),
        compiler_params=pltpu.CompilerParams(vmem_limit_bytes=24 * 1024 * 1024),
        cost_estimate=pl.CostEstimate(flops=1, bytes_accessed=1, transcendentals=0),
        name=f"stage{number}",
    )(*args)
    return tuple(out[:4]), tuple(out[4:])


def mesh_rows(node_links, node_offsets, counts, offsets, links):
    own = slice(NODE_COLS, 3 * NODE_COLS)
    links[...] = jnp.full_like(links, -1)
    offsets[...] = jnp.zeros_like(offsets)
    first = (lax.axis_index("tile") * 2 - 1) * NODE_COLS
    for k in range(4):
        links[k : k + 1, own] = node_links[k] - first
        offsets[k : k + 1, own] = node_offsets[k // 2, k % 2].astype(jnp.float32)
    for e in range(4 * NODE_COLS):
        counts[e : e + 1, :] = jnp.sum(jnp.where(links[0:4, :] == e, 1.0, 0.0), axis=0, keepdims=True)


def prepare_kernel(patches, all_offsets, *refs):
    blocks, offsets, sems = refs[:4], refs[4], refs[5]
    device = lax.axis_index("member")
    row, side = device // 2, lax.rem(device, 2)
    numbers = [2 * r + s for r in (row, 1 - row) for s in (side, 1 - side)]
    offsets_copy = pltpu.make_async_copy(all_offsets, offsets, sems.at[6])
    offsets_copy.start()
    copies = []
    for k in (2, 3, 0, 1):
        block, width = blocks[k], blocks[k].shape[1]
        for half in range(SIDE // width):
            source = patches.at[numbers[k], :, pl.ds(half * width, width)]
            target = block.at[pl.ds(half * NODES * SIDE, NODES * SIDE)]
            copies.append(pltpu.make_async_copy(source, target, sems.at[len(copies)]))
            copies[-1].start()
    offsets_copy.wait()
    line = lax.broadcasted_iota(jnp.int32, (EXTRA, 128), 0)
    for block, number in zip(blocks, numbers):
        rows = jnp.zeros((EXTRA, 128), jnp.float32)
        for partner in range(2):
            for part in range(2):
                for n in range(NODES):
                    value = offsets[partner, part, 0, NODES * number + n].astype(jnp.float32)
                    rows = jnp.where(line == 4 * partner + 2 * part + n, value, rows)
        for start in range(0, block.shape[1], 128):
            block[block.shape[0] - EXTRA :, start : start + 128] = rows.astype(jnp.bfloat16)
    for copy in copies:
        copy.wait()


def prepare(patches, offsets):
    return pl.pallas_call(
        prepare_kernel,
        out_shape=tuple(pltpu.VMEM(shape, jnp.bfloat16) for shape in ((HALVES, 128),) * 2 + ((BLOCK, SIDE),) * 2),
        in_specs=[pl.BlockSpec(memory_space=pltpu.HBM)] * 2,
        out_specs=(pl.BlockSpec(memory_space=pltpu.VMEM),) * 4,
        scratch_shapes=[pltpu.SMEM((2, 2, 1, 2 * GROUP), jnp.int32), pltpu.SemaphoreType.DMA((7,))],
        cost_estimate=pl.CostEstimate(flops=1, bytes_accessed=1, transcendentals=0),
        name="prepare",
    )(
        pltpu.with_memory_space_constraint(patches.reshape(4, NODES * SIDE, SIDE), pltpu.HBM),
        pltpu.with_memory_space_constraint(offsets, pltpu.HBM),
    )


def finish_kernel(total, every, counts, offsets, shifts_out, moved_out, shifts, moved, sems):
    device, tile = lax.axis_index("member"), lax.axis_index("tile")
    position = 4 * lax.axis_index("group") + device
    lane = lax.broadcasted_iota(jnp.int32, (2, 128), 1)
    part_row = lax.broadcasted_iota(jnp.int32, (2, 128), 0)
    own = slice(NODE_COLS, 3 * NODE_COLS)
    tiles = lax.axis_size("tile")
    places = [pair_places(side) for side in range(2)]
    spread = {}
    near_tiles = {0: tile, -1: jnp.maximum(tile - 1, 0), 1: jnp.minimum(tile + 1, tiles - 1)}

    def shifts_of(member, step, column):
        if (member, step, column) not in spread:
            values = every[member * tiles + near_tiles[step]]
            parts = [jnp.broadcast_to(values[:, column + part : column + part + 1], (2, 128)) for part in range(2)]
            spread[member, step, column] = jnp.where(part_row == 0, *parts)
        return spread[member, step, column]

    def put(held, start, row, section, partner, step, source=0):
        first = section + 2 * row
        for side in range(2):
            group, number = places[side][(first, first + partner)]
            for n in range(NODES):
                value = shifts_of(2 * row + side, step, FOUND * source + 2 * (GROUP * group + NODES * number + n))
                held = jnp.where(lane == start + 2 * side + n, value, held)
        return held

    def put_next(held, start, row, section, step):
        if row == 0 and section < 0:
            return put(held, start, 0, section + 4, 1, step, 1)
        if row == 1 and section > 2:
            return put(held, start, 1, section - 4, 1, step, 1)
        return put(held, start, row, section, 1, step)

    blank = jnp.zeros((2, 128), jnp.float32)
    next_all, second_all = [], []
    for section in range(-2, 5):
        held = put_next(blank, NODE_COLS, 0, section, 0)
        held = put_next(held, 2 * NODE_COLS, 1, section, 0)
        if -1 <= section < 4:
            held = put_next(held, 0, 1, section, -1)
            held = put_next(held, 3 * NODE_COLS, 0, section, 1)
        next_all.append(held)
    for section in range(4):
        held = put(blank, NODE_COLS, 0, section, 2, 0)
        if section < 2:
            held = put(held, 2 * NODE_COLS, 1, section, 2, 0)
        else:
            held = put(held, 2 * NODE_COLS, 1, section - 4, 2, 0, 1)
        second_all.append(held)

    def pick(values):
        chosen = values[3]
        for r in range(3):
            chosen = jnp.where(device == r, values[r], chosen)
        return chosen

    behind2, behind, here, ahead = (pick(next_all[k : k + 4]) for k in range(4))
    found_next = jnp.where(position + 1 < total, here, offsets[0:2, :])
    found_second = jnp.where(position + 2 < total, pick(second_all), offsets[2:4, :])
    has_next = [
        jnp.where((position + d >= 0) & (position + d + 1 < total), 1.0, 0.0).astype(jnp.float32)
        for d in (-2, -1, 0, 1)
    ]
    pulls = [-h * f for h, f in zip(has_next, (behind2, behind, here, ahead))]
    behind_pos, positions, ahead_pos = (0.25 * (pulls[k + 1] - pulls[k]) for k in range(3))
    neighbours = blank
    for e in range(4 * NODE_COLS):
        neighbours = neighbours + counts[e : e + 1, :] * positions[:, e : e + 1]
    in_plane = 0.25 * (neighbours - 4.0 * positions)
    pull = has_next[2] * (ahead_pos - positions - here)
    pull_behind = has_next[1] * (positions - behind_pos - behind)
    positions = positions + 0.5 * (in_plane + 0.5 * (pull - pull_behind))
    for part in range(2):
        shifts[0, part] = found_next[part : part + 1, own]
        shifts[1, part] = found_second[part : part + 1, own]
        moved[part] = positions[part : part + 1, own]
    copies = [
        pltpu.make_async_copy(shifts, shifts_out, sems.at[0]),
        pltpu.make_async_copy(moved, moved_out, sems.at[1]),
    ]
    for copy in copies:
        copy.start()
    for copy in copies:
        copy.wait()


def finish(every, counts, offsets, total):
    vmem, hbm = pl.BlockSpec(memory_space=pltpu.VMEM), pl.BlockSpec(memory_space=pltpu.HBM)
    nodes = 2 * NODE_COLS
    shapes = ((2, 2, 1, nodes), (2, 1, nodes))
    return pl.pallas_call(
        functools.partial(finish_kernel, total),
        out_shape=tuple(jax.ShapeDtypeStruct(shape, jnp.float32) for shape in shapes),
        in_specs=[vmem] * 3,
        out_specs=(hbm, hbm),
        scratch_shapes=[pltpu.VMEM(shape, jnp.float32) for shape in shapes] + [pltpu.SemaphoreType.DMA((2,))],
        cost_estimate=pl.CostEstimate(flops=1, bytes_accessed=1, transcendentals=0),
        name="finish",
    )(every, counts, offsets)


def shards(sections, offsets, node_links):
    patches = sections[0]
    groups, tiles = lax.axis_size("group"), lax.axis_size("tile")

    def send(value, steps):
        total = 4 * groups
        pairs = [(i, i + steps[i % 4]) for i in range(total) if 0 <= i + steps[i % 4] < total]
        return lax.ppermute(value, ("group", "member"), pairs)

    kept, beside, across, slanted = prepare(patches, offsets)
    across_in = send(across, (2, 2, -2, -2))
    border_in = send(kept, (-4, -4, 4, 4))
    border_beside_in = send(beside, (-3, -5, 5, 3))
    beside_in = send(beside, (1, -1, 1, -1))
    slanted_in = send(slanted, (3, 1, -1, -3))
    state, held = run_stage(0, [jnp.asarray(t) for t in tables()], (), [kept, border_in], (node_links, offsets))
    *consts, counts, own_offsets = held
    state, _ = run_stage(1, consts, state, [across_in])
    state, _ = run_stage(2, consts, state, [border_beside_in, beside_in])
    state, _ = run_stage(3, consts, state, [slanted_in])
    found = state[3]

    near = send(found, (4, 4, -4, -4))
    rest = jnp.zeros((1, 128 - 2 * FOUND), jnp.float32)
    found = jnp.concatenate([found[:, :FOUND], near[:, :FOUND], rest], axis=1)
    every = lax.all_to_all(jnp.broadcast_to(found[None], (4 * tiles, 1, 128)), ("member", "tile"), 0, 0)
    near_by = [pltpu.with_memory_space_constraint(x, pltpu.VMEM) for x in (every, counts, own_offsets)]
    return finish(*near_by, 4 * groups)


def solution(mesh):
    sections, tiles = mesh.devices.shape
    mesh = jax.sharding.Mesh(mesh.devices.reshape(sections // 4, 4, tiles), ("group", "member", "tile"))
    gz = ("group", "member")
    return jax.shard_map(
        shards,
        mesh=mesh,
        in_specs=(P(gz, "tile", None, None), P(None, None, gz, "tile"), P(None, gz, "tile")),
        out_specs=(P(None, None, gz, "tile"), P(None, gz, "tile")),
        check_vma=False,
    )
```

```python
import functools
import math

import jax
import jax.numpy as jnp
import ml_dtypes
import numpy as np
from jax import lax
from jax.experimental import pallas as pl
from jax.experimental.pallas import tpu as pltpu
from jax.sharding import PartitionSpec as P

NODE_COLS = 4
SIDE = 256
HALF = SIDE // 2
ROWS = 144
REACH = 4
SPAN = 16
GROUP = 4
NODES = 2
EXTRA = 16
BLOCK = NODES * SIDE + EXTRA
HALVES = 2 * NODES * SIDE + EXTRA
WINDOW = 6

STAGES = (
    ((), ()),
    ((((0, 2), (2, 4)),), (((1, 3), (3, 5)),)),
    ((((0, 1), (4, 5)), ((1, 2),)), (((0, 1), (4, 5)), ((3, 4),))),
    ((((2, 3), (3, 4)), ((1, 3), (3, 5))), (((2, 3), (1, 2)), ((0, 2), (2, 4)))),
)
GROUPS = 5
FOUND = 2 * GROUP * GROUPS


def pair_places(side):
    places, group = {}, 0
    for stage in STAGES:
        for pairs in stage[side]:
            for number, pair in enumerate(pairs):
                places.setdefault(pair, (group, number))
            group += 1
    return places


def stage_codes(number, side):
    codes = []
    for groups in zip(*STAGES[number]):
        both = [
            sum((a | b << 3 | (b - a - 1) << 6) << 8 * k for k, (a, b) in enumerate(pairs)) for pairs in groups
        ]
        codes.append(jnp.where(side == 0, jnp.int32(both[0]), jnp.int32(both[1])))
    return codes


def tables():
    index = np.arange(SIDE)

    def angle(phases):
        return (phases % SIDE).astype(np.float32) * np.float32(2.0 * math.pi / SIDE)

    phases = np.outer(index, index)
    cos_table = np.cos(angle(phases)).astype(ml_dtypes.bfloat16)
    sin_table = np.sin(angle(phases)).astype(ml_dtypes.bfloat16)
    right = np.concatenate([cos_table[: HALF + 1], sin_table[1:HALF]], axis=0)
    left = np.ascontiguousarray(right.T)
    row_freq = np.concatenate([np.arange(HALF + 1), -np.arange(1, HALF)])
    window = np.arange(-REACH, REACH + 1)
    fold_phase = 2.0 * math.pi * (np.outer(row_freq, window) % SIDE) / SIDE
    fold_cos, fold_sin = np.cos(fold_phase), np.sin(fold_phase)
    fold = np.zeros((2, 2, SIDE, 2, 2, 2, SPAN), np.float32)
    for odd in range(2):
        for part, out, value in ((0, 0, fold_cos), (1, 0, -fold_sin), (0, 1, fold_sin), (1, 1, fold_cos)):
            high = value.astype(np.float32).astype(ml_dtypes.bfloat16).astype(np.float32)
            fold[odd, part, :, odd, out, 0, : window.size] = high
            fold[odd, part, :, odd, out, 1, : window.size] = value - high
    fold = fold.reshape(2, 2 * SIDE, 128).astype(ml_dtypes.bfloat16)
    col_freq = np.arange(HALF + 1)
    twice = np.where((col_freq == 0) | (col_freq == HALF), 1.0, 2.0)[None, :] / SIDE
    col_phase = 2.0 * math.pi * (np.outer(window, col_freq) % SIDE) / SIDE
    close = np.zeros((2, SPAN, ROWS), np.float32)
    close[0, : window.size, : HALF + 1] = twice * np.cos(col_phase)
    close[1, : window.size, : HALF + 1] = twice * np.sin(col_phase)
    close = close.reshape(2 * SPAN, ROWS)
    high = close.astype(ml_dtypes.bfloat16)
    low = (close - high.astype(np.float32)).astype(ml_dtypes.bfloat16)
    lane, wide = np.arange(128)[:, None], np.arange(256)[None, :]
    spread = ((lane // 64 == wide // 128) & (lane % 64 < SPAN)).astype(ml_dtypes.bfloat16)
    return right, left, fold, np.concatenate([high, high, low], axis=1), spread


def transform(patch, right, left):
    half_product = lax.dot_general(
        right, patch, (((1,), (1,)), ((), ())), preferred_element_type=jnp.float32
    ).astype(jnp.bfloat16)
    full = jnp.dot(half_product, left, preferred_element_type=jnp.float32)
    lane = lax.broadcasted_iota(jnp.int32, (HALF, HALF), 1)
    row = lax.broadcasted_iota(jnp.int32, (HALF, HALF), 0)
    first_lane, first_row = lane == 0, row == 0
    cc, sc = full[:HALF, :HALF], full[:HALF, HALF:]
    last_c, last_s = full[HALF:, :HALF], full[HALF:, HALF:]
    cs, ss = jnp.where(first_row, 0.0, last_c), jnp.where(first_row, 0.0, last_s)

    def parts(cc, sc, cs, ss, edge):
        low_sc, low_ss = jnp.where(edge, 0.0, sc), jnp.where(edge, 0.0, ss)
        return jnp.concatenate(
            [
                cc - low_ss,
                jnp.where(edge, sc, cc + ss),
                -(cs + low_sc),
                jnp.where(edge, -ss, sc - cs),
            ],
            axis=1,
        ).astype(jnp.bfloat16)

    def with_size(spectrum):
        real, imag = spectrum[:, :SIDE].astype(jnp.float32), spectrum[:, SIDE:].astype(jnp.float32)
        square = real * real + imag * imag
        return spectrum, square * lax.rsqrt(jnp.maximum(square, 1e-30))

    tail = ROWS - HALF
    keep = row[:tail] == 0
    end_c, end_s = jnp.where(keep, last_c[:tail], 0.0), jnp.where(keep, last_s[:tail], 0.0)
    none = jnp.zeros_like(end_c)
    main = with_size(parts(cc, sc, cs, ss, first_lane))
    return main, with_size(parts(end_c, end_s, none, none, first_lane[:tail]))


def stage_kernel(number, consts, blocks, state, scratch):
    right, left, fold, close, spread = consts
    specs, sizes, offs, found = state
    power, folded, new_specs, new_sizes = scratch
    device = lax.axis_index("member")
    row, side = device // 2, lax.rem(device, 2)
    codes = stage_codes(number, side)
    first_group = sum(len(stage[0]) for stage in STAGES[:number])
    near, far = 4 * row, 4 * (1 - row)
    places = ((near + side, far + side), (2 + side,), (far + 1 - side, near + 1 - side), (3 - side,))[number]
    chunk = 16

    if number == 0:
        found[...] = jnp.zeros_like(found)
    right_table, left_table = right[...], left[...]

    def take(block, n, specs, sizes, at):
        patch = block[n * SIDE : (n + 1) * SIDE, :]
        if block.shape[1] < SIDE:
            patch = jnp.concatenate([patch, block[(NODES + n) * SIDE : (NODES + n + 1) * SIDE, :]], axis=1)
        main, end = transform(patch, right_table, left_table)
        specs[at, :HALF, :], sizes[at, :HALF, :] = main
        specs[at, HALF:, :], sizes[at, HALF:, :] = end

    for block, place in zip(blocks, places):
        offs[place] = block[block.shape[0] - EXTRA :, :128]
        for n in range(NODES if number < 3 else 0):
            take(block, n, specs, sizes, place * NODES + n)

    for n in range(NODES):
        if number == 3:
            take(blocks[0], n, new_specs, new_sizes, n)
        for k, j in [(k, j) for k, pairs in enumerate(STAGES[number][0]) for j in range(n, NODES * len(pairs), NODES)]:
            code = codes[k]
            bits = jnp.right_shift(code, 8 * (j // NODES))
            a_place, b_place = bits & 7, jnp.right_shift(bits, 3) & 7
            if number < 3:
                a_from, b_from = (specs, sizes, a_place * NODES + j % NODES), (specs, sizes, b_place * NODES + j % NODES)
            else:
                taken = a_place == places[0]
                a_from = (new_specs, new_sizes, j % NODES)
                b_from = (specs, sizes, jnp.where(taken, b_place, a_place) * NODES + j % NODES)
                sign = jnp.where(taken, 1.0, -1.0).astype(jnp.float32)

            def size_of(rows, a_from=a_from, b_from=b_from):
                return a_from[1][a_from[2], rows, :] * b_from[1][b_from[2], rows, :]

            total = jnp.zeros((8, SIDE), jnp.float32)
            for start in range(0, ROWS, chunk):
                rows = slice(start, start + chunk)
                size = size_of(rows)
                if start == 0:
                    edge = lax.broadcasted_iota(jnp.int32, (chunk, SIDE), 0) == 0
                    size = jnp.where(edge, 0.5 * size, size)
                elif start == HALF:
                    size = 0.5 * size
                total = total + size[:8] + size[8:]
            floor = jnp.sum(total) * (2.0 / (SIDE * SIDE)) + 1e-6
            for start in range(0, ROWS, chunk):
                rows = slice(start, start + chunk)
                scale = pl.reciprocal(size_of(rows) + floor, approx=True)
                a = a_from[0][a_from[2], rows, :].astype(jnp.float32)
                b = b_from[0][b_from[2], rows, :].astype(jnp.float32)
                ar, ai, br, bi = a[:, :SIDE], a[:, SIDE:], b[:, :SIDE], b[:, SIDE:]
                real = (ar * br + ai * bi) * scale
                imag = (ai * br - ar * bi) * (scale if number < 3 else scale * sign)
                to = slice(ROWS * (j // 2) + start, ROWS * (j // 2) + start + chunk)
                power[k, j % 2, to, :SIDE] = real.astype(jnp.bfloat16)
                power[k, j % 2, to, SIDE:] = imag.astype(jnp.bfloat16)
    for k, pairs in enumerate(STAGES[number][0]):
        held = NODES * len(pairs)
        used = ROWS * held // 2
        both = sum(
            jnp.dot(power[k, odd, :used, :], fold[odd], preferred_element_type=jnp.float32) for odd in range(2)
        )
        folded[:, 256 * k : 256 * k + 128] = both[:ROWS]
        folded[:, 256 * k + 128 : 256 * (k + 1)] = both[ROWS:] if held > 2 else jnp.zeros_like(both)
    if not codes:
        return

    sums = folded[...]
    high = sums.astype(jnp.bfloat16)
    low = (sums - high.astype(jnp.float32)).astype(jnp.bfloat16)
    parts = jnp.concatenate([high, low, high], axis=0)
    closed = jnp.dot(close[...], parts, preferred_element_type=jnp.float32)
    lane = lax.broadcasted_iota(jnp.int32, (SPAN, 128), 1)
    step_u = ((lane & (SPAN - 1)) - REACH).astype(jnp.float32)
    step_v = (lax.broadcasted_iota(jnp.int32, (SPAN, 128), 0) - REACH).astype(jnp.float32)
    all_offs, pieces = [], []
    for k, code in enumerate(codes):
        for pair in range(2):
            bits = jnp.right_shift(code, 8 * pair)
            own = offs[bits & 7].astype(jnp.float32)[:8]
            own = jnp.where((jnp.right_shift(bits, 6) & 1) == 0, own[:4], own[4:])
            off_y = jnp.where(lane[:1] < 64, own[0:1], own[1:2])
            off_x = jnp.where(lane[:1] < 64, own[2:3], own[3:4])
            all_offs.append(own)
            at = slice(256 * k + 128 * pair, 256 * k + 128 * (pair + 1))
            by_cos, by_sin = closed[:SPAN, at], closed[SPAN:, at]
            by_cos = by_cos + pltpu.roll(by_cos, 128 - SPAN, axis=1)
            by_sin = pltpu.roll(by_sin, 128 - 2 * SPAN, axis=1) + pltpu.roll(by_sin, 128 - 3 * SPAN, axis=1)
            correlation = by_cos - by_sin
            from_y, from_x = step_u - off_y, step_v - off_x
            inside = (jnp.abs(from_y) < 1.5) & (jnp.abs(from_x) < 1.5)
            weight = jnp.where(inside, jnp.exp(3.0 * jnp.tanh(correlation)), 0.0)
            sums = jnp.concatenate(
                [
                    jnp.sum(weight, axis=0, keepdims=True),
                    jnp.sum(weight * from_y, axis=0, keepdims=True),
                    jnp.sum(weight * from_x, axis=0, keepdims=True),
                    jnp.zeros((5, 128), jnp.float32),
                ],
                axis=0,
            )
            for _ in range(3):
                pieces.append(sums.astype(jnp.bfloat16))
                sums = sums - pieces[-1].astype(jnp.float32)
    whole = jnp.dot(jnp.concatenate(pieces, axis=0), spread[...], preferred_element_type=jnp.float32)
    result = found[...]
    for pair, own in enumerate(all_offs):
        parts = [whole[24 * pair + 8 * piece : 24 * pair + 8 * (piece + 1)] for piece in range(3)]
        total = parts[0] + parts[1] + parts[2]
        ratio_y, ratio_x = total[1:2] / total[0:1], total[2:3] / total[0:1]
        for n in range(NODES):
            at = slice(128 * n, 128 * (n + 1))
            column = 2 * (GROUP * first_group + NODES * pair + n)
            result = jnp.where(lane[:1] == column, own[n : n + 1] + ratio_y[:, at], result)
            result = jnp.where(lane[:1] == column + 1, own[NODES + n : NODES + n + 1] + ratio_x[:, at], result)
    found[...] = result


def run_stage(number, consts, state, blocks, mesh_inputs=()):
    vmem, hbm = pl.BlockSpec(memory_space=pltpu.VMEM), pl.BlockSpec(memory_space=pltpu.HBM)
    shapes = (
        ((WINDOW * NODES, ROWS, 2 * SIDE), jnp.bfloat16),
        ((WINDOW * NODES, ROWS, SIDE), jnp.float32),
        ((WINDOW, EXTRA, 128), jnp.bfloat16),
        ((1, 128), jnp.float32),
    )
    first = number == 0
    if first:
        consts = [pltpu.with_memory_space_constraint(c, pltpu.HBM) for c in consts]
        shapes += tuple((c.shape, c.dtype) for c in consts)
        shapes += (((4 * NODE_COLS, 128), jnp.float32), ((8, 128), jnp.float32))
        mesh_inputs = [pltpu.with_memory_space_constraint(x, pltpu.HBM) for x in mesh_inputs]
    count = len(consts)
    args = [*consts, *blocks, *state, *mesh_inputs]
    fixed = count + len(blocks)

    def kernel(*refs):
        outs, scratch = refs[len(args) : len(args) + len(shapes)], refs[len(args) + len(shapes) :]
        tables_in, blocks_in = refs[:count], refs[count:fixed]
        if first:
            held, sems = outs[4 : 4 + count], scratch[-1]
            sources = [*tables_in, *refs[fixed : len(args)]]
            targets = [*held, *scratch[4:6]]
            copies = [pltpu.make_async_copy(a, b, sems.at[k]) for k, (a, b) in enumerate(zip(sources, targets))]
            for copy in copies:
                copy.start()
            for copy in copies[:2]:
                copy.wait()
            tables_in = held
        stage_kernel(number, tables_in, blocks_in, outs[:4], scratch[:4])
        if first:
            for copy in copies[2:]:
                copy.wait()
            mesh_rows(*scratch[4:6], *outs[4 + count :], scratch[6])

    groups = max(len(STAGES[number][0]), 1)
    out = pl.pallas_call(
        kernel,
        out_shape=tuple(pltpu.VMEM(shape, dtype) for shape, dtype in shapes),
        in_specs=[hbm if first else vmem] * count
        + [vmem] * (len(args) - count - len(mesh_inputs))
        + [hbm] * len(mesh_inputs),
        out_specs=(vmem,) * len(shapes),
        input_output_aliases={fixed + k: k for k in range(len(state))},
        scratch_shapes=[
            pltpu.VMEM((groups, 2, 2 * ROWS, 2 * SIDE), jnp.bfloat16),
            pltpu.VMEM((ROWS, 256 * groups), jnp.float32),
            pltpu.VMEM((NODES, ROWS, 2 * SIDE), jnp.bfloat16),
            pltpu.VMEM((NODES, ROWS, SIDE), jnp.float32),
        ]
        + [pltpu.VMEM(x.shape, x.dtype) for x in mesh_inputs]
        + ([pltpu.VMEM((8, 128), jnp.int32), pltpu.SemaphoreType.DMA((count + 2,))] if first else []),
        compiler_params=pltpu.CompilerParams(vmem_limit_bytes=24 * 1024 * 1024),
        cost_estimate=pl.CostEstimate(flops=1, bytes_accessed=1, transcendentals=0),
        name=f"stage{number}",
    )(*args)
    return tuple(out[:4]), tuple(out[4:])


def mesh_rows(node_links, node_offsets, counts, offsets, links):
    own = slice(NODE_COLS, 3 * NODE_COLS)
    links[...] = jnp.full_like(links, -1)
    offsets[...] = jnp.zeros_like(offsets)
    first = (lax.axis_index("tile") * 2 - 1) * NODE_COLS
    for k in range(4):
        links[k : k + 1, own] = node_links[k] - first
        offsets[k : k + 1, own] = node_offsets[k // 2, k % 2].astype(jnp.float32)
    for e in range(4 * NODE_COLS):
        counts[e : e + 1, :] = jnp.sum(jnp.where(links[0:4, :] == e, 1.0, 0.0), axis=0, keepdims=True)


def prepare_kernel(patches, all_offsets, *refs):
    blocks, offsets, sems = refs[:4], refs[4], refs[5]
    device = lax.axis_index("member")
    row, side = device // 2, lax.rem(device, 2)
    numbers = [2 * r + s for r in (row, 1 - row) for s in (side, 1 - side)]
    offsets_copy = pltpu.make_async_copy(all_offsets, offsets, sems.at[6])
    offsets_copy.start()
    copies = []
    for k in (2, 3, 0, 1):
        block, width = blocks[k], blocks[k].shape[1]
        for half in range(SIDE // width):
            source = patches.at[numbers[k], :, pl.ds(half * width, width)]
            target = block.at[pl.ds(half * NODES * SIDE, NODES * SIDE)]
            copies.append(pltpu.make_async_copy(source, target, sems.at[len(copies)]))
            copies[-1].start()
    offsets_copy.wait()
    line = lax.broadcasted_iota(jnp.int32, (EXTRA, 128), 0)
    for block, number in zip(blocks, numbers):
        rows = jnp.zeros((EXTRA, 128), jnp.float32)
        for partner in range(2):
            for part in range(2):
                for n in range(NODES):
                    value = offsets[partner, part, 0, NODES * number + n].astype(jnp.float32)
                    rows = jnp.where(line == 4 * partner + 2 * part + n, value, rows)
        for start in range(0, block.shape[1], 128):
            block[block.shape[0] - EXTRA :, start : start + 128] = rows.astype(jnp.bfloat16)
    for copy in copies:
        copy.wait()


def prepare(patches, offsets):
    return pl.pallas_call(
        prepare_kernel,
        out_shape=tuple(pltpu.VMEM(shape, jnp.bfloat16) for shape in ((HALVES, 128),) * 2 + ((BLOCK, SIDE),) * 2),
        in_specs=[pl.BlockSpec(memory_space=pltpu.HBM)] * 2,
        out_specs=(pl.BlockSpec(memory_space=pltpu.VMEM),) * 4,
        scratch_shapes=[pltpu.SMEM((2, 2, 1, 2 * GROUP), jnp.int32), pltpu.SemaphoreType.DMA((7,))],
        cost_estimate=pl.CostEstimate(flops=1, bytes_accessed=1, transcendentals=0),
        name="prepare",
    )(
        pltpu.with_memory_space_constraint(patches.reshape(4, NODES * SIDE, SIDE), pltpu.HBM),
        pltpu.with_memory_space_constraint(offsets, pltpu.HBM),
    )


def finish_kernel(total, every, counts, offsets, shifts_out, moved_out, shifts, moved, sems):
    device, tile = lax.axis_index("member"), lax.axis_index("tile")
    position = 4 * lax.axis_index("group") + device
    lane = lax.broadcasted_iota(jnp.int32, (2, 128), 1)
    part_row = lax.broadcasted_iota(jnp.int32, (2, 128), 0)
    own = slice(NODE_COLS, 3 * NODE_COLS)
    tiles = lax.axis_size("tile")
    places = [pair_places(side) for side in range(2)]
    spread = {}
    near_tiles = {0: tile, -1: jnp.maximum(tile - 1, 0), 1: jnp.minimum(tile + 1, tiles - 1)}

    def shifts_of(member, step, column):
        if (member, step, column) not in spread:
            values = every[member * tiles + near_tiles[step]]
            parts = [jnp.broadcast_to(values[:, column + part : column + part + 1], (2, 128)) for part in range(2)]
            spread[member, step, column] = jnp.where(part_row == 0, *parts)
        return spread[member, step, column]

    def put(held, start, row, section, partner, step, source=0):
        first = section + 2 * row
        for side in range(2):
            group, number = places[side][(first, first + partner)]
            for n in range(NODES):
                value = shifts_of(2 * row + side, step, FOUND * source + 2 * (GROUP * group + NODES * number + n))
                held = jnp.where(lane == start + 2 * side + n, value, held)
        return held

    def put_next(held, start, row, section, step):
        if row == 0 and section < 0:
            return put(held, start, 0, section + 4, 1, step, 1)
        if row == 1 and section > 2:
            return put(held, start, 1, section - 4, 1, step, 1)
        return put(held, start, row, section, 1, step)

    blank = jnp.zeros((2, 128), jnp.float32)
    next_all, second_all = [], []
    for section in range(-2, 5):
        held = put_next(blank, NODE_COLS, 0, section, 0)
        held = put_next(held, 2 * NODE_COLS, 1, section, 0)
        if -1 <= section < 4:
            held = put_next(held, 0, 1, section, -1)
            held = put_next(held, 3 * NODE_COLS, 0, section, 1)
        next_all.append(held)
    for section in range(4):
        held = put(blank, NODE_COLS, 0, section, 2, 0)
        if section < 2:
            held = put(held, 2 * NODE_COLS, 1, section, 2, 0)
        else:
            held = put(held, 2 * NODE_COLS, 1, section - 4, 2, 0, 1)
        second_all.append(held)

    def pick(values):
        chosen = values[3]
        for r in range(3):
            chosen = jnp.where(device == r, values[r], chosen)
        return chosen

    behind2, behind, here, ahead = (pick(next_all[k : k + 4]) for k in range(4))
    found_next = jnp.where(position + 1 < total, here, offsets[0:2, :])
    found_second = jnp.where(position + 2 < total, pick(second_all), offsets[2:4, :])
    has_next = [
        jnp.where((position + d >= 0) & (position + d + 1 < total), 1.0, 0.0).astype(jnp.float32)
        for d in (-2, -1, 0, 1)
    ]
    pulls = [-h * f for h, f in zip(has_next, (behind2, behind, here, ahead))]
    behind_pos, positions, ahead_pos = (0.25 * (pulls[k + 1] - pulls[k]) for k in range(3))
    neighbours = blank
    for e in range(4 * NODE_COLS):
        neighbours = neighbours + counts[e : e + 1, :] * positions[:, e : e + 1]
    in_plane = 0.25 * (neighbours - 4.0 * positions)
    pull = has_next[2] * (ahead_pos - positions - here)
    pull_behind = has_next[1] * (positions - behind_pos - behind)
    positions = positions + 0.5 * (in_plane + 0.5 * (pull - pull_behind))
    for part in range(2):
        shifts[0, part] = found_next[part : part + 1, own]
        shifts[1, part] = found_second[part : part + 1, own]
        moved[part] = positions[part : part + 1, own]
    copies = [
        pltpu.make_async_copy(shifts, shifts_out, sems.at[0]),
        pltpu.make_async_copy(moved, moved_out, sems.at[1]),
    ]
    for copy in copies:
        copy.start()
    for copy in copies:
        copy.wait()


def finish(every, counts, offsets, total):
    vmem, hbm = pl.BlockSpec(memory_space=pltpu.VMEM), pl.BlockSpec(memory_space=pltpu.HBM)
    nodes = 2 * NODE_COLS
    shapes = ((2, 2, 1, nodes), (2, 1, nodes))
    return pl.pallas_call(
        functools.partial(finish_kernel, total),
        out_shape=tuple(jax.ShapeDtypeStruct(shape, jnp.float32) for shape in shapes),
        in_specs=[vmem] * 3,
        out_specs=(hbm, hbm),
        scratch_shapes=[pltpu.VMEM(shape, jnp.float32) for shape in shapes] + [pltpu.SemaphoreType.DMA((2,))],
        cost_estimate=pl.CostEstimate(flops=1, bytes_accessed=1, transcendentals=0),
        name="finish",
    )(every, counts, offsets)


def shards(sections, offsets, node_links):
    patches = sections[0]
    groups, tiles = lax.axis_size("group"), lax.axis_size("tile")

    def send(value, steps):
        total = 4 * groups
        pairs = [(i, i + steps[i % 4]) for i in range(total) if 0 <= i + steps[i % 4] < total]
        return lax.ppermute(value, ("group", "member"), pairs)

    kept, beside, across, slanted = prepare(patches, offsets)
    across_in = send(across, (2, 2, -2, -2))
    border_in = send(kept, (-4, -4, 4, 4))
    border_beside_in = send(beside, (-3, -5, 5, 3))
    beside_in = send(beside, (1, -1, 1, -1))
    slanted_in = send(slanted, (3, 1, -1, -3))
    state, held = run_stage(0, [jnp.asarray(t) for t in tables()], (), [kept, border_in], (node_links, offsets))
    *consts, counts, own_offsets = held
    state, _ = run_stage(1, consts, state, [across_in])
    state, _ = run_stage(2, consts, state, [border_beside_in, beside_in])
    state, _ = run_stage(3, consts, state, [slanted_in])
    found = state[3]

    near = send(found, (4, 4, -4, -4))
    rest = jnp.zeros((1, 128 - 2 * FOUND), jnp.float32)
    found = jnp.concatenate([found[:, :FOUND], near[:, :FOUND], rest], axis=1)
    every = lax.all_to_all(jnp.broadcast_to(found[None], (4 * tiles, 1, 128)), ("member", "tile"), 0, 0)
    near_by = [pltpu.with_memory_space_constraint(x, pltpu.VMEM) for x in (every, counts, own_offsets)]
    return finish(*near_by, 4 * groups)


def solution(mesh):
    sections, tiles = mesh.devices.shape
    mesh = jax.sharding.Mesh(mesh.devices.reshape(sections // 4, 4, tiles), ("group", "member", "tile"))
    gz = ("group", "member")
    return jax.shard_map(
        shards,
        mesh=mesh,
        in_specs=(P(gz, "tile", None, None), P(None, None, gz, "tile"), P(None, gz, "tile")),
        out_specs=(P(None, None, gz, "tile"), P(None, gz, "tile")),
        check_vma=False,
    )
```
